32 devices in a mesh: dp: 2 (over x), expert: 16 (over z, y, core).
Axes of the slice: x: 2, y: 2, z: 4, core: 2. Of those that a mesh axis runs over, the one named last changes fastest.
Arguments:
- tokens: bfloat16 [4096, 2048], P(('dp', 'expert')), may hold values from -6 to 6
- out_grad: bfloat16 [4096, 2048], P(('dp', 'expert')), may hold values from -6 to 6
- gate_saved: bfloat16 [4096, 6, 1408], P(('dp', 'expert')), may hold values from -6 to 6
- probs: float32 [4096, 6], P(('dp', 'expert')), may hold values from 0.1 to 1
- expert_ids: int32 [4096, 6], P(('dp', 'expert')), may hold values from 0 to 15, all different within a row; in each aligned block of 128 rows (0 to 127, 128 to 255, ...) at most 96 rows name the same one
- w_gate: bfloat16 [16, 2048, 1408], P('expert'), may hold values from -0.125 to 0.125
- w_up: bfloat16 [16, 2048, 1408], P('expert'), may hold values from -0.125 to 0.125
- w_down: bfloat16 [16, 1408, 2048], P('expert'), may hold values from -0.15625 to 0.15625
Outputs:
- input_grad: bfloat16 [4096, 2048], P(('dp', 'expert'))
- grad_gate: bfloat16 [16, 2048, 1408], P('expert', 'dp')
- grad_up: bfloat16 [16, 2048, 1408], P('expert', 'dp')
- grad_down: bfloat16 [16, 1408, 2048], P('expert', 'dp')
The draws below stay inside these ranges and needn't reach their ends.
Inputs may be any that keep to these rules, and one draw needn't show every extreme that they name: `expert_ids`: each token names 6 different experts. Among the 128 tokens of one aligned block (the tokens of one device) no expert is named more than 96 times, and in some block some expert is named exactly 96 times.
All inputs are finite; a program needn't handle non-finite values.
Results may differ from the reference program's by a relative error of at most 0.013.
Values may be sent and summed in bfloat16 or wider, within the bound.
No kernel may reach another device: no remote copies, remote signals or barrier semaphores. Data moves between devices by JAX's collectives and lax.ppermute only.
A program may use at most 192 MiB of HBM per device.

```python
import math
import jax
import jax.numpy as jnp
import numpy as np
from jax import lax

D = 2048
H = 1408
TOP = 6
TOK_DEV = 128
EXPERTS = 16
MOST = 96
TOKENS = 4096
N_DP = 2
N_EXPERT = 16


def steps_of(stream_key, dims, shards, smallest, largest):
    gain = 1.0
    for dim, blocks in shards:
        draws = jax.random.uniform(jax.random.fold_in(jax.random.fold_in(stream_key, 6), dim), (blocks,), jnp.float32, smallest / len(shards), largest / len(shards))
        gain = gain * jnp.repeat(jnp.exp(draws), dims[dim] // blocks).reshape((-1,) + (1,) * (len(dims) - 1 - dim))
    return gain


def assign_block(key, own, number, rows, number_of, top, reach, slope):
    ranking = jax.random.permutation(key, number_of)
    crowded, common = portions_of(number_of, rows * top, reach, slope, True), portions_of(number_of, rows * top, reach, slope, False)
    places = jnp.arange(number_of)

    def named(lengths, rotation):
        used = int((lengths > 0).sum())
        fixed = max(1, used // 4)
        moved = fixed + (places - fixed + rotation * (used - fixed)) % max(1, number_of - fixed)
        return jnp.zeros((number_of,), jnp.int32).at[ranking[jnp.where(places < fixed, places, moved)]].set(jnp.asarray(lengths, jnp.int32))

    lengths = jnp.where(number % 4 == 0, named(crowded, number // 4), named(common, number - number // 4 - 1))
    mixed = jax.random.permutation(jax.random.fold_in(own, 3), number_of)
    source_of, receiver = mixed[0:number_of // 2 * 2:2], mixed[1:number_of // 2 * 2:2]
    slack = jnp.minimum(lengths[source_of] - 1, reach - lengths[receiver]) // 2
    slack = jnp.where((source_of == ranking[0]) | (receiver == ranking[0]) | (lengths[receiver] == 0), 0, jnp.maximum(slack, 0))
    moved = jax.random.randint(jax.random.fold_in(own, 4), (number_of // 2,), 0, 1 << 20) % (slack + 1)
    lengths = lengths.at[source_of].add(-moved).at[receiver].add(moved)
    labels = jnp.searchsorted(jnp.cumsum(lengths), jnp.arange(rows * top), side="right").astype(jnp.int32)
    listing = labels.reshape(top, rows).T
    listing = listing[jax.random.permutation(jax.random.fold_in(own, 1), rows)]
    rotation = jax.random.randint(jax.random.fold_in(own, 2), (rows, 1), 0, top)
    return jnp.take_along_axis(listing, (jnp.arange(top)[None, :] + rotation) % top, axis=1)


def portions_of(number_of, total, limit, skew, full):
    loads = [(1 << 20) // math.isqrt(rank ** skew) + 1 for rank in range(1, number_of + 1)]
    largest = limit if full else min(limit, max(-(-total // number_of), total * loads[0] // sum(loads)))
    least = 1 if total - largest >= number_of - 1 else 0
    holding, spare = [largest] + [least] * (number_of - 1), total - largest - least * (number_of - 1)
    while spare > 0:
        movable = [i for i in range(1, number_of) if holding[i] < largest] or [i for i in range(1, number_of) if holding[i] < limit]
        whole, left = sum([loads[i] for i in movable]), spare
        for i in movable:
            extra = min(limit - holding[i], max(1, left * loads[i] // whole), spare)
            holding[i] = holding[i] + extra
            spare = spare - extra
    return np.array(holding)


def normal_values(own_key, dims, spread, limit, pieces=(), kind=jnp.bfloat16):
    drawn = spread * jax.random.normal(own_key, dims, jnp.float32)
    if pieces:
        drawn = drawn * steps_of(own_key, dims, pieces, -0.22, 0.18)
    return jnp.clip(drawn, -limit, limit).astype(kind)


def setup_inputs(seed: int = 0) -> dict:
    key_list = jax.random.split(jax.random.key(seed), 9)
    tokens = normal_values(key_list[0], (TOKENS, D), 1.0, 6.0, ((0, 32),))
    out_grad = normal_values(key_list[1], (TOKENS, D), 1.0, 6.0, ((0, 32),))
    gate_saved = normal_values(key_list[2], (TOKENS, TOP, H), 1.5, 6.0, ((0, 32),))
    probs = jnp.clip(jnp.exp(math.log(1.0) - 2.3025851 * jax.random.uniform(key_list[3], (TOKENS, TOP), jnp.float32) ** steps_of(key_list[3], (TOKENS, TOP), ((0, 32),), -0.2, 0.2)), 0.1, 1.0)
    expert_ids_keys = jax.random.split(jax.random.fold_in(key_list[4], 1), TOKENS // TOK_DEV)
    expert_ids_turns = jax.random.permutation(jax.random.fold_in(key_list[4], 3), TOKENS // TOK_DEV)
    expert_ids = jax.vmap(lambda own, number: assign_block(jax.random.fold_in(key_list[4], 2), own, number, TOK_DEV, EXPERTS, TOP, MOST, 3))(expert_ids_keys, expert_ids_turns).reshape((TOKENS, TOP))
    w_gate = normal_values(key_list[5], (EXPERTS, D, H), D ** -0.5, 0.125, ((0, 16),))
    w_up = normal_values(key_list[6], (EXPERTS, D, H), D ** -0.5, 0.125, ((0, 16),))
    w_down = normal_values(key_list[7], (EXPERTS, H, D), H ** -0.5, 0.15625, ((0, 16),))
    return {"tokens": tokens, "out_grad": out_grad, "gate_saved": gate_saved, "probs": probs, "expert_ids": expert_ids, "w_gate": w_gate, "w_up": w_up, "w_down": w_down}


grad_scale = 0.0625


def expert_rows(rows_in, routed_rows, gate_rows, gate_mat, up_mat, down_mat):
    up_act = jnp.dot(rows_in, up_mat, preferred_element_type=jnp.float32)
    gate_val = gate_rows.astype(jnp.float32)
    gate_sig = jax.nn.sigmoid(gate_val)
    gate_act = gate_val * gate_sig
    hidden_act = (gate_act * up_act).astype(jnp.bfloat16)
    hidden_grad = jnp.dot(routed_rows, down_mat.T, preferred_element_type=jnp.float32)
    up_grad = (hidden_grad * gate_act).astype(jnp.bfloat16)
    gate_grad = (hidden_grad * up_act * gate_sig * (1.0 + gate_val * (1.0 - gate_sig))).astype(jnp.bfloat16)
    input_part = (jnp.dot(gate_grad, gate_mat.T, preferred_element_type=jnp.float32)
                  + jnp.dot(up_grad, up_mat.T, preferred_element_type=jnp.float32)).astype(jnp.bfloat16)
    both_grads = jnp.concatenate([gate_grad, up_grad], axis=1)
    term_gate_up = jnp.dot(rows_in.T, both_grads, preferred_element_type=jnp.float32)
    term_down = jnp.dot(hidden_act.T, routed_rows, preferred_element_type=jnp.float32)
    return input_part, term_gate_up, term_down


def reference(tokens, out_grad, gate_saved, probs, expert_ids, w_gate, w_up, w_down):
    group_size = N_EXPERT * TOK_DEV
    slot_total = N_EXPERT * MOST
    group_routes = group_size * TOP
    routed = (probs[:, :, None] * out_grad[:, None, :].astype(jnp.float32)).astype(jnp.bfloat16)

    def per_expert(totals, expert):
        gate_mat = w_gate[expert]
        up_mat = w_up[expert]
        down_mat = w_down[expert]
        sum_gate_up = jnp.zeros((D, 2 * H), jnp.float32)
        sum_down = jnp.zeros((H, D), jnp.float32)
        for group_index in range(N_DP):
            group_start = group_index * group_size
            group_ids = expert_ids[group_start:group_start + group_size].reshape(group_routes)
            not_mine = (group_ids != expert).astype(jnp.int32)
            route_order = jnp.argsort(not_mine, stable=True)[:slot_total].astype(jnp.int32)
            matched = not_mine[route_order] == 0
            token_row = (route_order // TOP).astype(jnp.int32)
            rows_in = jnp.where(matched[:, None], tokens[group_start:group_start + group_size][token_row], 0)
            routed_rows = jnp.where(matched[:, None], routed[group_start:group_start + group_size].reshape(group_routes, D)[route_order], 0)
            gate_rows = jnp.where(matched[:, None], gate_saved[group_start:group_start + group_size].reshape(group_routes, H)[route_order], 0)
            input_part, term_gate_up, term_down = expert_rows(rows_in, routed_rows, gate_rows, gate_mat, up_mat, down_mat)
            totals = totals.at[group_start + token_row].add(jnp.where(matched[:, None], input_part.astype(jnp.float32), 0.0))
            sum_gate_up = sum_gate_up + lax.optimization_barrier(term_gate_up.astype(jnp.bfloat16)).astype(jnp.float32)
            sum_down = sum_down + lax.optimization_barrier(term_down.astype(jnp.bfloat16)).astype(jnp.float32)
        grad_gate = (grad_scale * sum_gate_up[:, :H]).astype(jnp.bfloat16)
        grad_up = (grad_scale * sum_gate_up[:, H:]).astype(jnp.bfloat16)
        grad_down = (grad_scale * sum_down).astype(jnp.bfloat16)
        return totals, (grad_gate, grad_up, grad_down)

    totals, grads = lax.scan(per_expert, jnp.zeros((TOKENS, D), jnp.float32), jnp.arange(EXPERTS, dtype=jnp.int32))
    return totals.astype(jnp.bfloat16), grads[0], grads[1], grads[2]
```

```python
import jax
import jax.numpy as jnp
from jax import lax
from jax.sharding import PartitionSpec as P

grad_scale = 0.0625
f32 = jnp.float32
bf16 = jnp.bfloat16


def dot(a, b, dims):
    return lax.dot_general(a, b, (dims, ((), ())), preferred_element_type=f32)


def chunk_widths(width):
    lanes = width // 128
    n = 4 if lanes >= 8 else 1
    sizes = [lanes // n + (1 if i >= n - lanes % n else 0) for i in range(n)]
    return [s * 128 for s in sizes]


def local(tokens, out_grad, gate_saved, probs, expert_ids, w_gate, w_up, w_down):
    n_peers = lax.axis_size("expert")
    n_dp = lax.axis_size("dp")
    me = lax.axis_index("expert")
    group = lax.axis_index("dp")
    tok_rows, model_width = tokens.shape
    top_k = expert_ids.shape[1]
    hidden_width = w_up.shape[2]
    cap = min(tok_rows, 2 * tok_rows * top_k // n_peers)
    n_routes = tok_rows * top_k
    n_slots = n_peers * cap
    gate_mat, up_mat, down_mat = w_gate[0], w_up[0], w_down[0]

    meta = jnp.concatenate([expert_ids.astype(f32), probs], axis=1)
    meta_all = lax.all_gather(meta, "expert", axis=0, tiled=False)
    tok_all = lax.all_gather(tokens, "expert", axis=0, tiled=False)
    grad_all = lax.all_gather(out_grad, "expert", axis=0, tiled=False)

    experts = jnp.arange(n_peers, dtype=jnp.int32)
    hit = expert_ids[:, :, None] == experts[None, None, :]
    named = jnp.any(hit, axis=1)
    rank = jnp.cumsum(named.astype(jnp.int32), axis=0) - 1
    slots = jnp.arange(cap, dtype=jnp.int32)
    pick = (
        hit[:, :, :, None] & (rank[:, None, :, None] == slots[None, None, None, :])
    ).astype(bf16)
    send_gate = lax.dot_general(
        pick.reshape(n_routes, n_slots),
        gate_saved.reshape(n_routes, hidden_width),
        (((0,), (0,)), ((), ())),
        preferred_element_type=f32,
    ).astype(bf16).reshape(n_peers, cap, hidden_width)

    widths = chunk_widths(hidden_width)
    starts = [sum(widths[:i]) for i in range(len(widths))]
    recv_gate = [
        lax.all_to_all(
            send_gate[:, :, s : s + w], "expert", split_axis=0, concat_axis=0, tiled=True
        ).reshape(n_slots, w)
        for s, w in zip(starts, widths)
    ]

    ids_all = meta_all[:, :, :top_k].astype(jnp.int32)
    mine = ids_all == me
    prob_all = jnp.sum(jnp.where(mine, meta_all[:, :, top_k:], 0.0), axis=2)
    mine = jnp.any(mine, axis=2)
    rank_all = jnp.cumsum(mine.astype(jnp.int32), axis=1) - 1
    place = (
        mine[:, None, :] & (rank_all[:, None, :] == slots[None, :, None])
    ).astype(bf16)
    by_block = (((2,), (1,)), ((0,), (0,)))
    rows_in = (
        lax.dot_general(place, tok_all, by_block, preferred_element_type=f32)
        .astype(bf16)
        .reshape(n_slots, model_width)
    )
    scaled = (prob_all[:, :, None] * grad_all.astype(f32)).astype(bf16)
    routed = (
        lax.dot_general(place, scaled, by_block, preferred_element_type=f32)
        .astype(bf16)
        .reshape(n_slots, model_width)
    )

    up_act = dot(rows_in, up_mat, ((1,), (0,)))
    hidden_grad = dot(routed, down_mat, ((1,), (1,)))

    piece = model_width // n_dp
    shifts = [[(i, (i + d) % n_dp) for i in range(n_dp)] for d in range(n_dp)]

    def rows_of(d):
        q = lax.rem(group + d, n_dp)
        return lax.dynamic_slice_in_dim(rows_in, q * piece, piece, 1)

    gate_out, up_out, hidden_parts, gate_parts, up_parts = [], [], [], [], []
    for s, w, gate_rows in zip(starts, widths, recv_gate):
        gate_val = gate_rows.astype(f32)
        gate_sig = jax.nn.sigmoid(gate_val)
        gate_act = gate_val * gate_sig
        up_c = up_act[:, s : s + w]
        grad_c = hidden_grad[:, s : s + w]
        hidden_parts.append((gate_act * up_c).astype(bf16))
        up_grad = (grad_c * gate_act).astype(bf16)
        gate_grad = (grad_c * up_c * gate_sig * (1.0 + gate_val * (1.0 - gate_sig))).astype(bf16)
        gate_parts.append(gate_grad)
        up_parts.append(up_grad)
        both = jnp.concatenate([gate_grad, up_grad], axis=1)
        arrived = []
        for d in range(1, n_dp):
            part = dot(rows_of(d), both, ((0,), (0,))).astype(bf16)
            arrived.append(lax.ppermute(part, "dp", shifts[d]))
        total = dot(rows_of(0), both, ((0,), (0,))).astype(bf16).astype(f32)
        for part in arrived:
            total = total + part.astype(f32)
        total = (grad_scale * total).astype(bf16)
        gate_out.append(total[:, :w])
        up_out.append(total[:, w:])

    hidden_act = jnp.concatenate(hidden_parts, axis=1)
    sum_down = dot(hidden_act, routed, ((0,), (0,))).astype(bf16)
    low = hidden_width // n_dp
    arrived = []
    for d in range(1, n_dp):
        q = lax.rem(group + d, n_dp)
        part = lax.dynamic_slice_in_dim(sum_down, q * low, low, 0)
        arrived.append(lax.ppermute(part, "dp", shifts[d]))
    down = lax.dynamic_slice_in_dim(sum_down, group * low, low, 0).astype(f32)
    for part in arrived:
        down = down + part.astype(f32)
    grad_down = (grad_scale * down).astype(bf16)[None]

    gate_grad = jnp.concatenate(gate_parts, axis=1)
    up_grad = jnp.concatenate(up_parts, axis=1)
    input_part = (
        (dot(gate_grad, gate_mat, ((1,), (1,))) + dot(up_grad, up_mat, ((1,), (1,))))
        .astype(bf16)
        .reshape(n_peers, cap, model_width)
    )
    spread = lax.dot_general(
        place, input_part, (((1,), (1,)), ((0,), (0,))), preferred_element_type=f32
    ).astype(bf16)
    input_grad = lax.psum_scatter(
        spread.reshape(n_peers * tok_rows, model_width), "expert", scatter_dimension=0, tiled=True
    )
    grad_gate = jnp.concatenate(gate_out, axis=1)[None]
    grad_up = jnp.concatenate(up_out, axis=1)[None]
    return (input_grad, grad_gate, grad_up, grad_down)


def solution(mesh):
    return jax.shard_map(
        local,
        mesh=mesh,
        in_specs=(
            P(("dp", "expert"), None),
            P(("dp", "expert"), None),
            P(("dp", "expert"), None, None),
            P(("dp", "expert"), None),
            P(("dp", "expert"), None),
            P("expert", None, None),
            P("expert", None, None),
            P("expert", None, None),
        ),
        out_specs=(
            P(("dp", "expert"), None),
            P("expert", "dp", None),
            P("expert", "dp", None),
            P("expert", "dp", None),
        ),
        check_vma=False,
    )
```

```python
import jax
import jax.numpy as jnp
import numpy as np
from jax import lax
from jax.experimental import pallas as pl
from jax.experimental.pallas import tpu as pltpu
from jax.sharding import PartitionSpec as P

grad_scale = 0.0625
f32 = jnp.float32
bf16 = jnp.bfloat16
i32 = jnp.int32


def dot(a, b, dims):
    return lax.dot_general(a, b, (dims, ((), ())), preferred_element_type=f32)


def chunk_widths(width):
    lanes = width // 128
    n = 4 if lanes >= 8 else 1
    sizes = [lanes // n + (1 if i >= n - lanes % n else 0) for i in range(n)]
    return [s * 128 for s in sizes]


def chip_cycle(n_chips):
    cols = n_chips // 4
    if n_chips % 4 or cols < 2:
        return list(range(n_chips))
    walk = [(row, 0) for row in range(4)]
    for step, row in enumerate((3, 2, 1, 0)):
        across = range(1, cols) if step % 2 == 0 else range(cols - 1, 0, -1)
        walk += [(row, col) for col in across]
    return [row * cols + col for row, col in walk]


def put_rows(order, table, shards, rows, routed, cap):
    count = len(shards)
    n_peers, _, _ = table.shape
    width = shards[0][0].shape[1]

    def body(order_ref, table_ref, *refs):
        parts = refs[: 2 * count]
        rows_ref, routed_ref = refs[-2:]
        step = pl.program_id(0)
        for i in range(count):

            @pl.when(step == i)
            def _():
                info = table_ref[0]
                place = (
                    lax.broadcasted_iota(i32, (cap, tok_rows_of), 1).astype(f32) == info[:, 0:1]
                ).astype(bf16)
                rows_ref[...] = jnp.dot(
                    place, parts[2 * i][...], preferred_element_type=f32
                ).astype(bf16)
                picked = jnp.dot(place, parts[2 * i + 1][...], preferred_element_type=f32)
                routed_ref[...] = (info[:, 1:2] * picked).astype(bf16)

    tok_rows_of = shards[0][2]
    in_specs = [pl.BlockSpec((1, cap, 2), lambda i, order: (order[i], 0, 0))]
    operands = [table]
    for tok, grad, height, tok_at, grad_at in shards:
        in_specs.append(pl.BlockSpec((height, width), lambda i, order, a=tok_at: (a, 0)))
        in_specs.append(pl.BlockSpec((height, width), lambda i, order, a=grad_at: (a, 0)))
        operands += [tok, grad]
    aliases = {}
    if rows is not None:
        aliases = {1 + len(operands): 0, 2 + len(operands): 1}
        in_specs += [pl.BlockSpec(memory_space=pl.ANY)] * 2
        operands += [rows, routed]
    n_slots = n_peers * cap
    shape = jax.ShapeDtypeStruct((n_slots, width), bf16)
    out_spec = pl.BlockSpec((cap, width), lambda i, order: (order[i], 0))
    return pl.pallas_call(
        body,
        out_shape=(shape, shape),
        grid_spec=pltpu.PrefetchScalarGridSpec(
            num_scalar_prefetch=1,
            grid=(count,),
            in_specs=in_specs,
            out_specs=(out_spec, out_spec),
        ),
        input_output_aliases=aliases,
        compiler_params=pltpu.CompilerParams(vmem_limit_bytes=40 * 1024 * 1024),
        cost_estimate=pl.CostEstimate(
            flops=4 * count * cap * tok_rows_of * width,
            bytes_accessed=4 * count * (tok_rows_of + cap) * width,
            transcendentals=0,
        ),
        name="put_rows",
    )(order, *operands)


def gather_rows(tokens, out_grad, table, cap):
    n_peers = lax.axis_size("expert")
    n_chips = n_peers // 2
    me = lax.axis_index("expert")
    cycle = chip_cycle(n_chips)
    spot = [cycle.index(c) for c in range(n_chips)]
    fwd = [(2 * cycle[i] + c, 2 * cycle[(i + 1) % n_chips] + c) for i in range(n_chips) for c in (0, 1)]
    bwd = [(b, a) for a, b in fwd]
    swap = [(i, i ^ 1) for i in range(n_peers)]
    my_core = me % 2
    my_spot = jnp.asarray(np.array(spot, np.int32))[me // 2]
    chip_at = jnp.asarray(np.array(cycle, np.int32))

    def source(distance, other):
        chip = chip_at[(my_spot - distance + n_chips) % n_chips]
        return 2 * chip + (1 - my_core if other else my_core)

    def other_core(x):
        return lax.ppermute(x, "expert", swap)

    tok_rows = tokens.shape[0]
    own = jnp.concatenate([tokens, out_grad], axis=0)

    def whole(x):
        return (x, x, tok_rows, 0, 1)

    def place(sources, shards, state):
        order = jnp.stack(sources).astype(i32)
        return put_rows(order, table, shards, *state, cap)

    state = (None, None)
    ahead, behind = own, own
    pending = ([source(0, False), source(0, True)], [whole(own), whole(other_core(own))])
    marks = []
    for d in range(1, n_chips // 2):
        ahead = lax.ppermute(ahead, "expert", fwd)
        behind = lax.ppermute(behind, "expert", bwd)
        marks.append((ahead, behind))
        state = place(*pending, state)
        pending = (
            [source(d, False), source(-d, False), source(d, True), source(-d, True)],
            [whole(ahead), whole(behind), whole(other_core(ahead)), whole(other_core(behind))],
        )
    far_tok = lax.ppermute(ahead[:tok_rows], "expert", fwd)
    far_grad = lax.ppermute(behind[tok_rows:], "expert", bwd)
    state = place(*pending, state)
    far = n_chips // 2
    state = place(
        [source(far, False), source(far, True)],
        [
            (far_tok, far_grad, tok_rows, 0, 0),
            (other_core(far_tok), other_core(far_grad), tok_rows, 0, 0),
        ],
        state,
    )
    return state, marks


def local(tokens, out_grad, gate_saved, probs, expert_ids, w_gate, w_up, w_down):
    n_peers = lax.axis_size("expert")
    n_dp = lax.axis_size("dp")
    group = lax.axis_index("dp")
    tok_rows, model_width = tokens.shape
    top_k = expert_ids.shape[1]
    hidden_width = w_up.shape[2]
    cap = min(tok_rows, 2 * tok_rows * top_k // n_peers)
    n_routes = tok_rows * top_k
    n_slots = n_peers * cap
    gate_mat, up_mat, down_mat = w_gate[0], w_up[0], w_down[0]

    experts = jnp.arange(n_peers, dtype=i32)
    hit = expert_ids[:, :, None] == experts[None, None, :]
    named = jnp.any(hit, axis=1)
    weight = jnp.sum(jnp.where(hit, probs[:, :, None], 0.0), axis=1)
    rank = jnp.cumsum(named.astype(i32), axis=0) - 1
    slots = jnp.arange(cap, dtype=i32)
    in_slot = named[:, :, None] & (rank[:, :, None] == slots[None, None, :])
    tok_of = jnp.sum(
        jnp.where(in_slot, jnp.arange(1, tok_rows + 1, dtype=f32)[:, None, None], 0.0), axis=0
    ) - 1.0
    weight_of = jnp.sum(jnp.where(in_slot, weight[:, :, None], 0.0), axis=0)
    table = lax.all_to_all(
        jnp.concatenate([tok_of, weight_of], axis=1),
        "expert",
        split_axis=0,
        concat_axis=0,
        tiled=True,
    )
    table = table.reshape(n_peers, 2, cap).transpose(0, 2, 1)
    (rows_in, routed), marks = gather_rows(tokens, out_grad, table, cap)

    pick = (
        hit[:, :, :, None] & (rank[:, None, :, None] == slots[None, None, None, :])
    ).astype(bf16)
    send_gate = lax.dot_general(
        pick.reshape(n_routes, n_slots),
        gate_saved.reshape(n_routes, hidden_width),
        (((0,), (0,)), ((), ())),
        preferred_element_type=f32,
    ).astype(bf16).reshape(n_peers, cap, hidden_width)

    widths = chunk_widths(hidden_width)
    starts = [sum(widths[:i]) for i in range(len(widths))]
    recv_gate = []
    for i, (s, w) in enumerate(zip(starts, widths)):
        part = send_gate[:, :, s : s + w]
        mark = marks[min(i + 1, len(marks) - 1)]
        part, _ = lax.optimization_barrier((part, mark))
        recv_gate.append(
            lax.all_to_all(part, "expert", split_axis=0, concat_axis=0, tiled=True).reshape(n_slots, w)
        )

    piece = model_width // n_dp
    shifts = [[(i, (i + d) % n_dp) for i in range(n_dp)] for d in range(n_dp)]

    def rows_of(rows, d):
        q = lax.rem(group + d, n_dp)
        return lax.dynamic_slice_in_dim(rows, q * piece, piece, 1)

    hidden_parts, both_parts, arrivals = [], [], []
    rows_now, routed_now = rows_in, routed
    for s, w, gate_rows in zip(starts, widths, recv_gate):
        up_c = dot(rows_now, up_mat[:, s : s + w], ((1,), (0,)))
        grad_c = dot(routed_now, down_mat[s : s + w], ((1,), (1,)))
        gate_val = gate_rows.astype(f32)
        gate_sig = jax.nn.sigmoid(gate_val)
        gate_act = gate_val * gate_sig
        hidden_parts.append((gate_act * up_c).astype(bf16))
        up_grad = (grad_c * gate_act).astype(bf16)
        gate_grad = (grad_c * up_c * gate_sig * (1.0 + gate_val * (1.0 - gate_sig))).astype(bf16)
        both = jnp.concatenate([gate_grad, up_grad], axis=1)
        both_parts.append(both)
        arrived, sent = [], []
        for d in range(1, n_dp):
            part = dot(rows_of(rows_now, d), both, ((0,), (0,))).astype(bf16)
            sent.append(part)
            arrived.append(lax.ppermute(part, "dp", shifts[d]))
        arrivals.append(arrived)
        rows_now, routed_now, _ = lax.optimization_barrier((rows_now, routed_now, sent))

    both_all = jnp.concatenate(both_parts, axis=1)
    both_all, _ = lax.optimization_barrier((both_all, rows_now))
    both_mat = jnp.concatenate(
        [m[:, s : s + w] for s, w in zip(starts, widths) for m in (gate_mat, up_mat)], axis=1
    )
    input_part = (
        dot(both_all, both_mat, ((1,), (1,))).astype(bf16).reshape(n_peers, cap, model_width)
    )
    place = (table[:, :, 0:1] == jnp.arange(tok_rows, dtype=f32)[None, None, :]).astype(bf16)
    spread = lax.dot_general(
        place, input_part, (((1,), (1,)), ((0,), (0,))), preferred_element_type=f32
    ).astype(bf16)
    input_grad = lax.psum_scatter(
        spread.reshape(n_peers * tok_rows, model_width), "expert", scatter_dimension=0, tiled=True
    )

    hidden_act = jnp.concatenate(hidden_parts, axis=1)
    rows_now, routed_now, _ = lax.optimization_barrier((rows_now, routed_now, spread))
    sum_down = dot(hidden_act, routed_now, ((0,), (0,))).astype(bf16)
    low = hidden_width // n_dp
    arrived = []
    for d in range(1, n_dp):
        q = lax.rem(group + d, n_dp)
        part = lax.dynamic_slice_in_dim(sum_down, q * low, low, 0)
        arrived.append(lax.ppermute(part, "dp", shifts[d]))
    down = lax.dynamic_slice_in_dim(sum_down, group * low, low, 0).astype(f32)
    for part in arrived:
        down = down + part.astype(f32)
    grad_down = (grad_scale * down).astype(bf16)[None]

    gate_out, up_out = [], []
    for w, both, arrived in zip(widths, both_parts, arrivals):
        total = dot(rows_of(rows_now, 0), both, ((0,), (0,))).astype(bf16).astype(f32)
        for part in arrived:
            total = total + part.astype(f32)
        total = (grad_scale * total).astype(bf16)
        gate_out.append(total[:, :w])
        up_out.append(total[:, w:])
    grad_gate = jnp.concatenate(gate_out, axis=1)[None]
    grad_up = jnp.concatenate(up_out, axis=1)[None]
    return (input_grad, grad_gate, grad_up, grad_down)


def solution(mesh):
    return jax.shard_map(
        local,
        mesh=mesh,
        in_specs=(
            P(("dp", "expert"), None),
            P(("dp", "expert"), None),
            P(("dp", "expert"), None, None),
            P(("dp", "expert"), None),
            P(("dp", "expert"), None),
            P("expert", None, None),
            P("expert", None, None),
            P("expert", None, None),
        ),
        out_specs=(
            P(("dp", "expert"), None),
            P("expert", "dp", None),
            P("expert", "dp", None),
            P("expert", "dp", None),
        ),
        check_vma=False,
    )
```

```python
import jax
import jax.numpy as jnp
import numpy as np
from jax import lax
from jax.experimental import pallas as pl
from jax.experimental.pallas import tpu as pltpu
from jax.sharding import PartitionSpec as P

grad_scale = 0.0625
f32 = jnp.float32
bf16 = jnp.bfloat16
i32 = jnp.int32


def dot(a, b, dims):
    return lax.dot_general(a, b, (dims, ((), ())), preferred_element_type=f32)


def chunk_widths(width):
    lanes = width // 128
    shares = (2, 4, 7, 11)
    ends = [-(-lanes * x // 11) * 128 for x in shares]
    return [e - s for s, e in zip([0] + ends, ends) if e > s]


def chip_cycle(n_chips):
    cols = n_chips // 4
    if n_chips % 4 or cols < 2:
        return list(range(n_chips))
    walk = [(row, 0) for row in range(4)]
    for step, row in enumerate((3, 2, 1, 0)):
        across = range(1, cols) if step % 2 == 0 else range(cols - 1, 0, -1)
        walk += [(row, col) for col in across]
    return [row * cols + col for row, col in walk]


def put_rows(order, table, shards, rows, routed, cap):
    count = len(shards)
    n_peers, _, _ = table.shape
    width = shards[0][0].shape[1]

    def body(order_ref, table_ref, *refs):
        parts = refs[: 2 * count]
        rows_ref, routed_ref = refs[-2:]
        step = pl.program_id(0)
        for i in range(count):

            @pl.when(step == i)
            def _():
                info = table_ref[0]
                place = (
                    lax.broadcasted_iota(i32, (cap, tok_rows_of), 1).astype(f32) == info[:, 0:1]
                ).astype(bf16)
                rows_ref[...] = jnp.dot(
                    place, parts[2 * i][...], preferred_element_type=f32
                ).astype(bf16)
                picked = jnp.dot(place, parts[2 * i + 1][...], preferred_element_type=f32)
                routed_ref[...] = (info[:, 1:2] * picked).astype(bf16)

    tok_rows_of = shards[0][2]
    in_specs = [pl.BlockSpec((1, cap, 2), lambda i, order: (order[i], 0, 0))]
    operands = [table]
    for tok, grad, height, tok_at, grad_at in shards:
        in_specs.append(pl.BlockSpec((height, width), lambda i, order, a=tok_at: (a, 0)))
        in_specs.append(pl.BlockSpec((height, width), lambda i, order, a=grad_at: (a, 0)))
        operands += [tok, grad]
    aliases = {}
    if rows is not None:
        aliases = {1 + len(operands): 0, 2 + len(operands): 1}
        in_specs += [pl.BlockSpec(memory_space=pl.ANY)] * 2
        operands += [rows, routed]
    n_slots = n_peers * cap
    shape = jax.ShapeDtypeStruct((n_slots, width), bf16)
    out_spec = pl.BlockSpec((cap, width), lambda i, order: (order[i], 0))
    return pl.pallas_call(
        body,
        out_shape=(shape, shape),
        grid_spec=pltpu.PrefetchScalarGridSpec(
            num_scalar_prefetch=1,
            grid=(count,),
            in_specs=in_specs,
            out_specs=(out_spec, out_spec),
        ),
        input_output_aliases=aliases,
        compiler_params=pltpu.CompilerParams(vmem_limit_bytes=40 * 1024 * 1024),
        cost_estimate=pl.CostEstimate(
            flops=4 * count * cap * tok_rows_of * width,
            bytes_accessed=4 * count * (tok_rows_of + cap) * width,
            transcendentals=0,
        ),
        name="put_rows",
    )(order, *operands)


def gather_rows(tokens, out_grad, table, cap):
    n_peers = lax.axis_size("expert")
    n_chips = n_peers // 2
    me = lax.axis_index("expert")
    cycle = chip_cycle(n_chips)
    spot = [cycle.index(c) for c in range(n_chips)]
    fwd = [(2 * cycle[i] + c, 2 * cycle[(i + 1) % n_chips] + c) for i in range(n_chips) for c in (0, 1)]
    bwd = [(b, a) for a, b in fwd]
    swap = [(i, i ^ 1) for i in range(n_peers)]
    my_core = me % 2
    my_spot = jnp.asarray(np.array(spot, np.int32))[me // 2]
    chip_at = jnp.asarray(np.array(cycle, np.int32))

    def source(distance, other):
        chip = chip_at[(my_spot - distance + n_chips) % n_chips]
        return 2 * chip + (1 - my_core if other else my_core)

    def other_core(x):
        return lax.ppermute(x, "expert", swap)

    tok_rows = tokens.shape[0]
    own = jnp.concatenate([tokens, out_grad], axis=0)

    def whole(x):
        return (x, x, tok_rows, 0, 1)

    def place(sources, shards, state):
        order = jnp.stack(sources).astype(i32)
        return put_rows(order, table, shards, *state, cap)

    state = (None, None)
    ahead, behind = own, own
    pending = ([source(0, False), source(0, True)], [whole(own), whole(other_core(own))])
    marks = []
    for d in range(1, n_chips // 2):
        ahead = lax.ppermute(ahead, "expert", fwd)
        behind = lax.ppermute(behind, "expert", bwd)
        marks.append((ahead, behind))
        state = place(*pending, state)
        pending = (
            [source(d, False), source(-d, False), source(d, True), source(-d, True)],
            [whole(ahead), whole(behind), whole(other_core(ahead)), whole(other_core(behind))],
        )
    far_tok = lax.ppermute(ahead[:tok_rows], "expert", fwd)
    far_grad = lax.ppermute(behind[tok_rows:], "expert", bwd)
    state = place(*pending, state)
    marks.append((far_tok, far_grad))
    far = n_chips // 2
    state = place(
        [source(far, False), source(far, True)],
        [
            (far_tok, far_grad, tok_rows, 0, 0),
            (other_core(far_tok), other_core(far_grad), tok_rows, 0, 0),
        ],
        state,
    )
    return state, marks


def row_block(n_slots):
    return next(r for r in (256, 192, 128, 96, 64, 48, 32, 16, n_slots) if n_slots % r == 0)


LIGHT = pl.CostEstimate(flops=1000, bytes_accessed=1000, transcendentals=0)


def chunk_grads(rows, routed, gate, up_part, down_part):
    n_slots, width = rows.shape
    w = gate.shape[1]
    r = row_block(n_slots)

    def body(rows_ref, routed_ref, gate_ref, up_ref, down_ref, hidden_ref, both_ref):
        up_act = jnp.dot(rows_ref[...], up_ref[...], preferred_element_type=f32)
        hidden_grad = dot(routed_ref[...], down_ref[...], ((1,), (1,)))
        gate_val = gate_ref[...].astype(f32)
        gate_sig = jax.nn.sigmoid(gate_val)
        gate_act = gate_val * gate_sig
        hidden_ref[...] = (gate_act * up_act).astype(bf16)
        both_ref[:, w:] = (hidden_grad * gate_act).astype(bf16)
        both_ref[:, :w] = (
            hidden_grad * up_act * gate_sig * (1.0 + gate_val * (1.0 - gate_sig))
        ).astype(bf16)

    return pl.pallas_call(
        body,
        out_shape=(
            jax.ShapeDtypeStruct((n_slots, w), bf16),
            jax.ShapeDtypeStruct((n_slots, 2 * w), bf16),
        ),
        grid=(n_slots // r,),
        in_specs=[
            pl.BlockSpec((r, width), lambda i: (i, 0)),
            pl.BlockSpec((r, width), lambda i: (i, 0)),
            pl.BlockSpec((r, w), lambda i: (i, 0)),
            pl.BlockSpec((width, w), lambda i: (0, 0)),
            pl.BlockSpec((w, width), lambda i: (0, 0)),
        ],
        out_specs=(
            pl.BlockSpec((r, w), lambda i: (i, 0)),
            pl.BlockSpec((r, 2 * w), lambda i: (i, 0)),
        ),
        compiler_params=pltpu.CompilerParams(vmem_limit_bytes=40 * 1024 * 1024),
        cost_estimate=LIGHT,
        name="chunk_grads",
    )(rows, routed, gate, up_part, down_part)


def spread_back(parts, starts, gate_mat, up_mat, table, tok_rows):
    n_peers, _, cap = table.shape
    width, hidden_width = gate_mat.shape
    n_blocks = max(b for b in range(1, n_peers + 1) if n_peers % b == 0 and b * cap <= 384)
    cols = min(512, width)

    def body(*refs):
        part_refs = refs[: len(parts)]
        gate_ref, up_ref, table_ref, out_ref = refs[len(parts) :]
        total = jnp.zeros((n_blocks * cap, cols), f32)
        for start, part_ref in zip(starts, part_refs):
            w = part_ref.shape[1] // 2
            total += dot(part_ref[:, :w], gate_ref[:, start : start + w], ((1,), (1,)))
            total += dot(part_ref[:, w:], up_ref[:, start : start + w], ((1,), (1,)))
        terms = total.astype(bf16)
        for b in range(n_blocks):
            tok = table_ref[b, 0:1, :]
            place = (lax.broadcasted_iota(i32, (tok_rows, cap), 0).astype(f32) == tok).astype(bf16)
            out_ref[b * tok_rows : (b + 1) * tok_rows, :] = jnp.dot(
                place, terms[b * cap : (b + 1) * cap], preferred_element_type=f32
            ).astype(bf16)

    rows = n_blocks * cap
    return pl.pallas_call(
        body,
        out_shape=jax.ShapeDtypeStruct((n_peers * tok_rows, width), bf16),
        grid=(width // cols, n_peers // n_blocks),
        in_specs=[pl.BlockSpec((rows, x.shape[1]), lambda j, i: (i, 0)) for x in parts]
        + [
            pl.BlockSpec((cols, hidden_width), lambda j, i: (j, 0)),
            pl.BlockSpec((cols, hidden_width), lambda j, i: (j, 0)),
            pl.BlockSpec((n_blocks, 2, cap), lambda j, i: (i, 0, 0)),
        ],
        out_specs=pl.BlockSpec((n_blocks * tok_rows, cols), lambda j, i: (i, j)),
        compiler_params=pltpu.CompilerParams(vmem_limit_bytes=40 * 1024 * 1024),
        cost_estimate=LIGHT,
        name="spread_back",
    )(*parts, gate_mat, up_mat, table)


def local(tokens, out_grad, gate_saved, probs, expert_ids, w_gate, w_up, w_down):
    n_peers = lax.axis_size("expert")
    n_dp = lax.axis_size("dp")
    group = lax.axis_index("dp")
    tok_rows, model_width = tokens.shape
    top_k = expert_ids.shape[1]
    hidden_width = w_up.shape[2]
    cap = min(tok_rows, 2 * tok_rows * top_k // n_peers)
    n_routes = tok_rows * top_k
    n_slots = n_peers * cap
    gate_mat, up_mat, down_mat = w_gate[0], w_up[0], w_down[0]

    experts = jnp.arange(n_peers, dtype=i32)
    hit = expert_ids[:, :, None] == experts[None, None, :]
    named = jnp.any(hit, axis=1)
    weight = jnp.sum(jnp.where(hit, probs[:, :, None], 0.0), axis=1)
    rank = jnp.cumsum(named.astype(i32), axis=0) - 1
    slots = jnp.arange(cap, dtype=i32)
    in_slot = named[:, :, None] & (rank[:, :, None] == slots[None, None, :])
    tok_of = jnp.sum(
        jnp.where(in_slot, jnp.arange(1, tok_rows + 1, dtype=f32)[:, None, None], 0.0), axis=0
    ) - 1.0
    weight_of = jnp.sum(jnp.where(in_slot, weight[:, :, None], 0.0), axis=0)
    table = lax.all_to_all(
        jnp.concatenate([tok_of, weight_of], axis=1),
        "expert",
        split_axis=0,
        concat_axis=0,
        tiled=True,
    )
    table = table.reshape(n_peers, 2, cap)
    (rows_in, routed), marks = gather_rows(tokens, out_grad, table.transpose(0, 2, 1), cap)

    pick = (
        hit[:, :, :, None] & (rank[:, None, :, None] == slots[None, None, None, :])
    ).astype(bf16)
    send_gate = lax.dot_general(
        pick.reshape(n_routes, n_slots),
        gate_saved.reshape(n_routes, hidden_width),
        (((0,), (0,)), ((), ())),
        preferred_element_type=f32,
    ).astype(bf16).reshape(n_peers, cap, hidden_width)

    widths = chunk_widths(hidden_width)
    starts = [sum(widths[:i]) for i in range(len(widths))]
    recv_gate = []
    for i, (s, w) in enumerate(zip(starts, widths)):
        part = send_gate[:, :, s : s + w]
        mark = marks[1 if i == 0 else -1]
        part, _ = lax.optimization_barrier((part, mark))
        recv_gate.append(
            lax.all_to_all(part, "expert", split_axis=0, concat_axis=0, tiled=True).reshape(n_slots, w)
        )

    piece = model_width // n_dp
    shifts = [[(i, (i + d) % n_dp) for i in range(n_dp)] for d in range(n_dp)]

    def rows_of(rows, d):
        q = lax.rem(group + d, n_dp)
        return lax.dynamic_slice_in_dim(rows, q * piece, piece, 1)

    up_parts = [up_mat[:, s : s + w] for s, w in zip(starts, widths)]
    down_parts = [down_mat[s : s + w] for s, w in zip(starts, widths)]
    up_parts, down_parts, _ = lax.optimization_barrier((up_parts, down_parts, marks[0]))
    hidden_parts, both_parts, arrivals = [], [], []
    rows_now, routed_now = rows_in, routed
    for c, w in enumerate(widths):
        hidden, both = chunk_grads(rows_now, routed_now, recv_gate[c], up_parts[c], down_parts[c])
        hidden_parts.append(hidden)
        both_parts.append(both)
        arrived, sent = [], []
        for d in range(1, n_dp):
            part = dot(rows_of(rows_now, d), both, ((0,), (0,))).astype(bf16)
            sent.append(part)
            arrived.append(lax.ppermute(part, "dp", shifts[d]))
        arrivals.append(arrived)
        rows_now, routed_now, _ = lax.optimization_barrier((rows_now, routed_now, sent))

    last, arrivals[0], _ = lax.optimization_barrier((both_parts[-1], arrivals[0], rows_now))
    spread = spread_back(both_parts[:-1] + [last], starts, gate_mat, up_mat, table, tok_rows)
    input_grad = lax.psum_scatter(spread, "expert", scatter_dimension=0, tiled=True)

    hidden_act = jnp.concatenate(hidden_parts, axis=1)
    rows_now, routed_now, arrivals[1], _ = lax.optimization_barrier(
        (rows_now, routed_now, arrivals[1], spread)
    )
    sum_down = dot(hidden_act, routed_now, ((0,), (0,))).astype(bf16)
    low = hidden_width // n_dp
    arrived = []
    for d in range(1, n_dp):
        q = lax.rem(group + d, n_dp)
        part = lax.dynamic_slice_in_dim(sum_down, q * low, low, 0)
        arrived.append(lax.ppermute(part, "dp", shifts[d]))
    down = lax.dynamic_slice_in_dim(sum_down, group * low, low, 0).astype(f32)
    for part in arrived:
        down = down + part.astype(f32)
    grad_down = (grad_scale * down).astype(bf16)[None]

    gate_out, up_out = [], []
    for w, both, arrived in zip(widths, both_parts, arrivals):
        total = dot(rows_of(rows_now, 0), both, ((0,), (0,))).astype(bf16).astype(f32)
        for part in arrived:
            total = total + part.astype(f32)
        total = (grad_scale * total).astype(bf16)
        gate_out.append(total[:, :w])
        up_out.append(total[:, w:])
    grad_gate = jnp.concatenate(gate_out, axis=1)[None]
    grad_up = jnp.concatenate(up_out, axis=1)[None]
    return (input_grad, grad_gate, grad_up, grad_down)


def solution(mesh):
    return jax.shard_map(
        local,
        mesh=mesh,
        in_specs=(
            P(("dp", "expert"), None),
            P(("dp", "expert"), None),
            P(("dp", "expert"), None, None),
            P(("dp", "expert"), None),
            P(("dp", "expert"), None),
            P("expert", None, None),
            P("expert", None, None),
            P("expert", None, None),
        ),
        out_specs=(
            P(("dp", "expert"), None),
            P("expert", "dp", None),
            P("expert", "dp", None),
            P("expert", "dp", None),
        ),
        check_vma=False,
    )
```

```python
import jax
import jax.numpy as jnp
import numpy as np
from jax import lax
from jax.experimental import pallas as pl
from jax.experimental.pallas import tpu as pltpu
from jax.sharding import PartitionSpec as P

grad_scale = 0.0625
f32 = jnp.float32
bf16 = jnp.bfloat16
i32 = jnp.int32


def dot(a, b, dims):
    return lax.dot_general(a, b, (dims, ((), ())), preferred_element_type=f32)


def chunk_widths(width):
    lanes = width // 128
    shares = (3, 6, 9, 11)
    ends = [-(-lanes * x // 11) * 128 for x in shares]
    return [e - s for s, e in zip([0] + ends, ends) if e > s]


def chip_cycle(n_chips):
    cols = n_chips // 4
    if n_chips % 4 or cols < 2:
        return list(range(n_chips))
    walk = [(row, 0) for row in range(4)]
    for step, row in enumerate((3, 2, 1, 0)):
        across = range(1, cols) if step % 2 == 0 else range(cols - 1, 0, -1)
        walk += [(row, col) for col in across]
    return [row * cols + col for row, col in walk]


def put_rows(order, table, shards, rows, routed, cap):
    count = len(shards)
    n_peers, _, _ = table.shape
    width = shards[0][0].shape[1]

    def body(order_ref, table_ref, *refs):
        parts = refs[: 2 * count]
        rows_ref, routed_ref = refs[-2:]
        step = pl.program_id(0)
        for i in range(count):

            @pl.when(step == i)
            def _():
                info = table_ref[0]
                place = (
                    lax.broadcasted_iota(i32, (cap, tok_rows_of), 1).astype(f32) == info[:, 0:1]
                ).astype(bf16)
                rows_ref[...] = jnp.dot(
                    place, parts[2 * i][...], preferred_element_type=f32
                ).astype(bf16)
                picked = jnp.dot(place, parts[2 * i + 1][...], preferred_element_type=f32)
                routed_ref[...] = (info[:, 1:2] * picked).astype(bf16)

    tok_rows_of = shards[0][2]
    in_specs = [pl.BlockSpec((1, cap, 2), lambda i, order: (order[i], 0, 0))]
    operands = [table]
    for tok, grad, height, tok_at, grad_at in shards:
        in_specs.append(pl.BlockSpec((height, width), lambda i, order, a=tok_at: (a, 0)))
        in_specs.append(pl.BlockSpec((height, width), lambda i, order, a=grad_at: (a, 0)))
        operands += [tok, grad]
    aliases = {}
    if rows is not None:
        aliases = {1 + len(operands): 0, 2 + len(operands): 1}
        in_specs += [pl.BlockSpec(memory_space=pl.ANY)] * 2
        operands += [rows, routed]
    n_slots = n_peers * cap
    shape = jax.ShapeDtypeStruct((n_slots, width), bf16)
    out_spec = pl.BlockSpec((cap, width), lambda i, order: (order[i], 0))
    return pl.pallas_call(
        body,
        out_shape=(shape, shape),
        grid_spec=pltpu.PrefetchScalarGridSpec(
            num_scalar_prefetch=1,
            grid=(count,),
            in_specs=in_specs,
            out_specs=(out_spec, out_spec),
        ),
        input_output_aliases=aliases,
        compiler_params=pltpu.CompilerParams(vmem_limit_bytes=40 * 1024 * 1024),
        cost_estimate=pl.CostEstimate(
            flops=4 * count * cap * tok_rows_of * width,
            bytes_accessed=4 * count * (tok_rows_of + cap) * width,
            transcendentals=0,
        ),
        name="put_rows",
    )(order, *operands)


class Ring:
    def __init__(self):
        self.n_peers = lax.axis_size("expert")
        self.n = self.n_peers // 2
        self.far = self.n // 2
        self.names = [self.far]
        for d in range(self.far - 1, 0, -1):
            self.names += [d, -d]
        self.names.append(0)
        cycle = chip_cycle(self.n)
        spot = [cycle.index(c) for c in range(self.n)]
        chips = range(self.n)
        self.fwd = [(2 * cycle[i] + c, 2 * cycle[(i + 1) % self.n] + c) for i in chips for c in (0, 1)]
        self.bwd = [(b, a) for a, b in self.fwd]
        self.swap = [(i, i ^ 1) for i in range(self.n_peers)]
        table = np.zeros((self.n_peers, self.n_peers), np.int32)
        for e in range(self.n_peers):
            for core in (0, 1):
                for j, d in enumerate(self.names):
                    chip = cycle[(spot[e // 2] - d) % self.n]
                    table[e, core * self.n + j] = 2 * chip + (e % 2 if core else 1 - e % 2)
        self.order = jnp.asarray(table)[lax.axis_index("expert")]

    def at(self, distance, other):
        return self.names.index(distance) + (0 if other else self.n)

    def ahead(self, x):
        return lax.ppermute(x, "expert", self.fwd)

    def behind(self, x):
        return lax.ppermute(x, "expert", self.bwd)

    def other_core(self, x):
        return lax.ppermute(x, "expert", self.swap)


def gather_rows(ring, tokens, out_grad, table, cap):
    tok_rows = tokens.shape[0]
    own = jnp.concatenate([tokens, out_grad], axis=0)

    def whole(x):
        return (x, x, tok_rows, 0, 1)

    def place(spots, shards, state):
        return put_rows(np.array(spots, np.int32), table, shards, *state, cap)

    state = (None, None)
    ahead, behind = own, own
    pending = ([ring.at(0, False), ring.at(0, True)], [whole(own), whole(ring.other_core(own))])
    marks = []
    for d in range(1, ring.far):
        ahead, behind = ring.ahead(ahead), ring.behind(behind)
        state = place(*pending, state)
        ahead, behind, state = lax.optimization_barrier((ahead, behind, state))
        marks.append((ahead, behind))
        pending = (
            [ring.at(d, False), ring.at(-d, False), ring.at(d, True), ring.at(-d, True)],
            [whole(x) for x in (ahead, behind, ring.other_core(ahead), ring.other_core(behind))],
        )
    far_tok = ring.ahead(ahead[:tok_rows])
    far_grad = ring.behind(behind[tok_rows:])
    state = place(*pending, state)
    far_tok, far_grad, state = lax.optimization_barrier((far_tok, far_grad, state))
    marks.append((far_tok, far_grad))
    state = place(
        [ring.at(ring.far, False), ring.at(ring.far, True)],
        [
            (far_tok, far_grad, tok_rows, 0, 0),
            (ring.other_core(far_tok), ring.other_core(far_grad), tok_rows, 0, 0),
        ],
        state,
    )
    return state, marks


def sum_back(ring, terms, tok_rows):
    def block(d):
        j = ring.names.index(d) * tok_rows
        return terms[j : j + tok_rows]

    def plus(a, b):
        return (a.astype(f32) + b.astype(f32)).astype(bf16)

    half = tok_rows // 2
    top = ring.ahead(block(ring.far)[:half])
    low = ring.behind(block(ring.far)[half:])
    d = ring.far - 1
    if d == 0:
        return plus(block(0), jnp.concatenate([top, low], axis=0)), (top, low)
    ahead = jnp.concatenate([plus(block(-d)[:half], top), block(-d)[half:]], axis=0)
    behind = jnp.concatenate([block(d)[:half], plus(block(d)[half:], low)], axis=0)
    ahead, behind = ring.ahead(ahead), ring.behind(behind)
    for d in range(ring.far - 2, 0, -1):
        ahead, behind = ring.ahead(plus(block(-d), ahead)), ring.behind(plus(block(d), behind))
    return (block(0).astype(f32) + ahead.astype(f32) + behind.astype(f32)).astype(bf16), (top, low)


def blocks_per_step(n_blocks, cap):
    return max(b for b in range(1, n_blocks + 1) if n_blocks % b == 0 and b * cap <= 384)


LIGHT = pl.CostEstimate(flops=1000, bytes_accessed=1000, transcendentals=0)


def chunk_grads(order, rows, routed, gate, up_part, down_part):
    n_slots, width = rows.shape
    n_peers, cap, w = gate.shape
    n = blocks_per_step(n_peers, cap)
    r = n * cap

    def body(order_ref, rows_ref, routed_ref, up_ref, down_ref, *refs):
        gate_refs, (hidden_ref, both_ref) = refs[:n], refs[n:]
        up_all = jnp.dot(rows_ref[...], up_ref[...], preferred_element_type=f32)
        grad_all = dot(routed_ref[...], down_ref[...], ((1,), (1,)))
        for b in range(n):
            at = slice(b * cap, (b + 1) * cap)
            up_act, hidden_grad = up_all[at], grad_all[at]
            gate_val = gate_refs[b][0].astype(f32)
            gate_sig = jax.nn.sigmoid(gate_val)
            gate_act = gate_val * gate_sig
            hidden_ref[at, :] = (gate_act * up_act).astype(bf16)
            both_ref[at, w:] = (hidden_grad * gate_act).astype(bf16)
            both_ref[at, :w] = (
                hidden_grad * up_act * gate_sig * (1.0 + gate_val * (1.0 - gate_sig))
            ).astype(bf16)

    return pl.pallas_call(
        body,
        out_shape=(
            jax.ShapeDtypeStruct((n_slots, w), bf16),
            jax.ShapeDtypeStruct((n_slots, 2 * w), bf16),
        ),
        grid_spec=pltpu.PrefetchScalarGridSpec(
            num_scalar_prefetch=1,
            grid=(n_slots // r,),
            in_specs=[
                pl.BlockSpec((r, width), lambda i, order: (i, 0)),
                pl.BlockSpec((r, width), lambda i, order: (i, 0)),
                pl.BlockSpec((width, w), lambda i, order: (0, 0)),
                pl.BlockSpec((w, width), lambda i, order: (0, 0)),
            ]
            + [
                pl.BlockSpec((1, cap, w), lambda i, order, b=b: (order[n * i + b], 0, 0))
                for b in range(n)
            ],
            out_specs=(
                pl.BlockSpec((r, w), lambda i, order: (i, 0)),
                pl.BlockSpec((r, 2 * w), lambda i, order: (i, 0)),
            ),
        ),
        compiler_params=pltpu.CompilerParams(vmem_limit_bytes=40 * 1024 * 1024),
        cost_estimate=LIGHT,
        name="chunk_grads",
    )(order, rows, routed, up_part, down_part, *[gate] * n)


def spread_back(parts, starts, gate_mat, up_mat, table, tok_rows, first, add):
    n_peers, _, cap = table.shape
    half = n_peers // 2
    width, hidden_width = gate_mat.shape
    n_blocks = blocks_per_step(half, cap)
    cols = min(512, width)
    rows = n_blocks * cap
    shift = 0 if first else half // n_blocks

    def body(*refs):
        part_refs = refs[: len(parts)]
        gate_ref, up_ref, table_ref = refs[len(parts) : len(parts) + 3]
        out_ref = refs[-1]
        total = jnp.zeros((rows, cols), f32)
        for start, part_ref in zip(starts, part_refs):
            w = part_ref.shape[1] // 2
            total += dot(part_ref[:, :w], gate_ref[:, start : start + w], ((1,), (1,)))
            total += dot(part_ref[:, w:], up_ref[:, start : start + w], ((1,), (1,)))
        terms = total.astype(bf16)
        for b in range(n_blocks):
            tok = table_ref[b, 0:1, :]
            place = (lax.broadcasted_iota(i32, (tok_rows, cap), 0).astype(f32) == tok).astype(bf16)
            spread = jnp.dot(place, terms[b * cap : (b + 1) * cap], preferred_element_type=f32)
            at = slice(b * tok_rows, (b + 1) * tok_rows)
            if add is not None:
                spread = spread + refs[-2][at, :].astype(f32)
            out_ref[at, :] = spread.astype(bf16)

    out_spec = pl.BlockSpec((n_blocks * tok_rows, cols), lambda j, i: (i, j))
    return pl.pallas_call(
        body,
        out_shape=jax.ShapeDtypeStruct((half * tok_rows, width), bf16),
        grid=(width // cols, half // n_blocks),
        in_specs=[pl.BlockSpec((rows, x.shape[1]), lambda j, i: (i + shift, 0)) for x in parts]
        + [
            pl.BlockSpec((cols, hidden_width), lambda j, i: (j, 0)),
            pl.BlockSpec((cols, hidden_width), lambda j, i: (j, 0)),
            pl.BlockSpec((n_blocks, 2, cap), lambda j, i: (i + shift, 0, 0)),
        ]
        + ([out_spec] if add is not None else []),
        out_specs=out_spec,
        compiler_params=pltpu.CompilerParams(vmem_limit_bytes=40 * 1024 * 1024),
        cost_estimate=LIGHT,
        name="spread_back",
    )(*parts, gate_mat, up_mat, table, *([add] if add is not None else []))


def local(tokens, out_grad, gate_saved, probs, expert_ids, w_gate, w_up, w_down):
    n_peers = lax.axis_size("expert")
    n_dp = lax.axis_size("dp")
    group = lax.axis_index("dp")
    tok_rows, model_width = tokens.shape
    top_k = expert_ids.shape[1]
    hidden_width = w_up.shape[2]
    cap = min(tok_rows, 2 * tok_rows * top_k // n_peers)
    n_routes = tok_rows * top_k
    n_slots = n_peers * cap
    gate_mat, up_mat, down_mat = w_gate[0], w_up[0], w_down[0]

    experts = jnp.arange(n_peers, dtype=i32)
    hit = expert_ids[:, :, None] == experts[None, None, :]
    named = jnp.any(hit, axis=1)
    weight = jnp.sum(jnp.where(hit, probs[:, :, None], 0.0), axis=1)
    rank = jnp.cumsum(named.astype(i32), axis=0) - 1
    slots = jnp.arange(cap, dtype=i32)
    in_slot = named[:, :, None] & (rank[:, :, None] == slots[None, None, :])
    tok_of = jnp.sum(
        jnp.where(in_slot, jnp.arange(1, tok_rows + 1, dtype=f32)[:, None, None], 0.0), axis=0
    ) - 1.0
    weight_of = jnp.sum(jnp.where(in_slot, weight[:, :, None], 0.0), axis=0)
    table = lax.all_to_all(
        jnp.concatenate([tok_of, weight_of], axis=1),
        "expert",
        split_axis=0,
        concat_axis=0,
        tiled=True,
    )
    ring = Ring()
    table = table.reshape(n_peers, 2, cap)[ring.order]
    (rows_in, routed), marks = gather_rows(ring, tokens, out_grad, table.transpose(0, 2, 1), cap)

    pick = (
        hit[:, :, :, None] & (rank[:, None, :, None] == slots[None, None, None, :])
    ).astype(bf16)
    send_gate = lax.dot_general(
        pick.reshape(n_routes, n_slots),
        gate_saved.reshape(n_routes, hidden_width),
        (((0,), (0,)), ((), ())),
        preferred_element_type=f32,
    ).astype(bf16).reshape(n_peers, cap, hidden_width)

    widths = chunk_widths(hidden_width)
    starts = [sum(widths[:i]) for i in range(len(widths))]

    def send_chunk(i, mark):
        part = send_gate[:, :, starts[i] : starts[i] + widths[i]]
        part, _ = lax.optimization_barrier((part, mark))
        return lax.all_to_all(part, "expert", split_axis=0, concat_axis=0, tiled=True)

    recv_gate = [send_chunk(i, marks[m]) for i, m in zip(range(len(widths)), (min(1, len(marks) - 1), -1))]

    piece = model_width // n_dp
    shifts = [[(i, (i + d) % n_dp) for i in range(n_dp)] for d in range(n_dp)]

    def rows_of(rows, d):
        q = lax.rem(group + d, n_dp)
        return lax.dynamic_slice_in_dim(rows, q * piece, piece, 1)

    up_parts = [up_mat[:, s : s + w] for s, w in zip(starts, widths)]
    down_parts = [down_mat[s : s + w] for s, w in zip(starts, widths)]
    up_parts, down_parts, _ = lax.optimization_barrier((up_parts, down_parts, marks[0]))
    hidden_parts, both_parts, arrivals = [], [], []
    rows_now, routed_now = rows_in, routed
    for c, w in enumerate(widths):
        hidden, both = chunk_grads(
            ring.order, rows_now, routed_now, recv_gate[c], up_parts[c], down_parts[c]
        )
        hidden_parts.append(hidden)
        both_parts.append(both)
        arrived, sent = [], []
        for d in range(1, n_dp):
            part = dot(rows_of(rows_now, d), both, ((0,), (0,))).astype(bf16)
            sent.append(part)
            arrived.append(lax.ppermute(part, "dp", shifts[d]))
        arrivals.append(arrived)
        rows_now, routed_now, _ = lax.optimization_barrier((rows_now, routed_now, sent))
        if c + 2 < len(widths):
            recv_gate.append(send_chunk(c + 2, sent))
        if c >= 1:
            rows_now, arrivals[c - 1] = lax.optimization_barrier((rows_now, arrivals[c - 1]))

    last, _ = lax.optimization_barrier((both_parts[-1], sent))
    parts = both_parts[:-1] + [last]
    theirs = spread_back(parts, starts, gate_mat, up_mat, table, tok_rows, True, None)
    mine = ring.other_core(theirs)

    hidden_act = jnp.concatenate(hidden_parts, axis=1)
    hidden_act, rows_now, _ = lax.optimization_barrier((hidden_act, rows_now, theirs))
    sum_down = dot(hidden_act, routed_now, ((0,), (0,))).astype(bf16)
    mine, rows_now, _ = lax.optimization_barrier((mine, rows_now, sum_down))
    terms = spread_back(parts, starts, gate_mat, up_mat, table, tok_rows, False, mine)
    input_grad, mark = sum_back(ring, terms, tok_rows)
    rows_now, arrivals[-1], _ = lax.optimization_barrier((rows_now, arrivals[-1], mark))

    low = hidden_width // n_dp
    arrived = []
    for d in range(1, n_dp):
        q = lax.rem(group + d, n_dp)
        part = lax.dynamic_slice_in_dim(sum_down, q * low, low, 0)
        arrived.append(lax.ppermute(part, "dp", shifts[d]))
    arrived, _ = lax.optimization_barrier((arrived, input_grad))
    down = lax.dynamic_slice_in_dim(sum_down, group * low, low, 0).astype(f32)
    for part in arrived:
        down = down + part.astype(f32)
    grad_down = (grad_scale * down).astype(bf16)[None]

    gate_out, up_out = [], []
    for w, both, arrived in zip(widths, both_parts, arrivals):
        total = dot(rows_of(rows_now, 0), both, ((0,), (0,))).astype(bf16).astype(f32)
        for part in arrived:
            total = total + part.astype(f32)
        total = (grad_scale * total).astype(bf16)
        gate_out.append(total[:, :w])
        up_out.append(total[:, w:])
    grad_gate = jnp.concatenate(gate_out, axis=1)[None]
    grad_up = jnp.concatenate(up_out, axis=1)[None]
    return (input_grad, grad_gate, grad_up, grad_down)


def solution(mesh):
    return jax.shard_map(
        local,
        mesh=mesh,
        in_specs=(
            P(("dp", "expert"), None),
            P(("dp", "expert"), None),
            P(("dp", "expert"), None, None),
            P(("dp", "expert"), None),
            P(("dp", "expert"), None),
            P("expert", None, None),
            P("expert", None, None),
            P("expert", None, None),
        ),
        out_specs=(
            P(("dp", "expert"), None),
            P("expert", "dp", None),
            P("expert", "dp", None),
            P("expert", "dp", None),
        ),
        check_vma=False,
    )
```

```python
import jax
import jax.numpy as jnp
import numpy as np
from jax import lax
from jax.experimental import pallas as pl
from jax.experimental.pallas import tpu as pltpu
from jax.sharding import PartitionSpec as P

grad_scale = 0.0625
f32 = jnp.float32
bf16 = jnp.bfloat16
i32 = jnp.int32
KERNEL_VMEM = 60 * 1024 * 1024


def dot(a, b, dims):
    return lax.dot_general(a, b, (dims, ((), ())), preferred_element_type=f32)


def chunk_widths(width):
    lanes = width // 128
    shares = (3, 6, 9, 11)
    ends = [-(-lanes * x // 11) * 128 for x in shares]
    return [e - s for s, e in zip([0] + ends, ends) if e > s]


def chip_cycle(n_chips):
    cols = n_chips // 4
    if n_chips % 4 or cols < 2:
        return list(range(n_chips))
    walk = [(row, 0) for row in range(4)]
    for step, row in enumerate((3, 2, 1, 0)):
        across = range(1, cols) if step % 2 == 0 else range(cols - 1, 0, -1)
        walk += [(row, col) for col in across]
    return [row * cols + col for row, col in walk]


def put_rows(order, table, shards, rows, routed, cap):
    count = len(shards)
    n_peers, _, _ = table.shape
    width = shards[0][0].shape[1]

    def body(order_ref, table_ref, *refs):
        parts = refs[: 2 * count]
        rows_ref, routed_ref = refs[-2:]
        step = pl.program_id(0)
        for i in range(count):

            @pl.when(step == i)
            def _():
                info = table_ref[0]
                place = (
                    lax.broadcasted_iota(i32, (cap, tok_rows_of), 1).astype(f32) == info[:, 0:1]
                ).astype(bf16)
                rows_ref[...] = jnp.dot(
                    place, parts[2 * i][...], preferred_element_type=f32
                ).astype(bf16)
                picked = jnp.dot(place, parts[2 * i + 1][...], preferred_element_type=f32)
                routed_ref[...] = (info[:, 1:2] * picked).astype(bf16)

    tok_rows_of = shards[0][2]
    in_specs = [pl.BlockSpec((1, cap, 2), lambda i, order: (order[i], 0, 0))]
    operands = [table]
    for tok, grad, height, tok_at, grad_at in shards:
        in_specs.append(pl.BlockSpec((height, width), lambda i, order, a=tok_at: (a, 0)))
        in_specs.append(pl.BlockSpec((height, width), lambda i, order, a=grad_at: (a, 0)))
        operands += [tok, grad]
    aliases = {}
    if rows is not None:
        aliases = {1 + len(operands): 0, 2 + len(operands): 1}
        in_specs += [pl.BlockSpec(memory_space=pl.ANY)] * 2
        operands += [rows, routed]
    n_slots = n_peers * cap
    shape = jax.ShapeDtypeStruct((n_slots, width), bf16)
    out_spec = pl.BlockSpec((cap, width), lambda i, order: (order[i], 0))
    return pl.pallas_call(
        body,
        out_shape=(shape, shape),
        grid_spec=pltpu.PrefetchScalarGridSpec(
            num_scalar_prefetch=1,
            grid=(count,),
            in_specs=in_specs,
            out_specs=(out_spec, out_spec),
        ),
        input_output_aliases=aliases,
        compiler_params=pltpu.CompilerParams(vmem_limit_bytes=KERNEL_VMEM),
        cost_estimate=pl.CostEstimate(
            flops=4 * count * cap * tok_rows_of * width,
            bytes_accessed=4 * count * (tok_rows_of + cap) * width,
            transcendentals=0,
        ),
        name="put_rows",
    )(order, *operands)


class Ring:
    def __init__(self):
        self.n_peers = lax.axis_size("expert")
        self.n = self.n_peers // 2
        self.far = self.n // 2
        self.names = [self.far]
        for d in range(self.far - 1, 0, -1):
            self.names += [d, -d]
        self.names.append(0)
        cycle = chip_cycle(self.n)
        spot = [cycle.index(c) for c in range(self.n)]
        chips = range(self.n)
        self.fwd = [(2 * cycle[i] + c, 2 * cycle[(i + 1) % self.n] + c) for i in chips for c in (0, 1)]
        self.bwd = [(b, a) for a, b in self.fwd]
        self.swap = [(i, i ^ 1) for i in range(self.n_peers)]
        table = np.zeros((self.n_peers, self.n_peers), np.int32)
        for e in range(self.n_peers):
            for core in (0, 1):
                for j, d in enumerate(self.names):
                    chip = cycle[(spot[e // 2] - d) % self.n]
                    table[e, core * self.n + j] = 2 * chip + (e % 2 if core else 1 - e % 2)
        self.order = jnp.asarray(table)[lax.axis_index("expert")]

    def at(self, distance, other):
        return self.names.index(distance) + (0 if other else self.n)

    def ahead(self, x):
        return lax.ppermute(x, "expert", self.fwd)

    def behind(self, x):
        return lax.ppermute(x, "expert", self.bwd)

    def other_core(self, x):
        return lax.ppermute(x, "expert", self.swap)


def gather_rows(ring, tokens, out_grad, table, cap, beside):
    tok_rows = tokens.shape[0]
    own = jnp.concatenate([tokens, out_grad], axis=0)
    beside = list(beside)

    def whole(x):
        return (x, x, tok_rows, 0, 1)

    def place(spots, shards, state):
        return put_rows(np.array(spots, np.int32), table, shards, *state, cap)

    state = (None, None)
    ahead, behind = own, own
    pending = ([ring.at(0, False), ring.at(0, True)], [whole(own), whole(ring.other_core(own))])
    marks = []
    for d in range(1, ring.far):
        ahead, behind = ring.ahead(ahead), ring.behind(behind)
        if d >= 2:
            state = place(*pending[0], state)
            pending = pending[1:]
            ahead, behind, state = lax.optimization_barrier((ahead, behind, state))
            if d - 2 < len(beside):
                ahead, behind, beside[d - 2] = lax.optimization_barrier(
                    (ahead, behind, beside[d - 2])
                )
        else:
            pending = [pending]
        marks.append((ahead, behind))
        pending.append(
            (
                [ring.at(d, False), ring.at(-d, False), ring.at(d, True), ring.at(-d, True)],
                [whole(x) for x in (ahead, behind, ring.other_core(ahead), ring.other_core(behind))],
            )
        )
    far_tok = ring.ahead(ahead[:tok_rows])
    far_grad = ring.behind(behind[tok_rows:])
    state = place(*pending[0], state)
    far_tok, far_grad, state = lax.optimization_barrier((far_tok, far_grad, state))
    marks.append((far_tok, far_grad))
    for spots, shards in pending[1:]:
        state = place(spots, shards, state)
    state = place(
        [ring.at(ring.far, False), ring.at(ring.far, True)],
        [
            (far_tok, far_grad, tok_rows, 0, 0),
            (ring.other_core(far_tok), ring.other_core(far_grad), tok_rows, 0, 0),
        ],
        state,
    )
    return state, marks, beside


def sum_back(ring, theirs, mine, tok_rows, beside):
    def rows(x, j, n=1):
        return x[j * tok_rows : (j + n) * tok_rows]

    handed = {ring.far: ring.other_core(rows(theirs, 0))}
    for j in range(1, 2 * ring.far - 1, 2):
        pair = ring.other_core(rows(theirs, j, 2))
        handed[ring.names[j]], handed[ring.names[j + 1]] = rows(pair, 0), rows(pair, 1)
    if ring.far > 0:
        handed[0] = ring.other_core(rows(theirs, 2 * ring.far - 1))

    def block(d):
        return rows(mine, ring.names.index(d)).astype(f32) + handed[d].astype(f32)

    def plus(d, *others):
        total = block(d)
        for x in others:
            total = total + x.astype(f32)
        return total.astype(bf16)

    half = tok_rows // 2
    first = plus(ring.far)
    top, low = ring.ahead(first[:half]), ring.behind(first[half:])
    top, low, beside = lax.optimization_barrier((top, low, beside))
    none = jnp.zeros_like(top)
    ahead = jnp.concatenate([top, none], axis=0)
    behind = jnp.concatenate([none, low], axis=0)
    for d in range(ring.far - 1, 0, -1):
        ahead, behind = ring.ahead(plus(-d, ahead)), ring.behind(plus(d, behind))
    return plus(0, ahead, behind), beside


def blocks_per_step(n_blocks, cap):
    return max(b for b in range(1, n_blocks + 1) if n_blocks % b == 0 and b * cap <= 384)


LIGHT = pl.CostEstimate(flops=1000, bytes_accessed=1000, transcendentals=0)


def chunk_grads(order, rows, routed, gate, up_part, down_part):
    n_slots, width = rows.shape
    n_peers, cap, w = gate.shape
    n = blocks_per_step(n_peers, cap)
    r = n * cap

    def body(order_ref, rows_ref, routed_ref, up_ref, down_ref, *refs):
        gate_refs, (hidden_ref, both_ref) = refs[:n], refs[n:]
        up_all = jnp.dot(rows_ref[...], up_ref[...], preferred_element_type=f32)
        grad_all = dot(routed_ref[...], down_ref[...], ((1,), (1,)))
        for b in range(n):
            at = slice(b * cap, (b + 1) * cap)
            up_act, hidden_grad = up_all[at], grad_all[at]
            gate_val = gate_refs[b][0].astype(f32)
            gate_sig = jax.nn.sigmoid(gate_val)
            gate_act = gate_val * gate_sig
            hidden_ref[at, :] = (gate_act * up_act).astype(bf16)
            both_ref[at, w:] = (hidden_grad * gate_act).astype(bf16)
            both_ref[at, :w] = (
                hidden_grad * up_act * gate_sig * (1.0 + gate_val * (1.0 - gate_sig))
            ).astype(bf16)

    return pl.pallas_call(
        body,
        out_shape=(
            jax.ShapeDtypeStruct((n_slots, w), bf16),
            jax.ShapeDtypeStruct((n_slots, 2 * w), bf16),
        ),
        grid_spec=pltpu.PrefetchScalarGridSpec(
            num_scalar_prefetch=1,
            grid=(n_slots // r,),
            in_specs=[
                pl.BlockSpec((r, width), lambda i, order: (i, 0)),
                pl.BlockSpec((r, width), lambda i, order: (i, 0)),
                pl.BlockSpec((width, w), lambda i, order: (0, 0)),
                pl.BlockSpec((w, width), lambda i, order: (0, 0)),
            ]
            + [
                pl.BlockSpec((1, cap, w), lambda i, order, b=b: (order[n * i + b], 0, 0))
                for b in range(n)
            ],
            out_specs=(
                pl.BlockSpec((r, w), lambda i, order: (i, 0)),
                pl.BlockSpec((r, 2 * w), lambda i, order: (i, 0)),
            ),
        ),
        compiler_params=pltpu.CompilerParams(vmem_limit_bytes=KERNEL_VMEM),
        cost_estimate=LIGHT,
        name="chunk_grads",
    )(order, rows, routed, up_part, down_part, *[gate] * n)


def spread_back(parts, starts, gate_mat, up_mat, table, tok_rows, first):
    n_peers, _, cap = table.shape
    half = n_peers // 2
    width, hidden_width = gate_mat.shape
    n_blocks = blocks_per_step(half, cap)
    cols = min(512, width)
    rows = n_blocks * cap
    shift = 0 if first else half // n_blocks

    def body(*refs):
        part_refs = refs[: len(parts)]
        gate_ref, up_ref, table_ref = refs[len(parts) : len(parts) + 3]
        out_ref = refs[-1]
        total = jnp.zeros((rows, cols), f32)
        for start, part_ref in zip(starts, part_refs):
            w = part_ref.shape[1] // 2
            total += dot(part_ref[:, :w], gate_ref[:, start : start + w], ((1,), (1,)))
            total += dot(part_ref[:, w:], up_ref[:, start : start + w], ((1,), (1,)))
        terms = total.astype(bf16)
        for b in range(n_blocks):
            tok = table_ref[b, 0:1, :]
            place = (lax.broadcasted_iota(i32, (tok_rows, cap), 0).astype(f32) == tok).astype(bf16)
            spread = jnp.dot(place, terms[b * cap : (b + 1) * cap], preferred_element_type=f32)
            out_ref[b * tok_rows : (b + 1) * tok_rows, :] = spread.astype(bf16)

    return pl.pallas_call(
        body,
        out_shape=jax.ShapeDtypeStruct((half * tok_rows, width), bf16),
        grid=(width // cols, half // n_blocks),
        in_specs=[pl.BlockSpec((rows, x.shape[1]), lambda j, i: (i + shift, 0)) for x in parts]
        + [
            pl.BlockSpec((cols, hidden_width), lambda j, i: (j, 0)),
            pl.BlockSpec((cols, hidden_width), lambda j, i: (j, 0)),
            pl.BlockSpec((n_blocks, 2, cap), lambda j, i: (i + shift, 0, 0)),
        ],
        out_specs=pl.BlockSpec((n_blocks * tok_rows, cols), lambda j, i: (i, j)),
        compiler_params=pltpu.CompilerParams(vmem_limit_bytes=KERNEL_VMEM),
        cost_estimate=LIGHT,
        name="spread_back",
    )(*parts, gate_mat, up_mat, table)


def local(tokens, out_grad, gate_saved, probs, expert_ids, w_gate, w_up, w_down):
    n_peers = lax.axis_size("expert")
    n_dp = lax.axis_size("dp")
    group = lax.axis_index("dp")
    tok_rows, model_width = tokens.shape
    top_k = expert_ids.shape[1]
    hidden_width = w_up.shape[2]
    cap = min(tok_rows, 2 * tok_rows * top_k // n_peers)
    n_routes = tok_rows * top_k
    n_slots = n_peers * cap
    gate_mat, up_mat, down_mat = w_gate[0], w_up[0], w_down[0]

    experts = jnp.arange(n_peers, dtype=i32)
    hit = expert_ids[:, :, None] == experts[None, None, :]
    named = jnp.any(hit, axis=1)
    weight = jnp.sum(jnp.where(hit, probs[:, :, None], 0.0), axis=1)
    rank = jnp.cumsum(named.astype(i32), axis=0) - 1
    slots = jnp.arange(cap, dtype=i32)
    in_slot = named[:, :, None] & (rank[:, :, None] == slots[None, None, :])
    tok_of = jnp.sum(
        jnp.where(in_slot, jnp.arange(1, tok_rows + 1, dtype=f32)[:, None, None], 0.0), axis=0
    ) - 1.0
    weight_of = jnp.sum(jnp.where(in_slot, weight[:, :, None], 0.0), axis=0)
    table = lax.all_to_all(
        jnp.concatenate([tok_of, weight_of], axis=1),
        "expert",
        split_axis=0,
        concat_axis=0,
        tiled=True,
    )
    ring = Ring()
    table = table.reshape(n_peers, 2, cap)[ring.order]
    pick = (
        hit[:, :, :, None] & (rank[:, None, :, None] == slots[None, None, None, :])
    ).astype(bf16)
    send_gate = lax.dot_general(
        pick.reshape(n_routes, n_slots),
        gate_saved.reshape(n_routes, hidden_width),
        (((0,), (0,)), ((), ())),
        preferred_element_type=f32,
    ).astype(bf16).reshape(n_peers, cap, hidden_width)

    widths = chunk_widths(hidden_width)
    starts = [sum(widths[:i]) for i in range(len(widths))]
    up_parts = [up_mat[:, s : s + w] for s, w in zip(starts, widths)]
    down_parts = [down_mat[s : s + w] for s, w in zip(starts, widths)]
    (rows_in, routed), marks, (send_gate, (up_parts, down_parts)) = gather_rows(
        ring, tokens, out_grad, table.transpose(0, 2, 1), cap, [send_gate, (up_parts, down_parts)]
    )

    def send_chunk(i, mark):
        part = send_gate[:, :, starts[i] : starts[i] + widths[i]]
        part, _ = lax.optimization_barrier((part, mark))
        return lax.all_to_all(part, "expert", split_axis=0, concat_axis=0, tiled=True)

    recv_gate = [send_chunk(i, marks[m]) for i, m in zip(range(len(widths)), (min(1, len(marks) - 1), -1))]

    piece = model_width // n_dp
    shifts = [[(i, (i + d) % n_dp) for i in range(n_dp)] for d in range(n_dp)]

    def rows_of(rows, d):
        q = lax.rem(group + d, n_dp)
        return lax.dynamic_slice_in_dim(rows, q * piece, piece, 1)

    hidden_parts, both_parts, arrivals, own_parts, down_sums = [], [], [], [], []
    rows_now, routed_now = rows_in, routed
    for c, w in enumerate(widths):
        hidden, both = chunk_grads(
            ring.order, rows_now, routed_now, recv_gate[c], up_parts[c], down_parts[c]
        )
        both_parts.append(both)
        arrived, sent = [], []
        for d in range(1, n_dp):
            part = dot(rows_of(rows_now, d), both, ((0,), (0,))).astype(bf16)
            sent.append(part)
            arrived.append(lax.ppermute(part, "dp", shifts[d]))
        arrivals.append(arrived)
        rows_now, routed_now, _ = lax.optimization_barrier((rows_now, routed_now, sent))
        if c + 2 < len(widths):
            recv_gate.append(send_chunk(c + 2, sent))
        if c + 1 < len(widths):
            own_parts.append(dot(rows_of(rows_now, 0), both, ((0,), (0,))).astype(bf16))
            down_sums.append(dot(hidden, routed_now, ((0,), (0,))).astype(bf16))
            if c >= 1:
                rows_now, arrivals[c - 1] = lax.optimization_barrier((rows_now, arrivals[c - 1]))
            rows_now, routed_now, own_parts[c], down_sums[c] = lax.optimization_barrier(
                (rows_now, routed_now, own_parts[c], down_sums[c])
            )

    last, _ = lax.optimization_barrier((both_parts[-1], sent))
    parts = both_parts[:-1] + [last]
    theirs = spread_back(parts, starts, gate_mat, up_mat, table, tok_rows, True)
    last, arrivals[:-1], _ = lax.optimization_barrier((last, arrivals[:-1], theirs))
    mine = spread_back(both_parts[:-1] + [last], starts, gate_mat, up_mat, table, tok_rows, False)

    hidden, rows_now, _ = lax.optimization_barrier((hidden, rows_now, mine))
    down_sums.append(dot(hidden, routed_now, ((0,), (0,))).astype(bf16))
    sum_down = jnp.concatenate(down_sums, axis=0)
    low = hidden_width // n_dp
    sent = []
    for d in range(1, n_dp):
        q = lax.rem(group + d, n_dp)
        sent.append(lax.dynamic_slice_in_dim(sum_down, q * low, low, 0))
    input_grad, sent = sum_back(ring, theirs, mine, tok_rows, sent)
    arrived = [lax.ppermute(part, "dp", shifts[d]) for d, part in enumerate(sent, 1)]
    rows_now, arrivals[-1], _ = lax.optimization_barrier((rows_now, arrivals[-1], sent))
    own_parts.append(dot(rows_of(rows_now, 0), both, ((0,), (0,))).astype(bf16))
    arrived, _ = lax.optimization_barrier((arrived, input_grad))
    down = lax.dynamic_slice_in_dim(sum_down, group * low, low, 0).astype(f32)
    for part in arrived:
        down = down + part.astype(f32)
    grad_down = (grad_scale * down).astype(bf16)[None]

    gate_out, up_out = [], []
    for w, own, arrived in zip(widths, own_parts, arrivals):
        total = own.astype(f32)
        for part in arrived:
            total = total + part.astype(f32)
        total = (grad_scale * total).astype(bf16)
        gate_out.append(total[:, :w])
        up_out.append(total[:, w:])
    grad_gate = jnp.concatenate(gate_out, axis=1)[None]
    grad_up = jnp.concatenate(up_out, axis=1)[None]
    return (input_grad, grad_gate, grad_up, grad_down)


def solution(mesh):
    return jax.shard_map(
        local,
        mesh=mesh,
        in_specs=(
            P(("dp", "expert"), None),
            P(("dp", "expert"), None),
            P(("dp", "expert"), None, None),
            P(("dp", "expert"), None),
            P(("dp", "expert"), None),
            P("expert", None, None),
            P("expert", None, None),
            P("expert", None, None),
        ),
        out_specs=(
            P(("dp", "expert"), None),
            P("expert", "dp", None),
            P("expert", "dp", None),
            P("expert", "dp", None),
        ),
        check_vma=False,
    )
```

```python
import jax
import jax.numpy as jnp
import numpy as np
from jax import lax
from jax.experimental import pallas as pl
from jax.experimental.pallas import tpu as pltpu
from jax.sharding import PartitionSpec as P

grad_scale = 0.0625
f32 = jnp.float32
bf16 = jnp.bfloat16
i32 = jnp.int32
KERNEL_VMEM = 60 * 1024 * 1024
COLS = 256


def dot(a, b, dims):
    return lax.dot_general(a, b, (dims, ((), ())), preferred_element_type=f32)


def chunk_widths(width):
    lanes = width // 128
    shares = (3, 6, 9, 11)
    ends = [-(-lanes * x // 11) * 128 for x in shares]
    return [e - s for s, e in zip([0] + ends, ends) if e > s]


def chip_cycle(n_chips):
    cols = n_chips // 4
    if n_chips % 4 or cols < 2:
        return list(range(n_chips))
    walk = [(row, 0) for row in range(4)]
    for step, row in enumerate((3, 2, 1, 0)):
        across = range(1, cols) if step % 2 == 0 else range(cols - 1, 0, -1)
        walk += [(row, col) for col in across]
    return [row * cols + col for row, col in walk]


def put_rows(order, table, shards, rows, routed, cap):
    count = len(shards)
    n_peers, _, _ = table.shape
    width = shards[0][0].shape[1]

    def body(order_ref, table_ref, *refs):
        parts = refs[: 2 * count]
        rows_ref, routed_ref = refs[-2:]
        step = pl.program_id(0)
        for i in range(count):

            @pl.when(step == i)
            def _():
                info = table_ref[0]
                place = (
                    lax.broadcasted_iota(i32, (cap, tok_rows_of), 1).astype(f32) == info[:, 0:1]
                ).astype(bf16)
                rows_ref[...] = jnp.dot(
                    place, parts[2 * i][...], preferred_element_type=f32
                ).astype(bf16)
                picked = jnp.dot(place, parts[2 * i + 1][...], preferred_element_type=f32)
                routed_ref[...] = (info[:, 1:2] * picked).astype(bf16)

    tok_rows_of = shards[0][2]
    in_specs = [pl.BlockSpec((1, cap, 2), lambda i, order: (order[i], 0, 0))]
    operands = [table]
    for tok, grad, height, tok_at, grad_at in shards:
        in_specs.append(pl.BlockSpec((height, width), lambda i, order, a=tok_at: (a, 0)))
        in_specs.append(pl.BlockSpec((height, width), lambda i, order, a=grad_at: (a, 0)))
        operands += [tok, grad]
    aliases = {}
    if rows is not None:
        aliases = {1 + len(operands): 0, 2 + len(operands): 1}
        in_specs += [pl.BlockSpec(memory_space=pl.ANY)] * 2
        operands += [rows, routed]
    n_slots = n_peers * cap
    shape = jax.ShapeDtypeStruct((n_slots, width), bf16)
    out_spec = pl.BlockSpec((cap, width), lambda i, order: (order[i], 0))
    return pl.pallas_call(
        body,
        out_shape=(shape, shape),
        grid_spec=pltpu.PrefetchScalarGridSpec(
            num_scalar_prefetch=1,
            grid=(count,),
            in_specs=in_specs,
            out_specs=(out_spec, out_spec),
        ),
        input_output_aliases=aliases,
        compiler_params=pltpu.CompilerParams(vmem_limit_bytes=KERNEL_VMEM),
        cost_estimate=pl.CostEstimate(
            flops=4 * count * cap * tok_rows_of * width,
            bytes_accessed=4 * count * (tok_rows_of + cap) * width,
            transcendentals=0,
        ),
        name="put_rows",
    )(order, *operands)


class Ring:
    def __init__(self):
        self.n_peers = lax.axis_size("expert")
        self.n = self.n_peers // 2
        self.far = self.n // 2
        self.names = [self.far]
        for d in range(self.far - 1, 0, -1):
            self.names += [d, -d]
        self.names.append(0)
        cycle = chip_cycle(self.n)
        spot = [cycle.index(c) for c in range(self.n)]
        chips = range(self.n)
        self.fwd = [(2 * cycle[i] + c, 2 * cycle[(i + 1) % self.n] + c) for i in chips for c in (0, 1)]
        self.bwd = [(b, a) for a, b in self.fwd]
        self.swap = [(i, i ^ 1) for i in range(self.n_peers)]
        table = np.zeros((self.n_peers, self.n_peers), np.int32)
        for e in range(self.n_peers):
            for core in (0, 1):
                for j, d in enumerate(self.names):
                    chip = cycle[(spot[e // 2] - d) % self.n]
                    table[e, core * self.n + j] = 2 * chip + (e % 2 if core else 1 - e % 2)
        self.order = jnp.asarray(table)[lax.axis_index("expert")]

    def at(self, distance, other):
        return self.names.index(distance) + (0 if other else self.n)

    def ahead(self, x):
        return lax.ppermute(x, "expert", self.fwd)

    def behind(self, x):
        return lax.ppermute(x, "expert", self.bwd)

    def other_core(self, x):
        return lax.ppermute(x, "expert", self.swap)


def gather_rows(ring, tokens, out_grad, table, cap, beside):
    tok_rows = tokens.shape[0]
    own = jnp.concatenate([tokens, out_grad], axis=0)
    beside = list(beside)

    def whole(x):
        return (x, x, tok_rows, 0, 1)

    def place(spots, shards, state):
        return put_rows(np.array(spots, np.int32), table, shards, *state, cap)

    state = (None, None)
    ahead, behind = own, own
    pending = ([ring.at(0, False), ring.at(0, True)], [whole(own), whole(ring.other_core(own))])
    marks = []
    for d in range(1, ring.far):
        ahead, behind = ring.ahead(ahead), ring.behind(behind)
        if d >= 2:
            state = place(*pending[0], state)
            pending = pending[1:]
            ahead, behind, state = lax.optimization_barrier((ahead, behind, state))
            if d - 2 < len(beside):
                ahead, behind, beside[d - 2] = lax.optimization_barrier(
                    (ahead, behind, beside[d - 2])
                )
        else:
            pending = [pending]
        marks.append((ahead, behind))
        pending.append(
            (
                [ring.at(d, False), ring.at(-d, False), ring.at(d, True), ring.at(-d, True)],
                [whole(x) for x in (ahead, behind, ring.other_core(ahead), ring.other_core(behind))],
            )
        )
    far_tok = ring.ahead(ahead[:tok_rows])
    far_grad = ring.behind(behind[tok_rows:])
    state = place(*pending[0], state)
    far_tok, far_grad, state = lax.optimization_barrier((far_tok, far_grad, state))
    marks.append((far_tok, far_grad))
    for spots, shards in pending[1:]:
        state = place(spots, shards, state)
    state = place(
        [ring.at(ring.far, False), ring.at(ring.far, True)],
        [
            (far_tok, far_grad, tok_rows, 0, 0),
            (ring.other_core(far_tok), ring.other_core(far_grad), tok_rows, 0, 0),
        ],
        state,
    )
    return state, marks, beside


def sum_back(ring, theirs, mine, tok_rows, beside):
    handed, ours = {}, {}
    j = 0
    for piece, own in zip(theirs, mine):
        piece = ring.other_core(piece)
        for at in range(0, piece.shape[0], tok_rows):
            handed[ring.names[j]] = piece[at : at + tok_rows]
            ours[ring.names[j]] = own[at : at + tok_rows]
            j += 1

    def plus(d, *others):
        total = ours[d].astype(f32) + handed[d].astype(f32)
        for x in others:
            total = total + x.astype(f32)
        return total.astype(bf16)

    half = tok_rows // 2
    first = plus(ring.far)
    top, low = ring.ahead(first[:half]), ring.behind(first[half:])
    top, low, beside = lax.optimization_barrier((top, low, beside))
    none = jnp.zeros_like(top)
    ahead = jnp.concatenate([top, none], axis=0)
    behind = jnp.concatenate([none, low], axis=0)
    for d in range(ring.far - 1, 0, -1):
        ahead, behind = ring.ahead(plus(-d, ahead)), ring.behind(plus(d, behind))
    return plus(0, ahead, behind), beside


def blocks_per_step(n_blocks, cap):
    return max(b for b in range(1, n_blocks + 1) if n_blocks % b == 0 and b * cap <= 384)


LIGHT = pl.CostEstimate(flops=1000, bytes_accessed=1000, transcendentals=0)


def chunk_grads(order, cols, rows, routed, gate, up_part, down_part):
    n_slots, width = rows.shape
    n_peers, cap, w = gate.shape
    n = blocks_per_step(n_peers, cap)
    r = n * cap
    n_rows, n_cols = n_slots // r, cols.shape[0]

    def body(order_ref, cols_ref, rows_ref, routed_ref, up_ref, down_ref, col_ref, *refs):
        gate_refs, (hidden_ref, both_ref, part_ref, held) = refs[:n], refs[n:]
        step = pl.program_id(0)

        @pl.when(step < n_rows)
        def _():
            up_all = jnp.dot(rows_ref[...], up_ref[...], preferred_element_type=f32)
            grad_all = dot(routed_ref[...], down_ref[...], ((1,), (1,)))
            for b in range(n):
                at = slice(b * cap, (b + 1) * cap)
                up_act, hidden_grad = up_all[at], grad_all[at]
                gate_val = gate_refs[b][0].astype(f32)
                gate_sig = jax.nn.sigmoid(gate_val)
                gate_act = gate_val * gate_sig
                hidden_ref[at, :] = (gate_act * up_act).astype(bf16)
                both_ref[at, w:] = (hidden_grad * gate_act).astype(bf16)
                both_ref[at, :w] = (
                    hidden_grad * up_act * gate_sig * (1.0 + gate_val * (1.0 - gate_sig))
                ).astype(bf16)
            held[pl.ds(pl.multiple_of(step * r, r), r), :] = both_ref[...]

        @pl.when(step >= n_rows)
        def _():
            part_ref[...] = dot(col_ref[...], held[...], ((0,), (0,))).astype(bf16)

    def row(i):
        return jnp.minimum(i, n_rows - 1)

    def col(i):
        return jnp.maximum(i - n_rows, 0)

    return pl.pallas_call(
        body,
        out_shape=(
            jax.ShapeDtypeStruct((n_slots, w), bf16),
            jax.ShapeDtypeStruct((n_slots, 2 * w), bf16),
            jax.ShapeDtypeStruct((n_cols * COLS, 2 * w), bf16),
        ),
        grid_spec=pltpu.PrefetchScalarGridSpec(
            num_scalar_prefetch=2,
            grid=(n_rows + n_cols,),
            in_specs=[
                pl.BlockSpec((r, width), lambda i, order, cols: (row(i), 0)),
                pl.BlockSpec((r, width), lambda i, order, cols: (row(i), 0)),
                pl.BlockSpec((width, w), lambda i, order, cols: (0, 0)),
                pl.BlockSpec((w, width), lambda i, order, cols: (0, 0)),
                pl.BlockSpec((n_slots, COLS), lambda i, order, cols: (0, cols[col(i)])),
            ]
            + [
                pl.BlockSpec((1, cap, w), lambda i, order, cols, b=b: (order[n * row(i) + b], 0, 0))
                for b in range(n)
            ],
            out_specs=(
                pl.BlockSpec((r, w), lambda i, order, cols: (row(i), 0)),
                pl.BlockSpec((r, 2 * w), lambda i, order, cols: (row(i), 0)),
                pl.BlockSpec((COLS, 2 * w), lambda i, order, cols: (col(i), 0)),
            ),
            scratch_shapes=[pltpu.VMEM((n_slots, 2 * w), bf16)],
        ),
        compiler_params=pltpu.CompilerParams(vmem_limit_bytes=KERNEL_VMEM),
        cost_estimate=LIGHT,
        name="chunk_grads",
    )(order, cols, rows, routed, up_part, down_part, rows, *[gate] * n)


def own_grads(cols, rows, routed, hidden, both):
    n_slots, width = rows.shape
    w = hidden.shape[1]
    n_own, n_down = cols.shape[0], width // COLS

    def body(cols_ref, rows_ref, routed_ref, hidden_ref, both_ref, own_ref, down_ref, turned):
        step = pl.program_id(0)

        @pl.when(step == 0)
        def _():
            turned[...] = hidden_ref[...].T

        @pl.when(step < n_own)
        def _():
            own_ref[...] = dot(rows_ref[...], both_ref[...], ((0,), (0,))).astype(bf16)

        @pl.when(step >= n_own)
        def _():
            down_ref[...] = jnp.dot(
                turned[...], routed_ref[...], preferred_element_type=f32
            ).astype(bf16)

    def own(i):
        return jnp.minimum(i, n_own - 1)

    def down(i):
        return jnp.maximum(i - n_own, 0)

    return pl.pallas_call(
        body,
        out_shape=(
            jax.ShapeDtypeStruct((n_own * COLS, 2 * w), bf16),
            jax.ShapeDtypeStruct((w, width), bf16),
        ),
        grid_spec=pltpu.PrefetchScalarGridSpec(
            num_scalar_prefetch=1,
            grid=(n_own + n_down,),
            in_specs=[
                pl.BlockSpec((n_slots, COLS), lambda i, cols: (0, cols[own(i)])),
                pl.BlockSpec((n_slots, COLS), lambda i, cols: (0, down(i))),
                pl.BlockSpec((n_slots, w), lambda i, cols: (0, 0)),
                pl.BlockSpec((n_slots, 2 * w), lambda i, cols: (0, 0)),
            ],
            out_specs=(
                pl.BlockSpec((COLS, 2 * w), lambda i, cols: (own(i), 0)),
                pl.BlockSpec((w, COLS), lambda i, cols: (0, down(i))),
            ),
            scratch_shapes=[pltpu.VMEM((w, n_slots), bf16)],
        ),
        compiler_params=pltpu.CompilerParams(vmem_limit_bytes=KERNEL_VMEM),
        cost_estimate=LIGHT,
        name="own_grads",
    )(cols, rows, routed, hidden, both)


def spread_back(parts, starts, gate_mat, up_mat, table, tok_rows, first, heights):
    n_peers, _, cap = table.shape
    half = n_peers // 2
    width, hidden_width = gate_mat.shape
    cols = min(512, width)
    rows = half * cap
    shift = 0 if first else 1
    owner = [(i, b) for i, height in enumerate(heights) for b in range(height)]

    def body(*refs):
        part_refs = refs[: len(parts)]
        gate_ref, up_ref, table_ref = refs[len(parts) : len(parts) + 3]
        out_refs = refs[len(parts) + 3 :]
        total = jnp.zeros((rows, cols), f32)
        for start, part_ref in zip(starts, part_refs):
            w = part_ref.shape[1] // 2
            total += dot(part_ref[:, :w], gate_ref[:, start : start + w], ((1,), (1,)))
            total += dot(part_ref[:, w:], up_ref[:, start : start + w], ((1,), (1,)))
        terms = total.astype(bf16)
        for j, (i, b) in enumerate(owner):
            tok = table_ref[j, 0:1, :]
            place = (lax.broadcasted_iota(i32, (tok_rows, cap), 0).astype(f32) == tok).astype(bf16)
            spread = jnp.dot(place, terms[j * cap : (j + 1) * cap], preferred_element_type=f32)
            out_refs[i][b * tok_rows : (b + 1) * tok_rows, :] = spread.astype(bf16)

    return pl.pallas_call(
        body,
        out_shape=[jax.ShapeDtypeStruct((h * tok_rows, width), bf16) for h in heights],
        grid=(width // cols,),
        in_specs=[pl.BlockSpec((rows, x.shape[1]), lambda j: (shift, 0)) for x in parts]
        + [
            pl.BlockSpec((cols, hidden_width), lambda j: (j, 0)),
            pl.BlockSpec((cols, hidden_width), lambda j: (j, 0)),
            pl.BlockSpec((half, 2, cap), lambda j: (shift, 0, 0)),
        ],
        out_specs=[pl.BlockSpec((h * tok_rows, cols), lambda j: (0, j)) for h in heights],
        compiler_params=pltpu.CompilerParams(vmem_limit_bytes=KERNEL_VMEM),
        cost_estimate=LIGHT,
        name="spread_back",
    )(*parts, gate_mat, up_mat, table)


def local(tokens, out_grad, gate_saved, probs, expert_ids, w_gate, w_up, w_down):
    n_peers = lax.axis_size("expert")
    n_dp = lax.axis_size("dp")
    group = lax.axis_index("dp")
    tok_rows, model_width = tokens.shape
    top_k = expert_ids.shape[1]
    hidden_width = w_up.shape[2]
    cap = min(tok_rows, 2 * tok_rows * top_k // n_peers)
    n_routes = tok_rows * top_k
    n_slots = n_peers * cap
    gate_mat, up_mat, down_mat = w_gate[0], w_up[0], w_down[0]

    experts = jnp.arange(n_peers, dtype=i32)
    hit = expert_ids[:, :, None] == experts[None, None, :]
    named = jnp.any(hit, axis=1)
    weight = jnp.sum(jnp.where(hit, probs[:, :, None], 0.0), axis=1)
    rank = jnp.cumsum(named.astype(i32), axis=0) - 1
    slots = jnp.arange(cap, dtype=i32)
    in_slot = named[:, :, None] & (rank[:, :, None] == slots[None, None, :])
    tok_of = jnp.sum(
        jnp.where(in_slot, jnp.arange(1, tok_rows + 1, dtype=f32)[:, None, None], 0.0), axis=0
    ) - 1.0
    choice = jnp.sum(jnp.where(hit, jnp.arange(top_k, dtype=f32)[None, :, None], 0.0), axis=1)
    choice_of = jnp.sum(jnp.where(in_slot, choice[:, :, None], 0.0), axis=0)
    weight_of = jnp.sum(jnp.where(in_slot, weight[:, :, None], 0.0), axis=0)
    table = lax.all_to_all(
        jnp.concatenate([tok_of, weight_of], axis=1),
        "expert",
        split_axis=0,
        concat_axis=0,
        tiled=True,
    )
    ring = Ring()
    table = table.reshape(n_peers, 2, cap)[ring.order]
    widths = chunk_widths(hidden_width)
    starts = [sum(widths[:i]) for i in range(len(widths))]
    route_gates = jnp.transpose(gate_saved, (1, 0, 2)).reshape(n_routes, hidden_width)
    route_of = (tok_of + tok_rows * choice_of).astype(i32).reshape(n_slots, 1)
    pick = (route_of == jnp.arange(n_routes, dtype=i32)[None, :]).astype(bf16)
    send_gate = [
        dot(pick, route_gates[:, s : s + w], ((1,), (0,))).astype(bf16).reshape(n_peers, cap, w)
        for s, w in zip(starts, widths)
    ]
    up_parts = [up_mat[:, s : s + w] for s, w in zip(starts, widths)]
    down_parts = [down_mat[s : s + w] for s, w in zip(starts, widths)]
    (rows_in, routed), marks, (send_gate, (up_parts, down_parts)) = gather_rows(
        ring, tokens, out_grad, table.transpose(0, 2, 1), cap, [send_gate, (up_parts, down_parts)]
    )

    def send_chunk(i, mark):
        part, _ = lax.optimization_barrier((send_gate[i], mark))
        return lax.all_to_all(part, "expert", split_axis=0, concat_axis=0, tiled=True)

    recv_gate = [send_chunk(i, marks[m]) for i, m in zip(range(len(widths)), (min(1, len(marks) - 1), -1))]

    piece = model_width // n_dp
    shifts = [[(i, (i + d) % n_dp) for i in range(n_dp)] for d in range(n_dp)]

    per_piece = piece // COLS
    peer_cols = jnp.concatenate(
        [
            lax.rem(group + d, n_dp) * per_piece + jnp.arange(per_piece, dtype=i32)
            for d in range(1, n_dp)
        ]
    )
    both_parts, arrivals, own_parts = [], [], []
    sum_down = jnp.zeros((hidden_width, model_width), bf16)
    rows_now, routed_now = rows_in, routed

    own_cols = group * per_piece + jnp.arange(per_piece, dtype=i32)

    for c, w in enumerate(widths):
        hidden, both, sent = chunk_grads(
            ring.order, peer_cols, rows_now, routed_now, recv_gate[c], up_parts[c], down_parts[c]
        )
        both_parts.append(both)
        arrivals.append(
            [
                lax.ppermute(sent[(d - 1) * piece : d * piece], "dp", shifts[d])
                for d in range(1, n_dp)
            ]
        )
        if c + 2 < len(widths):
            recv_gate.append(send_chunk(c + 2, sent))
        if c + 1 < len(widths):
            own, down = own_grads(own_cols, rows_now, routed_now, hidden, both)
            own_parts.append(own)
            sum_down = lax.dynamic_update_slice(sum_down, down, (starts[c], 0))
            if c >= 1:
                rows_now, arrivals[c - 1] = lax.optimization_barrier((rows_now, arrivals[c - 1]))
            rows_now, routed_now, own_parts[c], sum_down = lax.optimization_barrier(
                (rows_now, routed_now, own_parts[c], sum_down)
            )

    heights = [1] + [2] * (ring.far - 1) + [1]
    theirs = spread_back(both_parts, starts, gate_mat, up_mat, table, tok_rows, True, heights)
    last, arrivals[:-1], _ = lax.optimization_barrier((both, arrivals[:-1], theirs))
    mine = spread_back(
        both_parts[:-1] + [last], starts, gate_mat, up_mat, table, tok_rows, False, heights
    )

    hidden, _ = lax.optimization_barrier((hidden, mine))
    own, down = own_grads(own_cols, rows_now, routed_now, hidden, both)
    own_parts.append(own)
    sum_down = lax.dynamic_update_slice(sum_down, down, (starts[-1], 0))
    low = hidden_width // n_dp
    sent = []
    for d in range(1, n_dp):
        q = lax.rem(group + d, n_dp)
        sent.append(lax.dynamic_slice_in_dim(sum_down, q * low, low, 0))
    sent, arrivals[-1] = lax.optimization_barrier((sent, arrivals[-1]))
    input_grad, sent = sum_back(ring, theirs, mine, tok_rows, sent)
    arrived = [lax.ppermute(part, "dp", shifts[d]) for d, part in enumerate(sent, 1)]
    arrived, _ = lax.optimization_barrier((arrived, input_grad))
    down = lax.dynamic_slice_in_dim(sum_down, group * low, low, 0).astype(f32)
    for part in arrived:
        down = down + part.astype(f32)
    grad_down = (grad_scale * down).astype(bf16)[None]

    gate_out, up_out = [], []
    for w, own, arrived in zip(widths, own_parts, arrivals):
        total = own.astype(f32)
        for part in arrived:
            total = total + part.astype(f32)
        total = (grad_scale * total).astype(bf16)
        gate_out.append(total[:, :w])
        up_out.append(total[:, w:])
    grad_gate = jnp.concatenate(gate_out, axis=1)[None]
    grad_up = jnp.concatenate(up_out, axis=1)[None]
    return (input_grad, grad_gate, grad_up, grad_down)


def solution(mesh):
    return jax.shard_map(
        local,
        mesh=mesh,
        in_specs=(
            P(("dp", "expert"), None),
            P(("dp", "expert"), None),
            P(("dp", "expert"), None, None),
            P(("dp", "expert"), None),
            P(("dp", "expert"), None),
            P("expert", None, None),
            P("expert", None, None),
            P("expert", None, None),
        ),
        out_specs=(
            P(("dp", "expert"), None),
            P("expert", "dp", None),
            P("expert", "dp", None),
            P("expert", "dp", None),
        ),
        check_vma=False,
    )
```

```python
import jax
import jax.numpy as jnp
import numpy as np
from jax import lax
from jax.experimental import pallas as pl
from jax.experimental.pallas import tpu as pltpu
from jax.sharding import PartitionSpec as P

grad_scale = 0.0625
f32 = jnp.float32
bf16 = jnp.bfloat16
i32 = jnp.int32
KERNEL_VMEM = 60 * 1024 * 1024


def dot(a, b, dims):
    return lax.dot_general(a, b, (dims, ((), ())), preferred_element_type=f32)


def chunk_widths(width):
    lanes = width // 128
    shares = (3, 7, 11)
    ends = [-(-lanes * x // 11) * 128 for x in shares]
    return [e - s for s, e in zip([0] + ends, ends) if e > s]


def chip_cycle(n_chips):
    cols = n_chips // 4
    if n_chips % 4 or cols < 2:
        return list(range(n_chips))
    walk = [(row, 0) for row in range(4)]
    for step, row in enumerate((3, 2, 1, 0)):
        across = range(1, cols) if step % 2 == 0 else range(cols - 1, 0, -1)
        walk += [(row, col) for col in across]
    return [row * cols + col for row, col in walk]


def put_rows(order, table, shards, rows, routed, cap):
    count = len(shards)
    n_peers, _, _ = table.shape
    width = shards[0][0].shape[1]

    def body(order_ref, table_ref, *refs):
        parts = refs[: 2 * count]
        rows_ref, routed_ref = refs[-2:]
        step = pl.program_id(0)
        for i in range(count):

            @pl.when(step == i)
            def _():
                info = table_ref[0]
                place = (
                    lax.broadcasted_iota(i32, (cap, tok_rows_of), 1).astype(f32) == info[:, 0:1]
                ).astype(bf16)
                rows_ref[...] = jnp.dot(
                    place, parts[2 * i][...], preferred_element_type=f32
                ).astype(bf16)
                picked = jnp.dot(place, parts[2 * i + 1][...], preferred_element_type=f32)
                routed_ref[...] = (info[:, 1:2] * picked).astype(bf16)

    tok_rows_of = shards[0][2]
    in_specs = [pl.BlockSpec((1, cap, 2), lambda i, order: (order[i], 0, 0))]
    operands = [table]
    for tok, grad, height, tok_at, grad_at in shards:
        in_specs.append(pl.BlockSpec((height, width), lambda i, order, a=tok_at: (a, 0)))
        in_specs.append(pl.BlockSpec((height, width), lambda i, order, a=grad_at: (a, 0)))
        operands += [tok, grad]
    aliases = {}
    if rows is not None:
        aliases = {1 + len(operands): 0, 2 + len(operands): 1}
        in_specs += [pl.BlockSpec(memory_space=pl.ANY)] * 2
        operands += [rows, routed]
    n_slots = n_peers * cap
    shape = jax.ShapeDtypeStruct((n_slots, width), bf16)
    out_spec = pl.BlockSpec((cap, width), lambda i, order: (order[i], 0))
    return pl.pallas_call(
        body,
        out_shape=(shape, shape),
        grid_spec=pltpu.PrefetchScalarGridSpec(
            num_scalar_prefetch=1,
            grid=(count,),
            in_specs=in_specs,
            out_specs=(out_spec, out_spec),
        ),
        input_output_aliases=aliases,
        compiler_params=pltpu.CompilerParams(vmem_limit_bytes=KERNEL_VMEM),
        cost_estimate=pl.CostEstimate(
            flops=4 * count * cap * tok_rows_of * width,
            bytes_accessed=4 * count * (tok_rows_of + cap) * width,
            transcendentals=0,
        ),
        name="put_rows",
    )(order, *operands)


class Ring:
    def __init__(self):
        self.n_peers = lax.axis_size("expert")
        self.n = self.n_peers // 2
        self.far = self.n // 2
        self.names = [self.far]
        for d in range(self.far - 1, 0, -1):
            self.names += [d, -d]
        self.names.append(0)
        cycle = chip_cycle(self.n)
        spot = [cycle.index(c) for c in range(self.n)]
        chips = range(self.n)
        self.fwd = [(2 * cycle[i] + c, 2 * cycle[(i + 1) % self.n] + c) for i in chips for c in (0, 1)]
        self.bwd = [(b, a) for a, b in self.fwd]
        self.swap = [(i, i ^ 1) for i in range(self.n_peers)]
        table = np.zeros((self.n_peers, self.n_peers), np.int32)
        for e in range(self.n_peers):
            for core in (0, 1):
                for j, d in enumerate(self.names):
                    chip = cycle[(spot[e // 2] - d) % self.n]
                    table[e, core * self.n + j] = 2 * chip + (e % 2 if core else 1 - e % 2)
        self.order = jnp.asarray(table)[lax.axis_index("expert")]

    def at(self, distance, other):
        return self.names.index(distance) + (0 if other else self.n)

    def ahead(self, x):
        return lax.ppermute(x, "expert", self.fwd)

    def behind(self, x):
        return lax.ppermute(x, "expert", self.bwd)

    def other_core(self, x):
        return lax.ppermute(x, "expert", self.swap)


def gather_rows(ring, tokens, out_grad, table, cap, beside):
    tok_rows = tokens.shape[0]
    own = jnp.concatenate([tokens, out_grad], axis=0)
    beside = list(beside)

    def whole(x):
        return (x, x, tok_rows, 0, 1)

    def place(spots, shards, state):
        return put_rows(np.array(spots, np.int32), table, shards, *state, cap)

    state = (None, None)
    ahead, behind = own, own
    pending = ([ring.at(0, False), ring.at(0, True)], [whole(own), whole(ring.other_core(own))])
    marks = []
    for d in range(1, ring.far):
        ahead, behind = ring.ahead(ahead), ring.behind(behind)
        if d >= 2:
            state = place(*pending[0], state)
            pending = pending[1:]
            ahead, behind, state = lax.optimization_barrier((ahead, behind, state))
            if d - 2 < len(beside):
                ahead, behind, beside[d - 2] = lax.optimization_barrier(
                    (ahead, behind, beside[d - 2])
                )
        else:
            pending = [pending]
        marks.append((ahead, behind))
        pending.append(
            (
                [ring.at(d, False), ring.at(-d, False), ring.at(d, True), ring.at(-d, True)],
                [whole(x) for x in (ahead, behind, ring.other_core(ahead), ring.other_core(behind))],
            )
        )
    far_tok = ring.ahead(ahead[:tok_rows])
    far_grad = ring.behind(behind[tok_rows:])
    state = place(*pending[0], state)
    far_tok, far_grad, state = lax.optimization_barrier((far_tok, far_grad, state))
    marks.append((far_tok, far_grad))
    for spots, shards in pending[1:]:
        state = place(spots, shards, state)
    state = place(
        [ring.at(ring.far, False), ring.at(ring.far, True)],
        [
            (far_tok, far_grad, tok_rows, 0, 0),
            (ring.other_core(far_tok), ring.other_core(far_grad), tok_rows, 0, 0),
        ],
        state,
    )
    return state, marks, beside


def sum_back(ring, theirs, mine, tok_rows, fill):
    handed, ours = {}, {}
    j = 0
    for piece, own in zip(theirs, mine):
        piece = ring.other_core(piece)
        for at in range(0, piece.shape[0], tok_rows):
            handed[ring.names[j]] = piece[at : at + tok_rows]
            ours[ring.names[j]] = own[at : at + tok_rows]
            j += 1

    def plus(d, *others):
        total = ours[d].astype(f32) + handed[d].astype(f32)
        for x in others:
            total = total + x.astype(f32)
        return total.astype(bf16)

    half = tok_rows // 2
    first = plus(ring.far)
    top, low = ring.ahead(first[:half]), ring.behind(first[half:])
    beside = fill((top, low))
    none = jnp.zeros_like(top)
    ahead = jnp.concatenate([top, none], axis=0)
    behind = jnp.concatenate([none, low], axis=0)
    for d in range(ring.far - 1, 0, -1):
        ahead, behind = ring.ahead(plus(-d, ahead)), ring.behind(plus(d, behind))
        if d == ring.far - 1:
            ahead, behind, beside = lax.optimization_barrier((ahead, behind, beside))
    return plus(0, ahead, behind), beside


def blocks_per_step(n_blocks, cap):
    return max(b for b in range(1, n_blocks + 1) if n_blocks % b == 0 and b * cap <= 768)


LIGHT = pl.CostEstimate(flops=1000, bytes_accessed=1000, transcendentals=0)


def chunk_grads(order, cols, rows, routed, gate, up_mat, down_mat, start, piece):
    n_slots, width = rows.shape
    n_peers, cap, w = gate.shape
    n = blocks_per_step(n_peers, cap)
    r = n * cap
    n_rows, n_cols = n_slots // r, cols.shape[0]

    def body(order_ref, cols_ref, rows_ref, routed_ref, up_ref, down_ref, col_ref, *refs):
        gate_refs, (hidden_ref, both_ref, part_ref, held) = refs[:n], refs[n:]
        step = pl.program_id(0)

        @pl.when(step < n_rows)
        def _():
            up_all = jnp.dot(rows_ref[...], up_ref[...], preferred_element_type=f32)
            grad_all = dot(routed_ref[...], down_ref[...], ((1,), (1,)))
            for b in range(n):
                at = slice(b * cap, (b + 1) * cap)
                up_act, hidden_grad = up_all[at], grad_all[at]
                gate_val = gate_refs[b][0].astype(f32)
                gate_sig = jax.nn.sigmoid(gate_val)
                gate_act = gate_val * gate_sig
                hidden_ref[at, :] = (gate_act * up_act).astype(bf16)
                both_ref[at, w:] = (hidden_grad * gate_act).astype(bf16)
                both_ref[at, :w] = (
                    hidden_grad * up_act * gate_sig * (1.0 + gate_val * (1.0 - gate_sig))
                ).astype(bf16)
            held[pl.ds(pl.multiple_of(step * r, r), r), :] = both_ref[...]

        @pl.when(step >= n_rows)
        def _():
            part_ref[...] = dot(col_ref[...], held[...], ((0,), (0,))).astype(bf16)

    def row(i):
        return jnp.minimum(i, n_rows - 1)

    def col(i):
        return jnp.maximum(i - n_rows, 0)

    return pl.pallas_call(
        body,
        out_shape=(
            jax.ShapeDtypeStruct((n_slots, w), bf16),
            jax.ShapeDtypeStruct((n_slots, 2 * w), bf16),
            jax.ShapeDtypeStruct((n_cols * piece, 2 * w), bf16),
        ),
        grid_spec=pltpu.PrefetchScalarGridSpec(
            num_scalar_prefetch=2,
            grid=(n_rows + n_cols,),
            in_specs=[
                pl.BlockSpec((r, width), lambda i, order, cols: (row(i), 0)),
                pl.BlockSpec((r, width), lambda i, order, cols: (row(i), 0)),
                pl.BlockSpec((pl.Element(width), pl.Element(w)), lambda i, order, cols: (0, start)),
                pl.BlockSpec((pl.Element(w), pl.Element(width)), lambda i, order, cols: (start, 0)),
                pl.BlockSpec((n_slots, piece), lambda i, order, cols: (0, cols[col(i)])),
            ]
            + [
                pl.BlockSpec((1, cap, w), lambda i, order, cols, b=b: (order[n * row(i) + b], 0, 0))
                for b in range(n)
            ],
            out_specs=(
                pl.BlockSpec((r, w), lambda i, order, cols: (row(i), 0)),
                pl.BlockSpec((r, 2 * w), lambda i, order, cols: (row(i), 0)),
                pl.BlockSpec((piece, 2 * w), lambda i, order, cols: (col(i), 0)),
            ),
            scratch_shapes=[pltpu.VMEM((n_slots, 2 * w), bf16)],
        ),
        compiler_params=pltpu.CompilerParams(vmem_limit_bytes=KERNEL_VMEM),
        cost_estimate=LIGHT,
        name="chunk_grads",
    )(order, cols, rows, routed, up_mat, down_mat, rows, *[gate] * n)


def own_grads(cols, rows, routed, hidden, both, start, piece, total, hidden_width):
    n_slots, width = rows.shape
    w = hidden.shape[1]
    span = min(1024, width)
    n_own, n_down = cols.shape[0], width // span

    def body(cols_ref, rows_ref, routed_ref, hidden_ref, both_ref, *refs):
        own_ref, down_ref, turned = refs[-3:]
        step = pl.program_id(0)

        @pl.when(step < n_own)
        def _():
            own_ref[...] = dot(rows_ref[...], both_ref[...], ((0,), (0,))).astype(bf16)

        @pl.when(step == n_own)
        def _():
            turned[...] = hidden_ref[...].T

        @pl.when(step >= n_own)
        def _():
            down_ref[...] = jnp.dot(
                turned[...], routed_ref[...], preferred_element_type=f32
            ).astype(bf16)

    def own(i):
        return jnp.minimum(i, n_own - 1)

    def down(i):
        return jnp.maximum(i - n_own, 0)

    aliased = [] if total is None else [total]
    return pl.pallas_call(
        body,
        out_shape=(
            jax.ShapeDtypeStruct((n_own * piece, 2 * w), bf16),
            jax.ShapeDtypeStruct((hidden_width, width), bf16),
        ),
        grid_spec=pltpu.PrefetchScalarGridSpec(
            num_scalar_prefetch=1,
            grid=(n_own + n_down,),
            in_specs=[
                pl.BlockSpec((n_slots, piece), lambda i, cols: (0, cols[own(i)])),
                pl.BlockSpec((n_slots, span), lambda i, cols: (0, down(i))),
                pl.BlockSpec((n_slots, w), lambda i, cols: (0, 0)),
                pl.BlockSpec((n_slots, 2 * w), lambda i, cols: (0, 0)),
            ]
            + [pl.BlockSpec(memory_space=pl.ANY) for _ in aliased],
            out_specs=(
                pl.BlockSpec((piece, 2 * w), lambda i, cols: (own(i), 0)),
                pl.BlockSpec(
                    (pl.Element(w), pl.Element(span)), lambda i, cols: (start, down(i) * span)
                ),
            ),
            scratch_shapes=[pltpu.VMEM((w, n_slots), bf16)],
        ),
        input_output_aliases={5: 1} if aliased else {},
        compiler_params=pltpu.CompilerParams(vmem_limit_bytes=KERNEL_VMEM),
        cost_estimate=LIGHT,
        name="own_grads",
    )(cols, rows, routed, hidden, both, *aliased)


def spread_back(parts, starts, gate_mat, up_mat, table, tok_rows, first, heights):
    n_peers, _, cap = table.shape
    half = n_peers // 2
    width, hidden_width = gate_mat.shape
    cols = min(512, width)
    rows = half * cap
    shift = 0 if first else 1
    owner = [(i, b) for i, height in enumerate(heights) for b in range(height)]

    def body(*refs):
        part_refs = refs[: len(parts)]
        gate_ref, up_ref, table_ref = refs[len(parts) : len(parts) + 3]
        out_refs = refs[len(parts) + 3 :]
        total = jnp.zeros((rows, cols), f32)
        for start, part_ref in zip(starts, part_refs):
            w = part_ref.shape[1] // 2
            total += dot(part_ref[:, :w], gate_ref[:, start : start + w], ((1,), (1,)))
            total += dot(part_ref[:, w:], up_ref[:, start : start + w], ((1,), (1,)))
        terms = total.astype(bf16)
        for j, (i, b) in enumerate(owner):
            tok = table_ref[j, 0:1, :]
            place = (lax.broadcasted_iota(i32, (tok_rows, cap), 0).astype(f32) == tok).astype(bf16)
            spread = jnp.dot(place, terms[j * cap : (j + 1) * cap], preferred_element_type=f32)
            out_refs[i][b * tok_rows : (b + 1) * tok_rows, :] = spread.astype(bf16)

    return pl.pallas_call(
        body,
        out_shape=[jax.ShapeDtypeStruct((h * tok_rows, width), bf16) for h in heights],
        grid=(width // cols,),
        in_specs=[pl.BlockSpec((rows, x.shape[1]), lambda j: (shift, 0)) for x in parts]
        + [
            pl.BlockSpec((cols, hidden_width), lambda j: (j, 0)),
            pl.BlockSpec((cols, hidden_width), lambda j: (j, 0)),
            pl.BlockSpec((half, 2, cap), lambda j: (shift, 0, 0)),
        ],
        out_specs=[pl.BlockSpec((h * tok_rows, cols), lambda j: (0, j)) for h in heights],
        compiler_params=pltpu.CompilerParams(vmem_limit_bytes=KERNEL_VMEM),
        cost_estimate=LIGHT,
        name="spread_back",
    )(*parts, gate_mat, up_mat, table)


def local(tokens, out_grad, gate_saved, probs, expert_ids, w_gate, w_up, w_down):
    n_peers = lax.axis_size("expert")
    n_dp = lax.axis_size("dp")
    group = lax.axis_index("dp")
    tok_rows, model_width = tokens.shape
    top_k = expert_ids.shape[1]
    hidden_width = w_up.shape[2]
    cap = min(tok_rows, 2 * tok_rows * top_k // n_peers)
    n_routes = tok_rows * top_k
    n_slots = n_peers * cap
    gate_mat, up_mat, down_mat = w_gate[0], w_up[0], w_down[0]

    experts = jnp.arange(n_peers, dtype=i32)
    hit = expert_ids[:, :, None] == experts[None, None, :]
    named = jnp.any(hit, axis=1)
    weight = jnp.sum(jnp.where(hit, probs[:, :, None], 0.0), axis=1)
    rank = jnp.cumsum(named.astype(i32), axis=0) - 1
    slots = jnp.arange(cap, dtype=i32)
    in_slot = named[:, :, None] & (rank[:, :, None] == slots[None, None, :])
    tok_of = jnp.sum(
        jnp.where(in_slot, jnp.arange(1, tok_rows + 1, dtype=f32)[:, None, None], 0.0), axis=0
    ) - 1.0
    choice = jnp.sum(jnp.where(hit, jnp.arange(top_k, dtype=f32)[None, :, None], 0.0), axis=1)
    choice_of = jnp.sum(jnp.where(in_slot, choice[:, :, None], 0.0), axis=0)
    weight_of = jnp.sum(jnp.where(in_slot, weight[:, :, None], 0.0), axis=0)
    table = lax.all_to_all(
        jnp.concatenate([tok_of, weight_of], axis=1),
        "expert",
        split_axis=0,
        concat_axis=0,
        tiled=True,
    )
    ring = Ring()
    table = table.reshape(n_peers, 2, cap)[ring.order]
    widths = chunk_widths(hidden_width)
    starts = [sum(widths[:i]) for i in range(len(widths))]
    route_gates = jnp.transpose(gate_saved, (1, 0, 2)).reshape(n_routes, hidden_width)
    route_of = (tok_of + tok_rows * choice_of).astype(i32).reshape(n_slots, 1)
    pick = (route_of == jnp.arange(n_routes, dtype=i32)[None, :]).astype(bf16)
    send_gate = [
        dot(pick, route_gates[:, s : s + w], ((1,), (0,))).astype(bf16).reshape(n_peers, cap, w)
        for s, w in zip(starts, widths)
    ]
    (rows_in, routed), marks, (send_gate[1:],) = gather_rows(
        ring, tokens, out_grad, table.transpose(0, 2, 1), cap, [send_gate[1:]]
    )

    def send_chunk(i, mark):
        part = send_gate[i]
        if mark is not None:
            part, _ = lax.optimization_barrier((part, mark))
        return lax.all_to_all(part, "expert", split_axis=0, concat_axis=0, tiled=True)

    recv_gate = [send_chunk(i, mark) for i, mark in zip(range(len(widths)), (None, marks[-1]))]

    piece = model_width // n_dp
    shifts = [[(i, (i + d) % n_dp) for i in range(n_dp)] for d in range(n_dp)]

    peer_cols = lax.rem(group + jnp.arange(1, n_dp, dtype=i32), n_dp)
    own_cols = group.reshape(1).astype(i32)
    both_parts, arrivals, own_parts = [], [], []
    sum_down = None
    rows_now, routed_now = rows_in, routed

    for c, w in enumerate(widths):
        hidden, both, sent = chunk_grads(
            ring.order,
            peer_cols,
            rows_now,
            routed_now,
            recv_gate[c],
            up_mat,
            down_mat,
            starts[c],
            piece,
        )
        both_parts.append(both)
        arrivals.append(
            [
                lax.ppermute(sent[(d - 1) * piece : d * piece], "dp", shifts[d])
                for d in range(1, n_dp)
            ]
        )
        if c + 2 < len(widths):
            recv_gate.append(send_chunk(c + 2, sent))
        if c + 1 < len(widths):
            own, sum_down = own_grads(
                own_cols, rows_now, routed_now, hidden, both, starts[c], piece, sum_down, hidden_width
            )
            own_parts.append(own)
            if c >= 1:
                rows_now, arrivals[c - 1] = lax.optimization_barrier((rows_now, arrivals[c - 1]))
            rows_now, routed_now, own_parts[c], sum_down = lax.optimization_barrier(
                (rows_now, routed_now, own_parts[c], sum_down)
            )

    heights = [1] + [2] * (ring.far - 1) + [1]
    theirs = spread_back(both_parts, starts, gate_mat, up_mat, table, tok_rows, True, heights)
    last, arrivals[:-1], _ = lax.optimization_barrier((both, arrivals[:-1], theirs))
    mine = spread_back(
        both_parts[:-1] + [last], starts, gate_mat, up_mat, table, tok_rows, False, heights
    )

    low = hidden_width // n_dp

    def last_grads(mark):
        held, _ = lax.optimization_barrier((hidden, mark))
        own, total = own_grads(
            own_cols, rows_now, routed_now, held, both, starts[-1], piece, sum_down, hidden_width
        )
        sent = [
            lax.dynamic_slice_in_dim(total, lax.rem(group + d, n_dp) * low, low, 0)
            for d in range(1, n_dp)
        ]
        sent, arrived = lax.optimization_barrier((sent, arrivals[-1]))
        return own, total, sent, arrived

    input_grad, (own, sum_down, sent, arrivals[-1]) = sum_back(
        ring, theirs, mine, tok_rows, last_grads
    )
    own_parts.append(own)
    arrived = [lax.ppermute(part, "dp", shifts[d]) for d, part in enumerate(sent, 1)]
    arrived, _ = lax.optimization_barrier((arrived, input_grad))
    down = lax.dynamic_slice_in_dim(sum_down, group * low, low, 0).astype(f32)
    for part in arrived:
        down = down + part.astype(f32)
    grad_down = (grad_scale * down).astype(bf16)[None]

    gate_out, up_out = [], []
    for w, own, arrived in zip(widths, own_parts, arrivals):
        total = own.astype(f32)
        for part in arrived:
            total = total + part.astype(f32)
        total = (grad_scale * total).astype(bf16)
        gate_out.append(total[:, :w])
        up_out.append(total[:, w:])
    grad_gate = jnp.concatenate(gate_out, axis=1)[None]
    grad_up = jnp.concatenate(up_out, axis=1)[None]
    return (input_grad, grad_gate, grad_up, grad_down)


def solution(mesh):
    return jax.shard_map(
        local,
        mesh=mesh,
        in_specs=(
            P(("dp", "expert"), None),
            P(("dp", "expert"), None),
            P(("dp", "expert"), None, None),
            P(("dp", "expert"), None),
            P(("dp", "expert"), None),
            P("expert", None, None),
            P("expert", None, None),
            P("expert", None, None),
        ),
        out_specs=(
            P(("dp", "expert"), None),
            P("expert", "dp", None),
            P("expert", "dp", None),
            P("expert", "dp", None),
        ),
        check_vma=False,
    )
```

```python
import jax
import jax.numpy as jnp
import numpy as np
from jax import lax
from jax.experimental import pallas as pl
from jax.experimental.pallas import tpu as pltpu
from jax.sharding import PartitionSpec as P

grad_scale = 0.0625
f32 = jnp.float32
bf16 = jnp.bfloat16
i32 = jnp.int32
KERNEL_VMEM = 60 * 1024 * 1024
LIGHT = pl.CostEstimate(flops=1000, bytes_accessed=1000, transcendentals=0)


def dot(a, b, dims):
    return lax.dot_general(a, b, (dims, ((), ())), preferred_element_type=f32)


def chunk_widths(width):
    lanes = width // 128
    shares = (3, 7, 11)
    ends = [-(-lanes * x // 11) * 128 for x in shares]
    return [e - s for s, e in zip([0] + ends, ends) if e > s]


def chip_cycle(n_chips):
    cols = n_chips // 4
    if n_chips % 4 or cols < 2:
        return list(range(n_chips))
    walk = [(row, 0) for row in range(4)]
    for step, row in enumerate((3, 2, 1, 0)):
        across = range(1, cols) if step % 2 == 0 else range(cols - 1, 0, -1)
        walk += [(row, col) for col in across]
    return [row * cols + col for row, col in walk]


def put_rows(spots, table, shards, up_mat, down_mat, w, state, cap):
    count = len(shards)
    n_peers = table.shape[0]
    width = shards[0][0].shape[1]
    tok_rows = shards[0][2]

    def body(spots_ref, table_ref, up_ref, down_ref, *refs):
        parts = refs[: 2 * count]
        rows_ref, routed_ref, act_ref, grad_ref = refs[-4:]
        step = pl.program_id(0)
        for i in range(count):

            @pl.when(step == i)
            def _():
                info = table_ref[0]
                place = (
                    lax.broadcasted_iota(i32, (cap, tok_rows), 1).astype(f32) == info[:, 0:1]
                ).astype(bf16)
                rows_ref[...] = jnp.dot(
                    place, parts[2 * i][...], preferred_element_type=f32
                ).astype(bf16)
                picked = jnp.dot(place, parts[2 * i + 1][...], preferred_element_type=f32)
                routed_ref[...] = (info[:, 1:2] * picked).astype(bf16)

        act_ref[...] = jnp.dot(rows_ref[...], up_ref[...], preferred_element_type=f32)
        grad_ref[...] = dot(routed_ref[...], down_ref[...], ((1,), (1,)))

    in_specs = [
        pl.BlockSpec((1, cap, 2), lambda i, spots: (spots[i], 0, 0)),
        pl.BlockSpec((width, w), lambda i, spots: (0, 0)),
        pl.BlockSpec((w, width), lambda i, spots: (0, 0)),
    ]
    operands = [table, up_mat, down_mat]
    for tok, grad, height, tok_at, grad_at in shards:
        in_specs.append(pl.BlockSpec((height, width), lambda i, spots, a=tok_at: (a, 0)))
        in_specs.append(pl.BlockSpec((height, width), lambda i, spots, a=grad_at: (a, 0)))
        operands += [tok, grad]
    aliases = {}
    if state is not None:
        aliases = {1 + len(operands) + j: j for j in range(4)}
        in_specs += [pl.BlockSpec(memory_space=pl.ANY)] * 4
        operands += state
    n_slots = n_peers * cap

    def at(i, spots):
        return (spots[i], 0)

    return pl.pallas_call(
        body,
        out_shape=(
            jax.ShapeDtypeStruct((n_slots, width), bf16),
            jax.ShapeDtypeStruct((n_slots, width), bf16),
            jax.ShapeDtypeStruct((n_slots, w), f32),
            jax.ShapeDtypeStruct((n_slots, w), f32),
        ),
        grid_spec=pltpu.PrefetchScalarGridSpec(
            num_scalar_prefetch=1,
            grid=(count,),
            in_specs=in_specs,
            out_specs=(
                pl.BlockSpec((cap, width), at),
                pl.BlockSpec((cap, width), at),
                pl.BlockSpec((cap, w), at),
                pl.BlockSpec((cap, w), at),
            ),
        ),
        input_output_aliases=aliases,
        compiler_params=pltpu.CompilerParams(vmem_limit_bytes=KERNEL_VMEM),
        cost_estimate=LIGHT,
        name="put_rows",
    )(np.array(spots, np.int32), *operands)


class Ring:
    def __init__(self):
        self.n_peers = lax.axis_size("expert")
        self.n = self.n_peers // 2
        self.far = self.n // 2
        self.names = [self.far]
        for d in range(self.far - 1, 0, -1):
            self.names += [d, -d]
        self.names.append(0)
        cycle = chip_cycle(self.n)
        spot = [cycle.index(c) for c in range(self.n)]
        chips = range(self.n)
        self.fwd = [(2 * cycle[i] + c, 2 * cycle[(i + 1) % self.n] + c) for i in chips for c in (0, 1)]
        self.bwd = [(b, a) for a, b in self.fwd]
        self.swap = [(i, i ^ 1) for i in range(self.n_peers)]
        table = np.zeros((self.n_peers, self.n_peers), np.int32)
        for e in range(self.n_peers):
            for core in (0, 1):
                for j, d in enumerate(self.names):
                    chip = cycle[(spot[e // 2] - d) % self.n]
                    table[e, core * self.n + j] = 2 * chip + (e % 2 if core else 1 - e % 2)
        self.order = jnp.asarray(table)[lax.axis_index("expert")]

    def at(self, distance, other):
        return self.names.index(distance) + (0 if other else self.n)

    def ahead(self, x):
        return lax.ppermute(x, "expert", self.fwd)

    def behind(self, x):
        return lax.ppermute(x, "expert", self.bwd)

    def other_core(self, x):
        return lax.ppermute(x, "expert", self.swap)


def gather_rows(ring, tokens, out_grad, table, cap, up_mat, down_mat, first_width, beside):
    tok_rows = tokens.shape[0]
    own = jnp.concatenate([tokens, out_grad], axis=0)

    def whole(x):
        return (x, x, tok_rows, 0, 1)

    def place(spots, shards, state):
        return put_rows(spots, table, shards, up_mat, down_mat, first_width, state, cap)

    state = None
    ahead, behind = own, own
    pending = ([ring.at(0, False), ring.at(0, True)], [whole(own), whole(ring.other_core(own))])
    for d in range(1, ring.far):
        ahead, behind = ring.ahead(ahead), ring.behind(behind)
        if d >= 2:
            for spots, shards in pending:
                state = place(spots, shards, state)
            pending = []
            ahead, behind, state = lax.optimization_barrier((ahead, behind, state))
            if d == 2:
                ahead, behind, beside = lax.optimization_barrier((ahead, behind, beside))
        else:
            pending = [pending]
        pending.append(
            (
                [ring.at(d, False), ring.at(-d, False), ring.at(d, True), ring.at(-d, True)],
                [whole(x) for x in (ahead, behind, ring.other_core(ahead), ring.other_core(behind))],
            )
        )
    far_tok = ring.ahead(ahead[:tok_rows])
    far_grad = ring.behind(behind[tok_rows:])
    if ring.far == 1:
        pending = [pending]
    for spots, shards in pending:
        state = place(spots, shards, state)
    far_tok, far_grad, state = lax.optimization_barrier((far_tok, far_grad, state))
    theirs_tok, theirs_grad = ring.other_core(far_tok), ring.other_core(far_grad)
    state = place(
        [ring.at(ring.far, False), ring.at(ring.far, True)],
        [(far_tok, far_grad, tok_rows, 0, 0), (theirs_tok, theirs_grad, tok_rows, 0, 0)],
        state,
    )
    return state, (theirs_tok, theirs_grad), beside


def sum_back(ring, theirs, mine, tok_rows, fills):
    handed, ours = {}, {}
    j = 0
    for piece, own in zip(theirs, mine):
        piece = ring.other_core(piece)
        for at in range(0, piece.shape[0], tok_rows):
            handed[ring.names[j]] = piece[at : at + tok_rows]
            ours[ring.names[j]] = own[at : at + tok_rows]
            j += 1

    def plus(d, *others):
        total = ours[d].astype(f32) + handed[d].astype(f32)
        for x in others:
            total = total + x.astype(f32)
        return total.astype(bf16)

    half = tok_rows // 2
    first = plus(ring.far)
    top, low = ring.ahead(first[:half]), ring.behind(first[half:])
    none = jnp.zeros_like(top)
    ahead = jnp.concatenate([top, none], axis=0)
    behind = jnp.concatenate([none, low], axis=0)
    mark, filled = (top, low), []
    for d in range(ring.far - 1, 0, -1):
        ahead, behind = ring.ahead(plus(-d, ahead)), ring.behind(plus(d, behind))
        if len(filled) < len(fills):
            done = fills[len(filled)](mark)
            ahead, behind, done = lax.optimization_barrier((ahead, behind, done))
            filled.append(done)
        mark = (ahead, behind)
    for fill in fills[len(filled) :]:
        filled.append(fill(mark))
    return plus(0, ahead, behind), filled


def blocks_per_step(n_blocks, cap):
    return max(b for b in range(1, n_blocks + 1) if n_blocks % b == 0 and b * cap <= 768)


def chunk_grads(order, cols, rows, routed, gate, up_mat, down_mat, start, piece, ready):
    n_slots, width = rows.shape
    n_peers, cap, w = gate.shape
    n = blocks_per_step(n_peers, cap)
    r = n * cap
    n_rows, n_cols = n_slots // r, cols.shape[0]
    n_in = 4 if ready is None else 2

    def body(order_ref, cols_ref, *refs):
        ins, col_ref, gate_refs = refs[:n_in], refs[n_in], refs[n_in + 1 : n_in + 1 + n]
        hidden_ref, both_ref, part_ref, held = refs[n_in + 1 + n :]
        step = pl.program_id(0)

        @pl.when(step < n_rows)
        def _():
            if ready is None:
                up_all = jnp.dot(ins[0][...], ins[2][...], preferred_element_type=f32)
                grad_all = dot(ins[1][...], ins[3][...], ((1,), (1,)))
            else:
                up_all, grad_all = ins
            for b in range(n):
                at = slice(b * cap, (b + 1) * cap)
                up_act, hidden_grad = up_all[at, :], grad_all[at, :]
                gate_val = gate_refs[b][0].astype(f32)
                gate_sig = jax.nn.sigmoid(gate_val)
                gate_act = gate_val * gate_sig
                hidden_ref[at, :] = (gate_act * up_act).astype(bf16)
                both_ref[at, w:] = (hidden_grad * gate_act).astype(bf16)
                both_ref[at, :w] = (
                    hidden_grad * up_act * gate_sig * (1.0 + gate_val * (1.0 - gate_sig))
                ).astype(bf16)
            held[pl.ds(pl.multiple_of(step * r, r), r), :] = both_ref[...]

        @pl.when(step >= n_rows)
        def _():
            part_ref[...] = dot(col_ref[...], held[...], ((0,), (0,))).astype(bf16)

    def row(i):
        return jnp.minimum(i, n_rows - 1)

    def col(i):
        return jnp.maximum(i - n_rows, 0)

    def row_blocks(x):
        return pl.BlockSpec((r, x.shape[1]), lambda i, order, cols: (row(i), 0))

    if ready is None:
        operands = [rows, routed, up_mat, down_mat]
        in_specs = [
            row_blocks(rows),
            row_blocks(routed),
            pl.BlockSpec((pl.Element(width), pl.Element(w)), lambda i, order, cols: (0, start)),
            pl.BlockSpec((pl.Element(w), pl.Element(width)), lambda i, order, cols: (start, 0)),
        ]
    else:
        operands = list(ready)
        in_specs = [row_blocks(x) for x in ready]
    return pl.pallas_call(
        body,
        out_shape=(
            jax.ShapeDtypeStruct((n_slots, w), bf16),
            jax.ShapeDtypeStruct((n_slots, 2 * w), bf16),
            jax.ShapeDtypeStruct((n_cols * piece, 2 * w), bf16),
        ),
        grid_spec=pltpu.PrefetchScalarGridSpec(
            num_scalar_prefetch=2,
            grid=(n_rows + n_cols,),
            in_specs=in_specs
            + [pl.BlockSpec((n_slots, piece), lambda i, order, cols: (0, cols[col(i)]))]
            + [
                pl.BlockSpec((1, cap, w), lambda i, order, cols, b=b: (order[n * row(i) + b], 0, 0))
                for b in range(n)
            ],
            out_specs=(
                pl.BlockSpec((r, w), lambda i, order, cols: (row(i), 0)),
                pl.BlockSpec((r, 2 * w), lambda i, order, cols: (row(i), 0)),
                pl.BlockSpec((piece, 2 * w), lambda i, order, cols: (col(i), 0)),
            ),
            scratch_shapes=[pltpu.VMEM((n_slots, 2 * w), bf16)],
        ),
        compiler_params=pltpu.CompilerParams(vmem_limit_bytes=KERNEL_VMEM),
        cost_estimate=LIGHT,
        name="chunk_grads",
    )(order, cols, *operands, rows, *[gate] * n)


def own_half(cols, rows, both, piece):
    n_slots = rows.shape[0]
    w = both.shape[1]

    def body(cols_ref, rows_ref, both_ref, own_ref):
        own_ref[...] = dot(rows_ref[...], both_ref[...], ((0,), (0,))).astype(bf16)

    return pl.pallas_call(
        body,
        out_shape=jax.ShapeDtypeStruct((piece, w), bf16),
        grid_spec=pltpu.PrefetchScalarGridSpec(
            num_scalar_prefetch=1,
            grid=(1,),
            in_specs=[
                pl.BlockSpec((n_slots, piece), lambda i, cols: (0, cols[0])),
                pl.BlockSpec((n_slots, w), lambda i, cols: (0, 0)),
            ],
            out_specs=pl.BlockSpec((piece, w), lambda i, cols: (0, 0)),
        ),
        compiler_params=pltpu.CompilerParams(vmem_limit_bytes=KERNEL_VMEM),
        cost_estimate=LIGHT,
        name="own_half",
    )(cols, rows, both)


def down_rows(routed, hidden, start, total, hidden_width):
    n_slots, width = routed.shape
    w = hidden.shape[1]
    span = min(1024, width)

    def body(routed_ref, hidden_ref, *refs):
        down_ref, turned = refs[-2:]

        @pl.when(pl.program_id(0) == 0)
        def _():
            turned[...] = hidden_ref[...].T

        down_ref[...] = jnp.dot(turned[...], routed_ref[...], preferred_element_type=f32).astype(bf16)

    aliased = [] if total is None else [total]
    return pl.pallas_call(
        body,
        out_shape=jax.ShapeDtypeStruct((hidden_width, width), bf16),
        grid=(width // span,),
        in_specs=[
            pl.BlockSpec((n_slots, span), lambda i: (0, i)),
            pl.BlockSpec((n_slots, w), lambda i: (0, 0)),
        ]
        + [pl.BlockSpec(memory_space=pl.ANY) for _ in aliased],
        out_specs=pl.BlockSpec((pl.Element(w), pl.Element(span)), lambda i: (start, i * span)),
        scratch_shapes=[pltpu.VMEM((w, n_slots), bf16)],
        input_output_aliases={2: 0} if aliased else {},
        compiler_params=pltpu.CompilerParams(vmem_limit_bytes=KERNEL_VMEM),
        cost_estimate=LIGHT,
        name="down_rows",
    )(routed, hidden, *aliased)


def join_halves(own, arrived, start, totals, hidden_width):
    piece, both_width = own.shape
    w = both_width // 2
    r = min(256, piece)
    n_in = 1 + len(arrived)

    def body(*refs):
        gate_ref, up_ref = refs[-2:]
        for at, out_ref in ((slice(0, w), gate_ref), (slice(w, 2 * w), up_ref)):
            total = refs[0][:, at].astype(f32)
            for x in refs[1:n_in]:
                total = total + x[:, at].astype(f32)
            out_ref[...] = (grad_scale * total).astype(bf16)

    aliased = [] if totals is None else list(totals)
    shape = jax.ShapeDtypeStruct((piece, hidden_width), bf16)
    out_spec = pl.BlockSpec((pl.Element(r), pl.Element(w)), lambda i: (i * r, start))
    return pl.pallas_call(
        body,
        out_shape=(shape, shape),
        grid=(piece // r,),
        in_specs=[pl.BlockSpec((r, both_width), lambda i: (i, 0))] * n_in
        + [pl.BlockSpec(memory_space=pl.ANY) for _ in aliased],
        out_specs=(out_spec, out_spec),
        input_output_aliases={n_in: 0, n_in + 1: 1} if aliased else {},
        compiler_params=pltpu.CompilerParams(vmem_limit_bytes=KERNEL_VMEM),
        cost_estimate=LIGHT,
        name="join_halves",
    )(own, *arrived, *aliased)


def spread_back(parts, starts, gate_mat, up_mat, table, tok_rows, first, heights):
    n_peers, _, cap = table.shape
    half = n_peers // 2
    width, hidden_width = gate_mat.shape
    cols = min(512, width)
    rows = half * cap
    shift = 0 if first else 1
    owner = [(i, b) for i, height in enumerate(heights) for b in range(height)]

    def body(*refs):
        part_refs = refs[: len(parts)]
        gate_ref, up_ref, table_ref = refs[len(parts) : len(parts) + 3]
        out_refs = refs[len(parts) + 3 :]
        total = jnp.zeros((rows, cols), f32)
        for start, part_ref in zip(starts, part_refs):
            w = part_ref.shape[1] // 2
            total += dot(part_ref[:, :w], gate_ref[:, start : start + w], ((1,), (1,)))
            total += dot(part_ref[:, w:], up_ref[:, start : start + w], ((1,), (1,)))
        terms = total.astype(bf16)
        for j, (i, b) in enumerate(owner):
            tok = table_ref[j, 0:1, :]
            place = (lax.broadcasted_iota(i32, (tok_rows, cap), 0).astype(f32) == tok).astype(bf16)
            spread = jnp.dot(place, terms[j * cap : (j + 1) * cap], preferred_element_type=f32)
            out_refs[i][b * tok_rows : (b + 1) * tok_rows, :] = spread.astype(bf16)

    return pl.pallas_call(
        body,
        out_shape=[jax.ShapeDtypeStruct((h * tok_rows, width), bf16) for h in heights],
        grid=(width // cols,),
        in_specs=[pl.BlockSpec((rows, x.shape[1]), lambda j: (shift, 0)) for x in parts]
        + [
            pl.BlockSpec((cols, hidden_width), lambda j: (j, 0)),
            pl.BlockSpec((cols, hidden_width), lambda j: (j, 0)),
            pl.BlockSpec((half, 2, cap), lambda j: (shift, 0, 0)),
        ],
        out_specs=[pl.BlockSpec((h * tok_rows, cols), lambda j: (0, j)) for h in heights],
        compiler_params=pltpu.CompilerParams(vmem_limit_bytes=KERNEL_VMEM),
        cost_estimate=LIGHT,
        name="spread_back",
    )(*parts, gate_mat, up_mat, table)


def local(tokens, out_grad, gate_saved, probs, expert_ids, w_gate, w_up, w_down):
    n_peers = lax.axis_size("expert")
    n_dp = lax.axis_size("dp")
    group = lax.axis_index("dp")
    tok_rows, model_width = tokens.shape
    top_k = expert_ids.shape[1]
    hidden_width = w_up.shape[2]
    cap = min(tok_rows, 2 * tok_rows * top_k // n_peers)
    n_routes = tok_rows * top_k
    n_slots = n_peers * cap
    gate_mat, up_mat, down_mat = w_gate[0], w_up[0], w_down[0]

    experts = jnp.arange(n_peers, dtype=i32)
    hit = expert_ids[:, :, None] == experts[None, None, :]
    named = jnp.any(hit, axis=1)
    weight = jnp.sum(jnp.where(hit, probs[:, :, None], 0.0), axis=1)
    rank = jnp.cumsum(named.astype(i32), axis=0) - 1
    slots = jnp.arange(cap, dtype=i32)
    in_slot = named[:, :, None] & (rank[:, :, None] == slots[None, None, :])
    tok_of = jnp.sum(
        jnp.where(in_slot, jnp.arange(1, tok_rows + 1, dtype=f32)[:, None, None], 0.0), axis=0
    ) - 1.0
    choice = jnp.sum(jnp.where(hit, jnp.arange(top_k, dtype=f32)[None, :, None], 0.0), axis=1)
    choice_of = jnp.sum(jnp.where(in_slot, choice[:, :, None], 0.0), axis=0)
    weight_of = jnp.sum(jnp.where(in_slot, weight[:, :, None], 0.0), axis=0)
    table = lax.all_to_all(
        jnp.concatenate([tok_of, weight_of], axis=1),
        "expert",
        split_axis=0,
        concat_axis=0,
        tiled=True,
    )
    ring = Ring()
    table = table.reshape(n_peers, 2, cap)[ring.order]
    widths = chunk_widths(hidden_width)
    starts = [sum(widths[:i]) for i in range(len(widths))]
    route_gates = jnp.transpose(gate_saved, (1, 0, 2)).reshape(n_routes, hidden_width)
    route_of = (tok_of + tok_rows * choice_of).astype(i32).reshape(n_slots, 1)
    pick = (route_of == jnp.arange(n_routes, dtype=i32)[None, :]).astype(bf16)
    send_gate = [
        dot(pick, route_gates[:, s : s + w], ((1,), (0,))).astype(bf16).reshape(n_peers, cap, w)
        for s, w in zip(starts, widths)
    ]
    (rows_in, routed, up_first, grad_first), mark, send_gate[1:] = gather_rows(
        ring,
        tokens,
        out_grad,
        table.transpose(0, 2, 1),
        cap,
        up_mat,
        down_mat,
        widths[0],
        send_gate[1:],
    )

    def send_chunk(i, mark):
        part = send_gate[i]
        if mark is not None:
            part, _ = lax.optimization_barrier((part, mark))
        return lax.all_to_all(part, "expert", split_axis=0, concat_axis=0, tiled=True)

    recv_gate = [send_chunk(i, mark) for i, mark in zip(range(len(widths)), (None, mark))]

    piece = model_width // n_dp
    shifts = [[(i, (i + d) % n_dp) for i in range(n_dp)] for d in range(n_dp)]

    peer_cols = lax.rem(group + jnp.arange(1, n_dp, dtype=i32), n_dp)
    own_cols = group.reshape(1).astype(i32)
    both_parts, arrivals, own_parts = [], [], []
    sum_down = None
    rows_now, routed_now = rows_in, routed
    for c, w in enumerate(widths):
        hidden, both, sent = chunk_grads(
            ring.order,
            peer_cols,
            rows_now,
            routed_now,
            recv_gate[c],
            up_mat,
            down_mat,
            starts[c],
            piece,
            (up_first, grad_first) if c == 0 else None,
        )
        both_parts.append(both)
        arrivals.append(
            [
                lax.ppermute(sent[(d - 1) * piece : d * piece], "dp", shifts[d])
                for d in range(1, n_dp)
            ]
        )
        if c + 1 < len(widths):
            own = own_half(own_cols, rows_now, both, piece)
            sum_down = down_rows(routed_now, hidden, starts[c], sum_down, hidden_width)
            if c + 2 < len(widths):
                recv_gate.append(send_chunk(c + 2, own))
            if c >= 1:
                rows_now, arrivals[c - 1] = lax.optimization_barrier((rows_now, arrivals[c - 1]))
            rows_now, routed_now, own, sum_down = lax.optimization_barrier(
                (rows_now, routed_now, own, sum_down)
            )
            own_parts.append(own)

    heights = [1] + [2] * (ring.far - 1) + [1]
    theirs = spread_back(both_parts, starts, gate_mat, up_mat, table, tok_rows, True, heights)
    hidden, _ = lax.optimization_barrier((hidden, theirs))
    sum_down = down_rows(routed_now, hidden, starts[-1], sum_down, hidden_width)
    low = hidden_width // n_dp
    sent = [
        lax.dynamic_slice_in_dim(sum_down, lax.rem(group + d, n_dp) * low, low, 0)
        for d in range(1, n_dp)
    ]
    last, arrivals[:-1], sent = lax.optimization_barrier((both, arrivals[:-1], sent))
    arrived = [lax.ppermute(part, "dp", shifts[d]) for d, part in enumerate(sent, 1)]
    mine = spread_back(
        both_parts[:-1] + [last], starts, gate_mat, up_mat, table, tok_rows, False, heights
    )
    mine, arrivals[-1] = lax.optimization_barrier((mine, arrivals[-1]))

    def last_half(mark):
        held, _ = lax.optimization_barrier((both, mark))
        return own_half(own_cols, rows_now, held, piece), arrivals[-1]

    def join_first(mark):
        parts, _ = lax.optimization_barrier((own_parts, mark))
        joined = None
        for c, part in enumerate(parts):
            joined = join_halves(part, arrivals[c], starts[c], joined, hidden_width)
        return joined

    input_grad, ((own, arrivals[-1]), totals) = sum_back(
        ring, theirs, mine, tok_rows, [last_half, join_first]
    )
    arrived, _ = lax.optimization_barrier((arrived, input_grad))
    grad_gate, grad_up = join_halves(own, arrivals[-1], starts[-1], totals, hidden_width)
    down = lax.dynamic_slice_in_dim(sum_down, group * low, low, 0).astype(f32)
    for part in arrived:
        down = down + part.astype(f32)
    grad_down = (grad_scale * down).astype(bf16)[None]
    return (input_grad, grad_gate[None], grad_up[None], grad_down)


def solution(mesh):
    return jax.shard_map(
        local,
        mesh=mesh,
        in_specs=(
            P(("dp", "expert"), None),
            P(("dp", "expert"), None),
            P(("dp", "expert"), None, None),
            P(("dp", "expert"), None),
            P(("dp", "expert"), None),
            P("expert", None, None),
            P("expert", None, None),
            P("expert", None, None),
        ),
        out_specs=(
            P(("dp", "expert"), None),
            P("expert", "dp", None),
            P("expert", "dp", None),
            P("expert", "dp", None),
        ),
        check_vma=False,
    )
```

```python
import jax
import jax.numpy as jnp
import numpy as np
from jax import lax
from jax.experimental import pallas as pl
from jax.experimental.pallas import tpu as pltpu
from jax.sharding import PartitionSpec as P

grad_scale = 0.0625
f32 = jnp.float32
bf16 = jnp.bfloat16
i32 = jnp.int32
KERNEL_VMEM = 60 * 1024 * 1024
LIGHT = pl.CostEstimate(flops=1000, bytes_accessed=1000, transcendentals=0)


def dot(a, b, dims):
    return lax.dot_general(a, b, (dims, ((), ())), preferred_element_type=f32)


def chunk_widths(width):
    lanes = width // 128
    if lanes < 8:
        return [[width]]
    ends = [-(-lanes * x // 11) * 128 for x in (0, 2, 5, 8, 11)]
    sizes = [e - s for s, e in zip(ends, ends[1:])]
    return [sizes[:2], sizes[2:]]


def chip_cycle(n_chips):
    cols = n_chips // 4
    if n_chips % 4 or cols < 2:
        return list(range(n_chips))
    walk = [(row, 0) for row in range(4)]
    for step, row in enumerate((3, 2, 1, 0)):
        across = range(1, cols) if step % 2 == 0 else range(cols - 1, 0, -1)
        walk += [(row, col) for col in across]
    return [row * cols + col for row, col in walk]


def put_rows(spots, table, shards, up_mat, down_mat, w, state, cap):
    count = len(shards)
    n_peers = table.shape[0]
    width = shards[0][0].shape[1]
    tok_rows = shards[0][2]

    def body(spots_ref, table_ref, up_ref, down_ref, *refs):
        parts = refs[: 2 * count]
        rows_ref, routed_ref, act_ref, grad_ref = refs[-4:]
        step = pl.program_id(0)
        for i in range(count):

            @pl.when(step == i)
            def _():
                info = table_ref[0]
                place = (
                    lax.broadcasted_iota(i32, (cap, tok_rows), 1).astype(f32) == info[:, 0:1]
                ).astype(bf16)
                rows_ref[...] = jnp.dot(
                    place, parts[2 * i][...], preferred_element_type=f32
                ).astype(bf16)
                picked = jnp.dot(place, parts[2 * i + 1][...], preferred_element_type=f32)
                routed_ref[...] = (info[:, 1:2] * picked).astype(bf16)

        act_ref[...] = jnp.dot(rows_ref[...], up_ref[...], preferred_element_type=f32)
        grad_ref[...] = dot(routed_ref[...], down_ref[...], ((1,), (1,)))

    in_specs = [
        pl.BlockSpec((1, cap, 2), lambda i, spots: (spots[i], 0, 0)),
        pl.BlockSpec((width, w), lambda i, spots: (0, 0)),
        pl.BlockSpec((w, width), lambda i, spots: (0, 0)),
    ]
    operands = [table, up_mat, down_mat]
    for tok, grad, height, tok_at, grad_at in shards:
        in_specs.append(pl.BlockSpec((height, width), lambda i, spots, a=tok_at: (a, 0)))
        in_specs.append(pl.BlockSpec((height, width), lambda i, spots, a=grad_at: (a, 0)))
        operands += [tok, grad]
    aliases = {}
    if state is not None:
        aliases = {1 + len(operands) + j: j for j in range(4)}
        in_specs += [pl.BlockSpec(memory_space=pl.ANY)] * 4
        operands += state
    n_slots = n_peers * cap

    def at(i, spots):
        return (spots[i], 0)

    return pl.pallas_call(
        body,
        out_shape=(
            jax.ShapeDtypeStruct((n_slots, width), bf16),
            jax.ShapeDtypeStruct((n_slots, width), bf16),
            jax.ShapeDtypeStruct((n_slots, w), f32),
            jax.ShapeDtypeStruct((n_slots, w), f32),
        ),
        grid_spec=pltpu.PrefetchScalarGridSpec(
            num_scalar_prefetch=1,
            grid=(count,),
            in_specs=in_specs,
            out_specs=(
                pl.BlockSpec((cap, width), at),
                pl.BlockSpec((cap, width), at),
                pl.BlockSpec((cap, w), at),
                pl.BlockSpec((cap, w), at),
            ),
        ),
        input_output_aliases=aliases,
        compiler_params=pltpu.CompilerParams(vmem_limit_bytes=KERNEL_VMEM),
        cost_estimate=LIGHT,
        name="put_rows",
    )(np.array(spots, np.int32), *operands)


class Ring:
    def __init__(self):
        self.n_peers = lax.axis_size("expert")
        self.n = self.n_peers // 2
        self.far = self.n // 2
        self.names = [self.far]
        for d in range(self.far - 1, 0, -1):
            self.names += [d, -d]
        self.names.append(0)
        cycle = chip_cycle(self.n)
        spot = [cycle.index(c) for c in range(self.n)]
        chips = range(self.n)
        self.fwd = [(2 * cycle[i] + c, 2 * cycle[(i + 1) % self.n] + c) for i in chips for c in (0, 1)]
        self.bwd = [(b, a) for a, b in self.fwd]
        self.swap = [(i, i ^ 1) for i in range(self.n_peers)]
        table = np.zeros((self.n_peers, self.n_peers), np.int32)
        for e in range(self.n_peers):
            for core in (0, 1):
                for j, d in enumerate(self.names):
                    chip = cycle[(spot[e // 2] - d) % self.n]
                    table[e, core * self.n + j] = 2 * chip + (e % 2 if core else 1 - e % 2)
        self.order = jnp.asarray(table)[lax.axis_index("expert")]

    def at(self, distance, other):
        return self.names.index(distance) + (0 if other else self.n)

    def ahead(self, x):
        return lax.ppermute(x, "expert", self.fwd)

    def behind(self, x):
        return lax.ppermute(x, "expert", self.bwd)

    def other_core(self, x):
        return lax.ppermute(x, "expert", self.swap)


def gather_rows(ring, tokens, out_grad, table, cap, up_mat, down_mat, first_width, beside):
    tok_rows = tokens.shape[0]
    beside = list(beside)
    own = jnp.concatenate([tokens, out_grad], axis=0)

    def whole(x):
        return (x, x, tok_rows, 0, 1)

    def place(spots, shards, state):
        return put_rows(spots, table, shards, up_mat, down_mat, first_width, state, cap)

    state = None
    ahead, behind = own, own
    pending = [([ring.at(0, False), ring.at(0, True)], [whole(own), whole(ring.other_core(own))])]
    for d in range(1, ring.far):
        ahead, behind = ring.ahead(ahead), ring.behind(behind)
        if d == 1:
            ahead, behind, table = lax.optimization_barrier((ahead, behind, table))
        else:
            now, pending = (pending[:1], pending[1:]) if d == 2 else (pending, [])
            for spots, shards in now:
                state = place(spots, shards, state)
            ahead, behind, state = lax.optimization_barrier((ahead, behind, state))
            if d - 2 < len(beside):
                ahead, behind, beside[d - 2] = lax.optimization_barrier(
                    (ahead, behind, beside[d - 2])
                )
        pending.append(
            (
                [ring.at(d, False), ring.at(-d, False), ring.at(d, True), ring.at(-d, True)],
                [whole(x) for x in (ahead, behind, ring.other_core(ahead), ring.other_core(behind))],
            )
        )
    far_tok = ring.ahead(ahead[:tok_rows])
    far_grad = ring.behind(behind[tok_rows:])
    for spots, shards in pending:
        state = place(spots, shards, state)
    far_tok, far_grad, state = lax.optimization_barrier((far_tok, far_grad, state))
    theirs_tok, theirs_grad = ring.other_core(far_tok), ring.other_core(far_grad)
    state = place(
        [ring.at(ring.far, False), ring.at(ring.far, True)],
        [(far_tok, far_grad, tok_rows, 0, 0), (theirs_tok, theirs_grad, tok_rows, 0, 0)],
        state,
    )
    return state, (theirs_tok, theirs_grad), beside


def add_blocks(blocks, tok_rows, split):
    width = blocks[0][0][0].shape[1]
    operands = [x for terms in blocks for x in terms]
    half = tok_rows // 2

    def body(*refs):
        outs, at = refs[len(operands) :], 0
        for i, terms in enumerate(blocks):
            for lower in (0, half):
                total = jnp.zeros((half, width), f32)
                for j, (_, _, rows, first) in enumerate(terms):
                    if first <= lower < first + rows:
                        total += refs[at + j][lower - first : lower - first + half, :].astype(f32)
                if split:
                    outs[1 if lower else 0][...] = total.astype(bf16)
                else:
                    outs[i][lower : lower + half, :] = total.astype(bf16)
            at += len(terms)

    height, count = (half, 2) if split else (tok_rows, len(blocks))
    out = pl.pallas_call(
        body,
        out_shape=[jax.ShapeDtypeStruct((height, width), bf16)] * count,
        grid=(1,),
        in_specs=[
            pl.BlockSpec((rows, width), lambda i, at=at: (at, 0)) for _, at, rows, _ in operands
        ],
        out_specs=[pl.BlockSpec((height, width), lambda i: (0, 0))] * count,
        compiler_params=pltpu.CompilerParams(vmem_limit_bytes=KERNEL_VMEM),
        cost_estimate=LIGHT,
        name="add_blocks",
    )(*[x for x, _, _, _ in operands])
    return list(out)


def sum_back(ring, theirs, mine, tok_rows, fills):
    terms = {}
    j = 0
    for piece, own in zip(theirs, mine):
        piece = ring.other_core(piece)
        for at in range(piece.shape[0] // tok_rows):
            terms[ring.names[j]] = [(own, at, tok_rows, 0), (piece, at, tok_rows, 0)]
            j += 1

    half = tok_rows // 2
    top, low = add_blocks([terms[ring.far]], tok_rows, True)
    ahead, behind = (ring.ahead(top), 0, half, 0), (ring.behind(low), 0, half, half)
    mark, filled = (ahead[0], behind[0]), []
    for d in range(ring.far - 1, 0, -1):
        ahead, behind = add_blocks([terms[-d] + [ahead], terms[d] + [behind]], tok_rows, False)
        ahead, behind = ring.ahead(ahead), ring.behind(behind)
        if len(filled) < len(fills):
            done = fills[len(filled)](mark)
            ahead, behind, done = lax.optimization_barrier((ahead, behind, done))
            filled.append(done)
        mark = (ahead, behind)
        ahead, behind = (ahead, 0, tok_rows, 0), (behind, 0, tok_rows, 0)
    for fill in fills[len(filled) :]:
        filled.append(fill(mark))
    return add_blocks([terms[0] + [ahead, behind]], tok_rows, False)[0], filled


def blocks_per_step(n_blocks, cap):
    return max(b for b in range(1, n_blocks + 1) if n_blocks % b == 0 and b * cap <= 768)


def chunk_grads(order, cols, rows, routed, gate, gate_at, w, up_mat, down_mat, start, piece, ready):
    n_slots, width = rows.shape
    n_peers, cap, _ = gate.shape
    n = blocks_per_step(n_peers, cap)
    r = n * cap
    n_rows, n_cols = n_slots // r, cols.shape[0]
    n_in = 4 if ready is None else 2

    def body(order_ref, cols_ref, *refs):
        ins, col_ref, gate_refs = refs[:n_in], refs[n_in], refs[n_in + 1 : n_in + 1 + n]
        hidden_ref, both_ref, part_ref, held = refs[n_in + 1 + n :]
        step = pl.program_id(0)

        @pl.when(step < n_rows)
        def _():
            if ready is None:
                up_all = jnp.dot(ins[0][...], ins[2][...], preferred_element_type=f32)
                grad_all = dot(ins[1][...], ins[3][...], ((1,), (1,)))
            else:
                up_all, grad_all = ins
            for b in range(n):
                at = slice(b * cap, (b + 1) * cap)
                up_act, hidden_grad = up_all[at, :], grad_all[at, :]
                gate_val = gate_refs[b][0].astype(f32)
                gate_sig = jax.nn.sigmoid(gate_val)
                gate_act = gate_val * gate_sig
                hidden_ref[at, :] = (gate_act * up_act).astype(bf16)
                both_ref[at, w:] = (hidden_grad * gate_act).astype(bf16)
                both_ref[at, :w] = (
                    hidden_grad * up_act * gate_sig * (1.0 + gate_val * (1.0 - gate_sig))
                ).astype(bf16)
            held[pl.ds(pl.multiple_of(step * r, r), r), :] = both_ref[...]

        @pl.when(step >= n_rows)
        def _():
            part_ref[...] = dot(col_ref[...], held[...], ((0,), (0,))).astype(bf16)

    def row(i):
        return jnp.minimum(i, n_rows - 1)

    def col(i):
        return jnp.maximum(i - n_rows, 0)

    def row_blocks(x):
        return pl.BlockSpec((r, x.shape[1]), lambda i, order, cols: (row(i), 0))

    if ready is None:
        operands = [rows, routed, up_mat, down_mat]
        in_specs = [
            row_blocks(rows),
            row_blocks(routed),
            pl.BlockSpec((pl.Element(width), pl.Element(w)), lambda i, order, cols: (0, start)),
            pl.BlockSpec((pl.Element(w), pl.Element(width)), lambda i, order, cols: (start, 0)),
        ]
    else:
        operands = list(ready)
        in_specs = [row_blocks(x) for x in ready]
    return pl.pallas_call(
        body,
        out_shape=(
            jax.ShapeDtypeStruct((n_slots, w), bf16),
            jax.ShapeDtypeStruct((n_slots, 2 * w), bf16),
            jax.ShapeDtypeStruct((n_cols * piece, 2 * w), bf16),
        ),
        grid_spec=pltpu.PrefetchScalarGridSpec(
            num_scalar_prefetch=2,
            grid=(n_rows + n_cols,),
            in_specs=in_specs
            + [pl.BlockSpec((n_slots, piece), lambda i, order, cols: (0, cols[col(i)]))]
            + [
                pl.BlockSpec(
                    (pl.Element(1), pl.Element(cap), pl.Element(w)),
                    lambda i, order, cols, b=b: (order[n * row(i) + b], 0, gate_at),
                )
                for b in range(n)
            ],
            out_specs=(
                pl.BlockSpec((r, w), lambda i, order, cols: (row(i), 0)),
                pl.BlockSpec((r, 2 * w), lambda i, order, cols: (row(i), 0)),
                pl.BlockSpec((piece, 2 * w), lambda i, order, cols: (col(i), 0)),
            ),
            scratch_shapes=[pltpu.VMEM((n_slots, 2 * w), bf16)],
        ),
        compiler_params=pltpu.CompilerParams(vmem_limit_bytes=KERNEL_VMEM),
        cost_estimate=LIGHT,
        name="chunk_grads",
    )(order, cols, *operands, rows, *[gate] * n)


def own_half(cols, rows, both, piece):
    n_slots = rows.shape[0]
    w = both.shape[1]

    def body(cols_ref, rows_ref, both_ref, own_ref):
        own_ref[...] = dot(rows_ref[...], both_ref[...], ((0,), (0,))).astype(bf16)

    return pl.pallas_call(
        body,
        out_shape=jax.ShapeDtypeStruct((piece, w), bf16),
        grid_spec=pltpu.PrefetchScalarGridSpec(
            num_scalar_prefetch=1,
            grid=(1,),
            in_specs=[
                pl.BlockSpec((n_slots, piece), lambda i, cols: (0, cols[0])),
                pl.BlockSpec((n_slots, w), lambda i, cols: (0, 0)),
            ],
            out_specs=pl.BlockSpec((piece, w), lambda i, cols: (0, 0)),
        ),
        compiler_params=pltpu.CompilerParams(vmem_limit_bytes=KERNEL_VMEM),
        cost_estimate=LIGHT,
        name="own_half",
    )(cols, rows, both)


def down_rows(routed, hidden, start, total, hidden_width):
    n_slots, width = routed.shape
    w = hidden.shape[1]
    span = min(1024, width)

    def body(routed_ref, hidden_ref, *refs):
        down_ref, turned = refs[-2:]

        @pl.when(pl.program_id(0) == 0)
        def _():
            turned[...] = hidden_ref[...].T

        down_ref[...] = jnp.dot(turned[...], routed_ref[...], preferred_element_type=f32).astype(bf16)

    aliased = [] if total is None else [total]
    return pl.pallas_call(
        body,
        out_shape=jax.ShapeDtypeStruct((hidden_width, width), bf16),
        grid=(width // span,),
        in_specs=[
            pl.BlockSpec((n_slots, span), lambda i: (0, i)),
            pl.BlockSpec((n_slots, w), lambda i: (0, 0)),
        ]
        + [pl.BlockSpec(memory_space=pl.ANY) for _ in aliased],
        out_specs=pl.BlockSpec((pl.Element(w), pl.Element(span)), lambda i: (start, i * span)),
        scratch_shapes=[pltpu.VMEM((w, n_slots), bf16)],
        input_output_aliases={2: 0} if aliased else {},
        compiler_params=pltpu.CompilerParams(vmem_limit_bytes=KERNEL_VMEM),
        cost_estimate=LIGHT,
        name="down_rows",
    )(routed, hidden, *aliased)


def join_halves(own, arrived, start, totals, hidden_width):
    piece, both_width = own.shape
    w = both_width // 2
    r = min(256, piece)
    n_in = 1 + len(arrived)

    def body(*refs):
        gate_ref, up_ref = refs[-2:]
        for at, out_ref in ((slice(0, w), gate_ref), (slice(w, 2 * w), up_ref)):
            total = refs[0][:, at].astype(f32)
            for x in refs[1:n_in]:
                total = total + x[:, at].astype(f32)
            out_ref[...] = (grad_scale * total).astype(bf16)

    aliased = [] if totals is None else list(totals)
    shape = jax.ShapeDtypeStruct((piece, hidden_width), bf16)
    out_spec = pl.BlockSpec((pl.Element(r), pl.Element(w)), lambda i: (i * r, start))
    return pl.pallas_call(
        body,
        out_shape=(shape, shape),
        grid=(piece // r,),
        in_specs=[pl.BlockSpec((r, both_width), lambda i: (i, 0))] * n_in
        + [pl.BlockSpec(memory_space=pl.ANY) for _ in aliased],
        out_specs=(out_spec, out_spec),
        input_output_aliases={n_in: 0, n_in + 1: 1} if aliased else {},
        compiler_params=pltpu.CompilerParams(vmem_limit_bytes=KERNEL_VMEM),
        cost_estimate=LIGHT,
        name="join_halves",
    )(own, *arrived, *aliased)


def spread_back(parts, starts, gate_mat, up_mat, table, tok_rows, first, heights):
    n_peers, _, cap = table.shape
    half = n_peers // 2
    width, hidden_width = gate_mat.shape
    cols = min(512, width)
    rows = half * cap
    shift = 0 if first else 1
    owner = [(i, b) for i, height in enumerate(heights) for b in range(height)]

    def body(*refs):
        part_refs = refs[: len(parts)]
        gate_ref, up_ref, table_ref = refs[len(parts) : len(parts) + 3]
        out_refs = refs[len(parts) + 3 :]
        total = jnp.zeros((rows, cols), f32)
        for start, part_ref in zip(starts, part_refs):
            w = part_ref.shape[1] // 2
            total += dot(part_ref[:, :w], gate_ref[:, start : start + w], ((1,), (1,)))
            total += dot(part_ref[:, w:], up_ref[:, start : start + w], ((1,), (1,)))
        terms = total.astype(bf16)
        for j, (i, b) in enumerate(owner):
            tok = table_ref[j, 0:1, :]
            place = (lax.broadcasted_iota(i32, (tok_rows, cap), 0).astype(f32) == tok).astype(bf16)
            spread = jnp.dot(place, terms[j * cap : (j + 1) * cap], preferred_element_type=f32)
            out_refs[i][b * tok_rows : (b + 1) * tok_rows, :] = spread.astype(bf16)

    return pl.pallas_call(
        body,
        out_shape=[jax.ShapeDtypeStruct((h * tok_rows, width), bf16) for h in heights],
        grid=(width // cols,),
        in_specs=[pl.BlockSpec((rows, x.shape[1]), lambda j: (shift, 0)) for x in parts]
        + [
            pl.BlockSpec((cols, hidden_width), lambda j: (j, 0)),
            pl.BlockSpec((cols, hidden_width), lambda j: (j, 0)),
            pl.BlockSpec((half, 2, cap), lambda j: (shift, 0, 0)),
        ],
        out_specs=[pl.BlockSpec((h * tok_rows, cols), lambda j: (0, j)) for h in heights],
        compiler_params=pltpu.CompilerParams(vmem_limit_bytes=KERNEL_VMEM),
        cost_estimate=LIGHT,
        name="spread_back",
    )(*parts, gate_mat, up_mat, table)


def local(tokens, out_grad, gate_saved, probs, expert_ids, w_gate, w_up, w_down):
    n_peers = lax.axis_size("expert")
    n_dp = lax.axis_size("dp")
    group = lax.axis_index("dp")
    tok_rows, model_width = tokens.shape
    top_k = expert_ids.shape[1]
    hidden_width = w_up.shape[2]
    cap = min(tok_rows, 2 * tok_rows * top_k // n_peers)
    n_routes = tok_rows * top_k
    n_slots = n_peers * cap
    gate_mat, up_mat, down_mat = w_gate[0], w_up[0], w_down[0]

    experts = jnp.arange(n_peers, dtype=i32)
    hit = expert_ids[:, :, None] == experts[None, None, :]
    named = jnp.any(hit, axis=1)
    weight = jnp.sum(jnp.where(hit, probs[:, :, None], 0.0), axis=1)
    rank = jnp.cumsum(named.astype(i32), axis=0) - 1
    slots = jnp.arange(cap, dtype=i32)
    in_slot = named[:, :, None] & (rank[:, :, None] == slots[None, None, :])
    tok_of = jnp.sum(
        jnp.where(in_slot, jnp.arange(1, tok_rows + 1, dtype=f32)[:, None, None], 0.0), axis=0
    ) - 1.0
    choice = jnp.sum(jnp.where(hit, jnp.arange(top_k, dtype=f32)[None, :, None], 0.0), axis=1)
    choice_of = jnp.sum(jnp.where(in_slot, choice[:, :, None], 0.0), axis=0)
    weight_of = jnp.sum(jnp.where(in_slot, weight[:, :, None], 0.0), axis=0)
    table = lax.all_to_all(
        jnp.concatenate([tok_of, weight_of], axis=1),
        "expert",
        split_axis=0,
        concat_axis=0,
        tiled=True,
    )
    ring = Ring()
    table = table.reshape(n_peers, 2, cap)[ring.order]
    groups = chunk_widths(hidden_width)
    widths = [w for group_widths in groups for w in group_widths]
    starts = [sum(widths[:i]) for i in range(len(widths))]
    spans = [sum(group_widths) for group_widths in groups]
    offsets = [sum(spans[:i]) for i in range(len(spans))]
    route_gates = jnp.transpose(gate_saved, (1, 0, 2)).reshape(n_routes, hidden_width)
    route_of = (tok_of + tok_rows * choice_of).astype(i32).reshape(n_slots, 1)
    pick = (route_of == jnp.arange(n_routes, dtype=i32)[None, :]).astype(bf16)
    send_gate = [
        dot(pick, route_gates[:, s : s + w], ((1,), (0,))).astype(bf16).reshape(n_peers, cap, w)
        for s, w in zip(offsets, spans)
    ]
    def exchange(part):
        return lax.all_to_all(part, "expert", split_axis=0, concat_axis=0, tiled=True)

    (rows_in, routed, up_first, grad_first), mark, (_, (recv_gate, rest)) = gather_rows(
        ring,
        tokens,
        out_grad,
        table.transpose(0, 2, 1),
        cap,
        up_mat,
        down_mat,
        widths[0],
        [send_gate[:1], ([exchange(send_gate[0])], send_gate[1:])],
    )
    rest, _ = lax.optimization_barrier((rest, mark))
    recv_gate = recv_gate + [exchange(part) for part in rest]
    gate_of = [
        (recv_gate[i], sum(group_widths[:j]))
        for i, group_widths in enumerate(groups)
        for j in range(len(group_widths))
    ]

    piece = model_width // n_dp
    shifts = [[(i, (i + d) % n_dp) for i in range(n_dp)] for d in range(n_dp)]

    peer_cols = lax.rem(group + jnp.arange(1, n_dp, dtype=i32), n_dp)
    own_cols = group.reshape(1).astype(i32)
    both_parts, hidden_parts, arrivals = [], [], []
    own_parts, sum_down = [], None
    early = len(groups[0])
    rows_now, routed_now = rows_in, routed
    for c, w in enumerate(widths):
        if c == early:
            for e in range(early):
                own_parts.append(own_half(own_cols, rows_now, both_parts[e], piece))
                sum_down = down_rows(
                    routed_now, hidden_parts[e], starts[e], sum_down, hidden_width
                )
            rows_now, routed_now, own_parts, sum_down = lax.optimization_barrier(
                (rows_now, routed_now, own_parts, sum_down)
            )
        if c >= 2:
            rows_now, arrivals[c - 2] = lax.optimization_barrier((rows_now, arrivals[c - 2]))
        gate, gate_at = gate_of[c]
        hidden, both, sent = chunk_grads(
            ring.order,
            peer_cols,
            rows_now,
            routed_now,
            gate,
            gate_at,
            w,
            up_mat,
            down_mat,
            starts[c],
            piece,
            (up_first, grad_first) if c == 0 else None,
        )
        both_parts.append(both)
        hidden_parts.append(hidden)
        arrivals.append(
            [
                lax.ppermute(sent[(d - 1) * piece : d * piece], "dp", shifts[d])
                for d in range(1, n_dp)
            ]
        )
        rows_now, routed_now, _ = lax.optimization_barrier((rows_now, routed_now, sent))

    heights = [1] + [2] * (ring.far - 1) + [1]
    theirs = spread_back(both_parts, starts, gate_mat, up_mat, table, tok_rows, True, heights)
    late = list(range(min(early, len(widths)), len(widths)))
    for c in late:
        hidden, _ = lax.optimization_barrier((hidden_parts[c], theirs))
        sum_down = down_rows(routed_now, hidden, starts[c], sum_down, hidden_width)
    if not late:
        own_parts = [own_half(own_cols, rows_now, x, piece) for x in both_parts]
        for c, hidden in enumerate(hidden_parts):
            sum_down = down_rows(routed_now, hidden, starts[c], sum_down, hidden_width)
    low = hidden_width // n_dp
    sent = [
        lax.dynamic_slice_in_dim(sum_down, lax.rem(group + d, n_dp) * low, low, 0)
        for d in range(1, n_dp)
    ]
    last, arrivals[:-1], sent = lax.optimization_barrier((both_parts[-1], arrivals[:-1], sent))
    arrived = [lax.ppermute(part, "dp", shifts[d]) for d, part in enumerate(sent, 1)]
    mine = spread_back(
        both_parts[:-1] + [last], starts, gate_mat, up_mat, table, tok_rows, False, heights
    )
    mine, arrivals[-1] = lax.optimization_barrier((mine, arrivals[-1]))

    def late_halves(mark):
        parts, _ = lax.optimization_barrier((both_parts, mark))
        return [own_half(own_cols, rows_now, parts[c], piece) for c in late]

    def join_early(mark):
        parts, _ = lax.optimization_barrier((own_parts, mark))
        joined = None
        for c, part in enumerate(parts):
            joined = join_halves(part, arrivals[c], starts[c], joined, hidden_width)
        return joined

    input_grad, (late_parts, totals) = sum_back(
        ring, theirs, mine, tok_rows, [late_halves, join_early]
    )
    arrived, _ = lax.optimization_barrier((arrived, input_grad))
    for c, part in zip(late, late_parts):
        totals = join_halves(part, arrivals[c], starts[c], totals, hidden_width)
    grad_gate, grad_up = totals
    down = lax.dynamic_slice_in_dim(sum_down, group * low, low, 0).astype(f32)
    for part in arrived:
        down = down + part.astype(f32)
    grad_down = (grad_scale * down).astype(bf16)[None]
    return (input_grad, grad_gate[None], grad_up[None], grad_down)


def solution(mesh):
    return jax.shard_map(
        local,
        mesh=mesh,
        in_specs=(
            P(("dp", "expert"), None),
            P(("dp", "expert"), None),
            P(("dp", "expert"), None, None),
            P(("dp", "expert"), None),
            P(("dp", "expert"), None),
            P("expert", None, None),
            P("expert", None, None),
            P("expert", None, None),
        ),
        out_specs=(
            P(("dp", "expert"), None),
            P("expert", "dp", None),
            P("expert", "dp", None),
            P("expert", "dp", None),
        ),
        check_vma=False,
    )
```

```python
import jax
import jax.numpy as jnp
import numpy as np
from jax import lax
from jax.experimental import pallas as pl
from jax.experimental.pallas import tpu as pltpu
from jax.sharding import PartitionSpec as P

grad_scale = 0.0625
f32 = jnp.float32
bf16 = jnp.bfloat16
i32 = jnp.int32
KERNEL_VMEM = 60 * 1024 * 1024
LIGHT = pl.CostEstimate(flops=1000, bytes_accessed=1000, transcendentals=0)


def dot(a, b, dims):
    return lax.dot_general(a, b, (dims, ((), ())), preferred_element_type=f32)


def chunk_widths(width):
    lanes = width // 128
    shares = (3, 7, 11)
    ends = [-(-lanes * x // 11) * 128 for x in shares]
    return [e - s for s, e in zip([0] + ends, ends) if e > s]


def chip_cycle(n_chips):
    cols = n_chips // 4
    if n_chips % 4 or cols < 2:
        return list(range(n_chips))
    walk = [(row, 0) for row in range(4)]
    for step, row in enumerate((3, 2, 1, 0)):
        across = range(1, cols) if step % 2 == 0 else range(cols - 1, 0, -1)
        walk += [(row, col) for col in across]
    return [row * cols + col for row, col in walk]


def put_rows(order, table, shards, rows, routed, cap):
    count = len(shards)
    n_peers, _, _ = table.shape
    width = shards[0][0].shape[1]

    def body(order_ref, table_ref, *refs):
        parts = refs[: 2 * count]
        rows_ref, routed_ref = refs[-2:]
        step = pl.program_id(0)
        for i in range(count):

            @pl.when(step == i)
            def _():
                info = table_ref[0]
                place = (
                    lax.broadcasted_iota(i32, (cap, tok_rows_of), 1).astype(f32) == info[:, 0:1]
                ).astype(bf16)
                rows_ref[...] = jnp.dot(
                    place, parts[2 * i][...], preferred_element_type=f32
                ).astype(bf16)
                picked = jnp.dot(place, parts[2 * i + 1][...], preferred_element_type=f32)
                routed_ref[...] = (info[:, 1:2] * picked).astype(bf16)

    tok_rows_of = shards[0][2]
    in_specs = [pl.BlockSpec((1, cap, 2), lambda i, order: (order[i], 0, 0))]
    operands = [table]
    for tok, grad, height, tok_at, grad_at in shards:
        in_specs.append(pl.BlockSpec((height, width), lambda i, order, a=tok_at: (a, 0)))
        in_specs.append(pl.BlockSpec((height, width), lambda i, order, a=grad_at: (a, 0)))
        operands += [tok, grad]
    aliases = {}
    if rows is not None:
        aliases = {1 + len(operands): 0, 2 + len(operands): 1}
        in_specs += [pl.BlockSpec(memory_space=pl.ANY)] * 2
        operands += [rows, routed]
    n_slots = n_peers * cap
    shape = jax.ShapeDtypeStruct((n_slots, width), bf16)
    out_spec = pl.BlockSpec((cap, width), lambda i, order: (order[i], 0))
    return pl.pallas_call(
        body,
        out_shape=(shape, shape),
        grid_spec=pltpu.PrefetchScalarGridSpec(
            num_scalar_prefetch=1,
            grid=(count,),
            in_specs=in_specs,
            out_specs=(out_spec, out_spec),
        ),
        input_output_aliases=aliases,
        compiler_params=pltpu.CompilerParams(vmem_limit_bytes=KERNEL_VMEM),
        cost_estimate=pl.CostEstimate(
            flops=4 * count * cap * tok_rows_of * width,
            bytes_accessed=4 * count * (tok_rows_of + cap) * width,
            transcendentals=0,
        ),
        name="put_rows",
    )(order, *operands)


class Ring:
    def __init__(self):
        self.n_peers = lax.axis_size("expert")
        self.n = self.n_peers // 2
        self.far = self.n // 2
        self.names = [self.far]
        for d in range(self.far - 1, 0, -1):
            self.names += [d, -d]
        self.names.append(0)
        cycle = chip_cycle(self.n)
        spot = [cycle.index(c) for c in range(self.n)]
        chips = range(self.n)
        self.fwd = [(2 * cycle[i] + c, 2 * cycle[(i + 1) % self.n] + c) for i in chips for c in (0, 1)]
        self.bwd = [(b, a) for a, b in self.fwd]
        self.swap = [(i, i ^ 1) for i in range(self.n_peers)]
        table = np.zeros((self.n_peers, self.n_peers), np.int32)
        for e in range(self.n_peers):
            for core in (0, 1):
                for j, d in enumerate(self.names):
                    chip = cycle[(spot[e // 2] - d) % self.n]
                    table[e, core * self.n + j] = 2 * chip + (e % 2 if core else 1 - e % 2)
        self.order = jnp.asarray(table)[lax.axis_index("expert")]

    def at(self, distance, other):
        return self.names.index(distance) + (0 if other else self.n)

    def ahead(self, x):
        return lax.ppermute(x, "expert", self.fwd)

    def behind(self, x):
        return lax.ppermute(x, "expert", self.bwd)

    def other_core(self, x):
        return lax.ppermute(x, "expert", self.swap)


def gather_rows(ring, tokens, out_grad, table, cap, beside):
    tok_rows = tokens.shape[0]
    beside = list(beside)
    own = jnp.concatenate([tokens, out_grad], axis=0)

    def whole(x):
        return (x, x, tok_rows, 0, 1)

    def place(spots, shards, state):
        return put_rows(np.array(spots, np.int32), table, shards, *state, cap)

    state = (None, None)
    ahead, behind = own, own
    pending = [([ring.at(0, False), ring.at(0, True)], [whole(own), whole(ring.other_core(own))])]
    for d in range(1, ring.far):
        ahead, behind = ring.ahead(ahead), ring.behind(behind)
        if d >= 2:
            now, pending = (pending[:1], pending[1:]) if d == 2 else (pending, [])
            for spots, shards in now:
                state = place(spots, shards, state)
            ahead, behind, state = lax.optimization_barrier((ahead, behind, state))
            if d - 2 < len(beside):
                ahead, behind, beside[d - 2] = lax.optimization_barrier(
                    (ahead, behind, beside[d - 2])
                )
        pending.append(
            (
                [ring.at(d, False), ring.at(-d, False), ring.at(d, True), ring.at(-d, True)],
                [whole(x) for x in (ahead, behind, ring.other_core(ahead), ring.other_core(behind))],
            )
        )
    far_tok = ring.ahead(ahead[:tok_rows])
    far_grad = ring.behind(behind[tok_rows:])
    for spots, shards in pending:
        state = place(spots, shards, state)
    far_tok, far_grad, state = lax.optimization_barrier((far_tok, far_grad, state))
    theirs_tok, theirs_grad = ring.other_core(far_tok), ring.other_core(far_grad)
    state = place(
        [ring.at(ring.far, False), ring.at(ring.far, True)],
        [(far_tok, far_grad, tok_rows, 0, 0), (theirs_tok, theirs_grad, tok_rows, 0, 0)],
        state,
    )
    return state, (theirs_tok, theirs_grad), beside


def add_blocks(blocks, tok_rows, split):
    width = blocks[0][0][0].shape[1]
    operands = [x for terms in blocks for x in terms]
    half = tok_rows // 2

    def body(*refs):
        outs, at = refs[len(operands) :], 0
        for i, terms in enumerate(blocks):
            for lower in (0, half):
                total = jnp.zeros((half, width), f32)
                for j, (_, _, rows, first) in enumerate(terms):
                    if first <= lower < first + rows:
                        total += refs[at + j][lower - first : lower - first + half, :].astype(f32)
                if split:
                    outs[1 if lower else 0][...] = total.astype(bf16)
                else:
                    outs[i][lower : lower + half, :] = total.astype(bf16)
            at += len(terms)

    height, count = (half, 2) if split else (tok_rows, len(blocks))
    out = pl.pallas_call(
        body,
        out_shape=[jax.ShapeDtypeStruct((height, width), bf16)] * count,
        grid=(1,),
        in_specs=[
            pl.BlockSpec((rows, width), lambda i, at=at: (at, 0)) for _, at, rows, _ in operands
        ],
        out_specs=[pl.BlockSpec((height, width), lambda i: (0, 0))] * count,
        compiler_params=pltpu.CompilerParams(vmem_limit_bytes=KERNEL_VMEM),
        cost_estimate=LIGHT,
        name="add_blocks",
    )(*[x for x, _, _, _ in operands])
    return list(out)


def sum_back(ring, theirs, mine, tok_rows, fills):
    terms = {}
    j = 0
    for piece, own in zip(theirs, mine):
        piece = ring.other_core(piece)
        for at in range(piece.shape[0] // tok_rows):
            terms[ring.names[j]] = [(own, at, tok_rows, 0), (piece, at, tok_rows, 0)]
            j += 1

    half = tok_rows // 2
    top, low = add_blocks([terms[ring.far]], tok_rows, True)
    ahead, behind = (ring.ahead(top), 0, half, 0), (ring.behind(low), 0, half, half)
    mark, filled = (ahead[0], behind[0]), []
    for d in range(ring.far - 1, 0, -1):
        ahead, behind = add_blocks([terms[-d] + [ahead], terms[d] + [behind]], tok_rows, False)
        ahead, behind = ring.ahead(ahead), ring.behind(behind)
        if len(filled) < len(fills):
            done = fills[len(filled)](mark)
            ahead, behind, done = lax.optimization_barrier((ahead, behind, done))
            filled.append(done)
        mark = (ahead, behind)
        ahead, behind = (ahead, 0, tok_rows, 0), (behind, 0, tok_rows, 0)
    for fill in fills[len(filled) :]:
        filled.append(fill(mark))
    return add_blocks([terms[0] + [ahead, behind]], tok_rows, False)[0], filled


def blocks_per_step(n_blocks, cap):
    return max(b for b in range(1, n_blocks + 1) if n_blocks % b == 0 and b * cap <= 768)


def chunk_grads(order, cols, rows, routed, gate, up_mat, down_mat, start, piece):
    n_slots, width = rows.shape
    n_peers, cap, w = gate.shape
    n = blocks_per_step(n_peers, cap)
    r = n * cap
    n_rows, n_cols = n_slots // r, cols.shape[0]

    def body(order_ref, cols_ref, rows_ref, routed_ref, up_ref, down_ref, col_ref, *refs):
        gate_refs, (hidden_ref, both_ref, part_ref, held) = refs[:n], refs[n:]
        step = pl.program_id(0)

        @pl.when(step < n_rows)
        def _():
            up_all = jnp.dot(rows_ref[...], up_ref[...], preferred_element_type=f32)
            grad_all = dot(routed_ref[...], down_ref[...], ((1,), (1,)))
            for b in range(n):
                at = slice(b * cap, (b + 1) * cap)
                up_act, hidden_grad = up_all[at], grad_all[at]
                gate_val = gate_refs[b][0].astype(f32)
                gate_sig = jax.nn.sigmoid(gate_val)
                gate_act = gate_val * gate_sig
                hidden_ref[at, :] = (gate_act * up_act).astype(bf16)
                both_ref[at, w:] = (hidden_grad * gate_act).astype(bf16)
                both_ref[at, :w] = (
                    hidden_grad * up_act * gate_sig * (1.0 + gate_val * (1.0 - gate_sig))
                ).astype(bf16)
            held[pl.ds(pl.multiple_of(step * r, r), r), :] = both_ref[...]

        @pl.when(step >= n_rows)
        def _():
            part_ref[...] = dot(col_ref[...], held[...], ((0,), (0,))).astype(bf16)

    def row(i):
        return jnp.minimum(i, n_rows - 1)

    def col(i):
        return jnp.maximum(i - n_rows, 0)

    return pl.pallas_call(
        body,
        out_shape=(
            jax.ShapeDtypeStruct((n_slots, w), bf16),
            jax.ShapeDtypeStruct((n_slots, 2 * w), bf16),
            jax.ShapeDtypeStruct((n_cols * piece, 2 * w), bf16),
        ),
        grid_spec=pltpu.PrefetchScalarGridSpec(
            num_scalar_prefetch=2,
            grid=(n_rows + n_cols,),
            in_specs=[
                pl.BlockSpec((r, width), lambda i, order, cols: (row(i), 0)),
                pl.BlockSpec((r, width), lambda i, order, cols: (row(i), 0)),
                pl.BlockSpec((pl.Element(width), pl.Element(w)), lambda i, order, cols: (0, start)),
                pl.BlockSpec((pl.Element(w), pl.Element(width)), lambda i, order, cols: (start, 0)),
                pl.BlockSpec((n_slots, piece), lambda i, order, cols: (0, cols[col(i)])),
            ]
            + [
                pl.BlockSpec((1, cap, w), lambda i, order, cols, b=b: (order[n * row(i) + b], 0, 0))
                for b in range(n)
            ],
            out_specs=(
                pl.BlockSpec((r, w), lambda i, order, cols: (row(i), 0)),
                pl.BlockSpec((r, 2 * w), lambda i, order, cols: (row(i), 0)),
                pl.BlockSpec((piece, 2 * w), lambda i, order, cols: (col(i), 0)),
            ),
            scratch_shapes=[pltpu.VMEM((n_slots, 2 * w), bf16)],
        ),
        compiler_params=pltpu.CompilerParams(vmem_limit_bytes=KERNEL_VMEM),
        cost_estimate=LIGHT,
        name="chunk_grads",
    )(order, cols, rows, routed, up_mat, down_mat, rows, *[gate] * n)


def own_half(cols, rows, both, piece):
    n_slots = rows.shape[0]
    w = both.shape[1]

    def body(cols_ref, rows_ref, both_ref, own_ref):
        own_ref[...] = dot(rows_ref[...], both_ref[...], ((0,), (0,))).astype(bf16)

    return pl.pallas_call(
        body,
        out_shape=jax.ShapeDtypeStruct((piece, w), bf16),
        grid_spec=pltpu.PrefetchScalarGridSpec(
            num_scalar_prefetch=1,
            grid=(1,),
            in_specs=[
                pl.BlockSpec((n_slots, piece), lambda i, cols: (0, cols[0])),
                pl.BlockSpec((n_slots, w), lambda i, cols: (0, 0)),
            ],
            out_specs=pl.BlockSpec((piece, w), lambda i, cols: (0, 0)),
        ),
        compiler_params=pltpu.CompilerParams(vmem_limit_bytes=KERNEL_VMEM),
        cost_estimate=LIGHT,
        name="own_half",
    )(cols, rows, both)


def down_rows(routed, hidden, start, total, hidden_width):
    n_slots, width = routed.shape
    w = hidden.shape[1]
    span = min(1024, width)

    def body(routed_ref, hidden_ref, *refs):
        down_ref, turned = refs[-2:]

        @pl.when(pl.program_id(0) == 0)
        def _():
            turned[...] = hidden_ref[...].T

        down_ref[...] = jnp.dot(turned[...], routed_ref[...], preferred_element_type=f32).astype(bf16)

    aliased = [] if total is None else [total]
    return pl.pallas_call(
        body,
        out_shape=jax.ShapeDtypeStruct((hidden_width, width), bf16),
        grid=(width // span,),
        in_specs=[
            pl.BlockSpec((n_slots, span), lambda i: (0, i)),
            pl.BlockSpec((n_slots, w), lambda i: (0, 0)),
        ]
        + [pl.BlockSpec(memory_space=pl.ANY) for _ in aliased],
        out_specs=pl.BlockSpec((pl.Element(w), pl.Element(span)), lambda i: (start, i * span)),
        scratch_shapes=[pltpu.VMEM((w, n_slots), bf16)],
        input_output_aliases={2: 0} if aliased else {},
        compiler_params=pltpu.CompilerParams(vmem_limit_bytes=KERNEL_VMEM),
        cost_estimate=LIGHT,
        name="down_rows",
    )(routed, hidden, *aliased)


def join_halves(own, arrived, start, totals, hidden_width):
    piece, both_width = own.shape
    w = both_width // 2
    r = min(256, piece)
    n_in = 1 + len(arrived)

    def body(*refs):
        gate_ref, up_ref = refs[-2:]
        for at, out_ref in ((slice(0, w), gate_ref), (slice(w, 2 * w), up_ref)):
            total = refs[0][:, at].astype(f32)
            for x in refs[1:n_in]:
                total = total + x[:, at].astype(f32)
            out_ref[...] = (grad_scale * total).astype(bf16)

    aliased = [] if totals is None else list(totals)
    shape = jax.ShapeDtypeStruct((piece, hidden_width), bf16)
    out_spec = pl.BlockSpec((pl.Element(r), pl.Element(w)), lambda i: (i * r, start))
    return pl.pallas_call(
        body,
        out_shape=(shape, shape),
        grid=(piece // r,),
        in_specs=[pl.BlockSpec((r, both_width), lambda i: (i, 0))] * n_in
        + [pl.BlockSpec(memory_space=pl.ANY) for _ in aliased],
        out_specs=(out_spec, out_spec),
        input_output_aliases={n_in: 0, n_in + 1: 1} if aliased else {},
        compiler_params=pltpu.CompilerParams(vmem_limit_bytes=KERNEL_VMEM),
        cost_estimate=LIGHT,
        name="join_halves",
    )(own, *arrived, *aliased)


def spread_back(parts, starts, gate_mat, up_mat, table, tok_rows, first, heights):
    n_peers, _, cap = table.shape
    half = n_peers // 2
    width, hidden_width = gate_mat.shape
    cols = min(512, width)
    rows = half * cap
    shift = 0 if first else 1
    owner = [(i, b) for i, height in enumerate(heights) for b in range(height)]

    def body(*refs):
        part_refs = refs[: len(parts)]
        gate_ref, up_ref, table_ref = refs[len(parts) : len(parts) + 3]
        out_refs = refs[len(parts) + 3 :]
        total = jnp.zeros((rows, cols), f32)
        for start, part_ref in zip(starts, part_refs):
            w = part_ref.shape[1] // 2
            total += dot(part_ref[:, :w], gate_ref[:, start : start + w], ((1,), (1,)))
            total += dot(part_ref[:, w:], up_ref[:, start : start + w], ((1,), (1,)))
        terms = total.astype(bf16)
        for j, (i, b) in enumerate(owner):
            tok = table_ref[j, 0:1, :]
            place = (lax.broadcasted_iota(i32, (tok_rows, cap), 0).astype(f32) == tok).astype(bf16)
            spread = jnp.dot(place, terms[j * cap : (j + 1) * cap], preferred_element_type=f32)
            out_refs[i][b * tok_rows : (b + 1) * tok_rows, :] = spread.astype(bf16)

    return pl.pallas_call(
        body,
        out_shape=[jax.ShapeDtypeStruct((h * tok_rows, width), bf16) for h in heights],
        grid=(width // cols,),
        in_specs=[pl.BlockSpec((rows, x.shape[1]), lambda j: (shift, 0)) for x in parts]
        + [
            pl.BlockSpec((cols, hidden_width), lambda j: (j, 0)),
            pl.BlockSpec((cols, hidden_width), lambda j: (j, 0)),
            pl.BlockSpec((half, 2, cap), lambda j: (shift, 0, 0)),
        ],
        out_specs=[pl.BlockSpec((h * tok_rows, cols), lambda j: (0, j)) for h in heights],
        compiler_params=pltpu.CompilerParams(vmem_limit_bytes=KERNEL_VMEM),
        cost_estimate=LIGHT,
        name="spread_back",
    )(*parts, gate_mat, up_mat, table)


def local(tokens, out_grad, gate_saved, probs, expert_ids, w_gate, w_up, w_down):
    n_peers = lax.axis_size("expert")
    n_dp = lax.axis_size("dp")
    group = lax.axis_index("dp")
    tok_rows, model_width = tokens.shape
    top_k = expert_ids.shape[1]
    hidden_width = w_up.shape[2]
    cap = min(tok_rows, 2 * tok_rows * top_k // n_peers)
    n_routes = tok_rows * top_k
    n_slots = n_peers * cap
    gate_mat, up_mat, down_mat = w_gate[0], w_up[0], w_down[0]

    experts = jnp.arange(n_peers, dtype=i32)
    hit = expert_ids[:, :, None] == experts[None, None, :]
    named = jnp.any(hit, axis=1)
    weight = jnp.sum(jnp.where(hit, probs[:, :, None], 0.0), axis=1)
    rank = jnp.cumsum(named.astype(i32), axis=0) - 1
    slots = jnp.arange(cap, dtype=i32)
    in_slot = named[:, :, None] & (rank[:, :, None] == slots[None, None, :])
    tok_of = jnp.sum(
        jnp.where(in_slot, jnp.arange(1, tok_rows + 1, dtype=f32)[:, None, None], 0.0), axis=0
    ) - 1.0
    choice = jnp.sum(jnp.where(hit, jnp.arange(top_k, dtype=f32)[None, :, None], 0.0), axis=1)
    choice_of = jnp.sum(jnp.where(in_slot, choice[:, :, None], 0.0), axis=0)
    weight_of = jnp.sum(jnp.where(in_slot, weight[:, :, None], 0.0), axis=0)
    table = lax.all_to_all(
        jnp.concatenate([tok_of, weight_of], axis=1),
        "expert",
        split_axis=0,
        concat_axis=0,
        tiled=True,
    )
    ring = Ring()
    table = table.reshape(n_peers, 2, cap)[ring.order]
    widths = chunk_widths(hidden_width)
    starts = [sum(widths[:i]) for i in range(len(widths))]
    route_gates = jnp.transpose(gate_saved, (1, 0, 2)).reshape(n_routes, hidden_width)
    route_of = (tok_of + tok_rows * choice_of).astype(i32).reshape(n_slots, 1)
    pick = (route_of == jnp.arange(n_routes, dtype=i32)[None, :]).astype(bf16)
    send_gate = [
        dot(pick, route_gates[:, s : s + w], ((1,), (0,))).astype(bf16).reshape(n_peers, cap, w)
        for s, w in zip(starts, widths)
    ]
    (rows_in, routed), mark, (send_gate[1:],) = gather_rows(
        ring, tokens, out_grad, table.transpose(0, 2, 1), cap, [send_gate[1:]]
    )

    def send_chunk(i, mark):
        part = send_gate[i]
        if mark is not None:
            part, _ = lax.optimization_barrier((part, mark))
        return lax.all_to_all(part, "expert", split_axis=0, concat_axis=0, tiled=True)

    recv_gate = [send_chunk(i, m) for i, m in zip(range(len(widths)), (None, mark))]

    piece = model_width // n_dp
    shifts = [[(i, (i + d) % n_dp) for i in range(n_dp)] for d in range(n_dp)]

    peer_cols = lax.rem(group + jnp.arange(1, n_dp, dtype=i32), n_dp)
    own_cols = group.reshape(1).astype(i32)
    both_parts, hidden_parts, arrivals = [], [], []
    own_parts, sum_down = [], None
    early = len(widths) - 1
    rows_now, routed_now = rows_in, routed
    for c, w in enumerate(widths):
        hidden, both, sent = chunk_grads(
            ring.order,
            peer_cols,
            rows_now,
            routed_now,
            recv_gate[c],
            up_mat,
            down_mat,
            starts[c],
            piece,
        )
        both_parts.append(both)
        hidden_parts.append(hidden)
        arrivals.append(
            [
                lax.ppermute(sent[(d - 1) * piece : d * piece], "dp", shifts[d])
                for d in range(1, n_dp)
            ]
        )
        if c + 2 < len(widths):
            recv_gate.append(send_chunk(c + 2, sent))
        if c < early:
            own_parts.append(own_half(own_cols, rows_now, both, piece))
            sum_down = down_rows(routed_now, hidden, starts[c], sum_down, hidden_width)
            if c >= 1:
                rows_now, arrivals[c - 1] = lax.optimization_barrier((rows_now, arrivals[c - 1]))
            rows_now, routed_now, own_parts[c], sum_down = lax.optimization_barrier(
                (rows_now, routed_now, own_parts[c], sum_down)
            )

    heights = [1] + [2] * (ring.far - 1) + [1]
    theirs = spread_back(both_parts, starts, gate_mat, up_mat, table, tok_rows, True, heights)
    late = list(range(early, len(widths)))
    for c in late:
        hidden, _ = lax.optimization_barrier((hidden_parts[c], theirs))
        sum_down = down_rows(routed_now, hidden, starts[c], sum_down, hidden_width)
    low = hidden_width // n_dp
    sent = [
        lax.dynamic_slice_in_dim(sum_down, lax.rem(group + d, n_dp) * low, low, 0)
        for d in range(1, n_dp)
    ]
    last, arrivals[:-1], sent = lax.optimization_barrier((both_parts[-1], arrivals[:-1], sent))
    arrived = [lax.ppermute(part, "dp", shifts[d]) for d, part in enumerate(sent, 1)]
    mine = spread_back(
        both_parts[:-1] + [last], starts, gate_mat, up_mat, table, tok_rows, False, heights
    )
    mine, arrivals[-1] = lax.optimization_barrier((mine, arrivals[-1]))

    def late_halves(mark):
        parts, _ = lax.optimization_barrier((both_parts, mark))
        return [own_half(own_cols, rows_now, parts[c], piece) for c in late]

    def join_early(mark):
        parts, _ = lax.optimization_barrier((own_parts, mark))
        joined = None
        for c, part in enumerate(parts):
            joined = join_halves(part, arrivals[c], starts[c], joined, hidden_width)
        return joined

    input_grad, (late_parts, totals) = sum_back(
        ring, theirs, mine, tok_rows, [late_halves, join_early]
    )
    arrived, _ = lax.optimization_barrier((arrived, input_grad))
    for c, part in zip(late, late_parts):
        totals = join_halves(part, arrivals[c], starts[c], totals, hidden_width)
    grad_gate, grad_up = totals
    down = lax.dynamic_slice_in_dim(sum_down, group * low, low, 0).astype(f32)
    for part in arrived:
        down = down + part.astype(f32)
    grad_down = (grad_scale * down).astype(bf16)[None]
    return (input_grad, grad_gate[None], grad_up[None], grad_down)


def solution(mesh):
    return jax.shard_map(
        local,
        mesh=mesh,
        in_specs=(
            P(("dp", "expert"), None),
            P(("dp", "expert"), None),
            P(("dp", "expert"), None, None),
            P(("dp", "expert"), None),
            P(("dp", "expert"), None),
            P("expert", None, None),
            P("expert", None, None),
            P("expert", None, None),
        ),
        out_specs=(
            P(("dp", "expert"), None),
            P("expert", "dp", None),
            P("expert", "dp", None),
            P("expert", "dp", None),
        ),
        check_vma=False,
    )
```

```python
import jax
import jax.numpy as jnp
import numpy as np
from jax import lax
from jax.experimental import pallas as pl
from jax.experimental.pallas import tpu as pltpu
from jax.sharding import PartitionSpec as P

grad_scale = 0.0625
f32 = jnp.float32
bf16 = jnp.bfloat16
i32 = jnp.int32
KERNEL_VMEM = 60 * 1024 * 1024
LIGHT = pl.CostEstimate(flops=1000, bytes_accessed=1000, transcendentals=0)


def dot(a, b, dims):
    return lax.dot_general(a, b, (dims, ((), ())), preferred_element_type=f32)


def chunk_widths(width):
    lanes = width // 128
    shares = (3, 7, 11)
    ends = [-(-lanes * x // 11) * 128 for x in shares]
    return [e - s for s, e in zip([0] + ends, ends) if e > s]


def chip_cycle(n_chips):
    cols = n_chips // 4
    if n_chips % 4 or cols < 2:
        return list(range(n_chips))
    walk = [(row, 0) for row in range(4)]
    for step, row in enumerate((3, 2, 1, 0)):
        across = range(1, cols) if step % 2 == 0 else range(cols - 1, 0, -1)
        walk += [(row, col) for col in across]
    return [row * cols + col for row, col in walk]


def put_rows(order, table, shards, rows, routed, cap):
    count = len(shards)
    n_peers, _, _ = table.shape
    width = shards[0][0].shape[1]

    def body(order_ref, table_ref, *refs):
        parts = refs[: 2 * count]
        rows_ref, routed_ref = refs[-2:]
        step = pl.program_id(0)
        for i in range(count):

            @pl.when(step == i)
            def _():
                info = table_ref[0]
                place = (
                    lax.broadcasted_iota(i32, (cap, tok_rows_of), 1).astype(f32) == info[:, 0:1]
                ).astype(bf16)
                rows_ref[...] = jnp.dot(
                    place, parts[2 * i][...], preferred_element_type=f32
                ).astype(bf16)
                picked = jnp.dot(place, parts[2 * i + 1][...], preferred_element_type=f32)
                routed_ref[...] = (info[:, 1:2] * picked).astype(bf16)

    tok_rows_of = shards[0][2]
    in_specs = [pl.BlockSpec((1, cap, 2), lambda i, order: (order[i], 0, 0))]
    operands = [table]
    for tok, grad, height, tok_at, grad_at in shards:
        in_specs.append(pl.BlockSpec((height, width), lambda i, order, a=tok_at: (a, 0)))
        in_specs.append(pl.BlockSpec((height, width), lambda i, order, a=grad_at: (a, 0)))
        operands += [tok, grad]
    aliases = {}
    if rows is not None:
        aliases = {1 + len(operands): 0, 2 + len(operands): 1}
        in_specs += [pl.BlockSpec(memory_space=pl.ANY)] * 2
        operands += [rows, routed]
    n_slots = n_peers * cap
    shape = jax.ShapeDtypeStruct((n_slots, width), bf16)
    out_spec = pl.BlockSpec((cap, width), lambda i, order: (order[i], 0))
    return pl.pallas_call(
        body,
        out_shape=(shape, shape),
        grid_spec=pltpu.PrefetchScalarGridSpec(
            num_scalar_prefetch=1,
            grid=(count,),
            in_specs=in_specs,
            out_specs=(out_spec, out_spec),
        ),
        input_output_aliases=aliases,
        compiler_params=pltpu.CompilerParams(vmem_limit_bytes=KERNEL_VMEM),
        cost_estimate=pl.CostEstimate(
            flops=4 * count * cap * tok_rows_of * width,
            bytes_accessed=4 * count * (tok_rows_of + cap) * width,
            transcendentals=0,
        ),
        name="put_rows",
    )(order, *operands)


class Ring:
    def __init__(self):
        self.n_peers = lax.axis_size("expert")
        self.n = self.n_peers // 2
        self.far = self.n // 2
        self.names = [self.far]
        for d in range(self.far - 1, 0, -1):
            self.names += [d, -d]
        self.names.append(0)
        cycle = chip_cycle(self.n)
        spot = [cycle.index(c) for c in range(self.n)]
        chips = range(self.n)
        self.fwd = [(2 * cycle[i] + c, 2 * cycle[(i + 1) % self.n] + c) for i in chips for c in (0, 1)]
        self.bwd = [(b, a) for a, b in self.fwd]
        self.swap = [(i, i ^ 1) for i in range(self.n_peers)]
        table = np.zeros((self.n_peers, self.n_peers), np.int32)
        for e in range(self.n_peers):
            for core in (0, 1):
                for j, d in enumerate(self.names):
                    chip = cycle[(spot[e // 2] - d) % self.n]
                    table[e, core * self.n + j] = 2 * chip + (e % 2 if core else 1 - e % 2)
        self.order = jnp.asarray(table)[lax.axis_index("expert")]

    def at(self, distance, other):
        return self.names.index(distance) + (0 if other else self.n)

    def ahead(self, x):
        return lax.ppermute(x, "expert", self.fwd)

    def behind(self, x):
        return lax.ppermute(x, "expert", self.bwd)

    def other_core(self, x):
        return lax.ppermute(x, "expert", self.swap)


def gather_rows(ring, tokens, out_grad, table, cap, beside):
    tok_rows = tokens.shape[0]
    beside = list(beside)
    own = jnp.concatenate([tokens, out_grad], axis=0)

    def whole(x):
        return (x, x, tok_rows, 0, 1)

    def place(spots, shards, state):
        return put_rows(np.array(spots, np.int32), table, shards, *state, cap)

    state = (None, None)
    ahead, behind = own, own
    pending = [([ring.at(0, False), ring.at(0, True)], [whole(own), whole(ring.other_core(own))])]
    for d in range(1, ring.far):
        ahead, behind = ring.ahead(ahead), ring.behind(behind)
        if d >= 2:
            now, pending = pending[:1], pending[1:]
            for spots, shards in now:
                state = place(spots, shards, state)
            ahead, behind, state = lax.optimization_barrier((ahead, behind, state))
            if d - 2 < len(beside):
                ahead, behind, beside[d - 2] = lax.optimization_barrier(
                    (ahead, behind, beside[d - 2])
                )
        pending.append(
            (
                [ring.at(d, False), ring.at(-d, False), ring.at(d, True), ring.at(-d, True)],
                [whole(x) for x in (ahead, behind, ring.other_core(ahead), ring.other_core(behind))],
            )
        )
    mark = (ahead, behind)
    far_tok = ring.ahead(ahead[:tok_rows])
    far_grad = ring.behind(behind[tok_rows:])
    for spots, shards in pending:
        state = place(spots, shards, state)
    far_tok, far_grad, state = lax.optimization_barrier((far_tok, far_grad, state))
    theirs_tok, theirs_grad = ring.other_core(far_tok), ring.other_core(far_grad)
    state = place(
        [ring.at(ring.far, False), ring.at(ring.far, True)],
        [(far_tok, far_grad, tok_rows, 0, 0), (theirs_tok, theirs_grad, tok_rows, 0, 0)],
        state,
    )
    return state, mark, beside


def add_blocks(blocks, tok_rows, split, cols):
    operands = [x for terms in blocks for x in terms]
    half = tok_rows // 2

    def body(*refs):
        outs, at = refs[len(operands) :], 0
        for i, terms in enumerate(blocks):
            for lower in (0, half):
                total = jnp.zeros((half, cols), f32)
                for j, (_, _, rows, first, _) in enumerate(terms):
                    if first <= lower < first + rows:
                        total += refs[at + j][lower - first : lower - first + half, :].astype(f32)
                if split:
                    outs[1 if lower else 0][...] = total.astype(bf16)
                else:
                    outs[i][lower : lower + half, :] = total.astype(bf16)
            at += len(terms)

    height, count = (half, 2) if split else (tok_rows, len(blocks))
    out = pl.pallas_call(
        body,
        out_shape=[jax.ShapeDtypeStruct((height, cols), bf16)] * count,
        grid=(1,),
        in_specs=[
            pl.BlockSpec((rows, cols), lambda i, at=at, col=col: (at, col))
            for _, at, rows, _, col in operands
        ],
        out_specs=[pl.BlockSpec((height, cols), lambda i: (0, 0))] * count,
        compiler_params=pltpu.CompilerParams(vmem_limit_bytes=KERNEL_VMEM),
        cost_estimate=LIGHT,
        name="add_blocks",
    )(*[x[0] for x in operands])
    return list(out)


def sum_back(ring, handed, mine, tok_rows, fills):
    width = mine[0].shape[1]
    cols, half = width // 2, tok_rows // 2
    terms = [{}, {}]
    j = 0
    for piece, own in zip(handed, mine):
        for at in range(piece.shape[0] // tok_rows):
            for h in (0, 1):
                terms[h][ring.names[j]] = [(x, at, tok_rows, 0, h) for x in (own, piece)]
            j += 1

    moving = []
    for h in (0, 1):
        top, low = add_blocks([terms[h][ring.far]], tok_rows, True, cols)
        moving.append([(ring.ahead(top), 0, half, 0, 0), (ring.behind(low), 0, half, half, 0)])
    mark, filled = moving[0][0][0], []
    for d in range(ring.far - 1, 0, -1):
        for h in (0, 1):
            ahead, behind = add_blocks(
                [terms[h][-d] + moving[h][:1], terms[h][d] + moving[h][1:]], tok_rows, False, cols
            )
            ahead, behind = ring.ahead(ahead), ring.behind(behind)
            if h == 0 and len(filled) < len(fills):
                done = fills[len(filled)](mark)
                ahead, behind, done = lax.optimization_barrier((ahead, behind, done))
                filled.append(done)
            moving[h] = [(ahead, 0, tok_rows, 0, 0), (behind, 0, tok_rows, 0, 0)]
        mark = moving[0][0][0]
    for fill in fills[len(filled) :]:
        filled.append(fill(mark))
    done = [add_blocks([terms[h][0] + moving[h]], tok_rows, False, cols)[0] for h in (0, 1)]
    return jnp.concatenate(done, axis=1), filled


def join_down(group, total, arrived):
    low, width = arrived[0].shape
    r = low // 4 if low % 64 == 0 else low
    steps = low // r

    def body(group_ref, *refs):
        out = refs[0][...].astype(f32)
        for x in refs[1:-1]:
            out = out + x[...].astype(f32)
        refs[-1][...] = (grad_scale * out).astype(bf16)

    return pl.pallas_call(
        body,
        out_shape=jax.ShapeDtypeStruct((low, width), bf16),
        grid_spec=pltpu.PrefetchScalarGridSpec(
            num_scalar_prefetch=1,
            grid=(steps,),
            in_specs=[pl.BlockSpec((r, width), lambda i, group: (group[0] * steps + i, 0))]
            + [pl.BlockSpec((r, width), lambda i, group: (i, 0))] * len(arrived),
            out_specs=pl.BlockSpec((r, width), lambda i, group: (i, 0)),
        ),
        compiler_params=pltpu.CompilerParams(vmem_limit_bytes=KERNEL_VMEM),
        cost_estimate=LIGHT,
        name="join_down",
    )(group, total, *arrived)


def blocks_per_step(n_blocks, cap):
    return max(b for b in range(1, n_blocks + 1) if n_blocks % b == 0 and b * cap <= 768)


def chunk_grads(order, cols, rows, routed, gate, up_mat, down_mat, start, piece):
    n_slots, width = rows.shape
    n_peers, cap, w = gate.shape
    n = blocks_per_step(n_peers, cap)
    r = n * cap
    n_rows, n_cols = n_slots // r, cols.shape[0]

    def body(order_ref, cols_ref, rows_ref, routed_ref, up_ref, down_ref, col_ref, *refs):
        gate_refs, (hidden_ref, both_ref, part_ref, held) = refs[:n], refs[n:]
        step = pl.program_id(0)

        @pl.when(step < n_rows)
        def _():
            up_all = jnp.dot(rows_ref[...], up_ref[...], preferred_element_type=f32)
            grad_all = dot(routed_ref[...], down_ref[...], ((1,), (1,)))
            for b in range(n):
                at = slice(b * cap, (b + 1) * cap)
                up_act, hidden_grad = up_all[at], grad_all[at]
                gate_val = gate_refs[b][0].astype(f32)
                gate_sig = jax.nn.sigmoid(gate_val)
                gate_act = gate_val * gate_sig
                hidden_ref[at, :] = (gate_act * up_act).astype(bf16)
                both_ref[at, w:] = (hidden_grad * gate_act).astype(bf16)
                both_ref[at, :w] = (
                    hidden_grad * up_act * gate_sig * (1.0 + gate_val * (1.0 - gate_sig))
                ).astype(bf16)
            held[pl.ds(pl.multiple_of(step * r, r), r), :] = both_ref[...]

        @pl.when(step >= n_rows)
        def _():
            part_ref[...] = dot(col_ref[...], held[...], ((0,), (0,))).astype(bf16)

    def row(i):
        return jnp.minimum(i, n_rows - 1)

    def col(i):
        return jnp.maximum(i - n_rows, 0)

    return pl.pallas_call(
        body,
        out_shape=(
            jax.ShapeDtypeStruct((n_slots, w), bf16),
            jax.ShapeDtypeStruct((n_slots, 2 * w), bf16),
            jax.ShapeDtypeStruct((n_cols * piece, 2 * w), bf16),
        ),
        grid_spec=pltpu.PrefetchScalarGridSpec(
            num_scalar_prefetch=2,
            grid=(n_rows + n_cols,),
            in_specs=[
                pl.BlockSpec((r, width), lambda i, order, cols: (row(i), 0)),
                pl.BlockSpec((r, width), lambda i, order, cols: (row(i), 0)),
                pl.BlockSpec((pl.Element(width), pl.Element(w)), lambda i, order, cols: (0, start)),
                pl.BlockSpec((pl.Element(w), pl.Element(width)), lambda i, order, cols: (start, 0)),
                pl.BlockSpec((n_slots, piece), lambda i, order, cols: (0, cols[col(i)])),
            ]
            + [
                pl.BlockSpec((1, cap, w), lambda i, order, cols, b=b: (order[n * row(i) + b], 0, 0))
                for b in range(n)
            ],
            out_specs=(
                pl.BlockSpec((r, w), lambda i, order, cols: (row(i), 0)),
                pl.BlockSpec((r, 2 * w), lambda i, order, cols: (row(i), 0)),
                pl.BlockSpec((piece, 2 * w), lambda i, order, cols: (col(i), 0)),
            ),
            scratch_shapes=[pltpu.VMEM((n_slots, 2 * w), bf16)],
        ),
        compiler_params=pltpu.CompilerParams(vmem_limit_bytes=KERNEL_VMEM),
        cost_estimate=LIGHT,
        name="chunk_grads",
    )(order, cols, rows, routed, up_mat, down_mat, rows, *[gate] * n)


def own_half(cols, rows, both, piece):
    n_slots = rows.shape[0]
    w = both.shape[1]

    def body(cols_ref, rows_ref, both_ref, own_ref):
        own_ref[...] = dot(rows_ref[...], both_ref[...], ((0,), (0,))).astype(bf16)

    return pl.pallas_call(
        body,
        out_shape=jax.ShapeDtypeStruct((piece, w), bf16),
        grid_spec=pltpu.PrefetchScalarGridSpec(
            num_scalar_prefetch=1,
            grid=(1,),
            in_specs=[
                pl.BlockSpec((n_slots, piece), lambda i, cols: (0, cols[0])),
                pl.BlockSpec((n_slots, w), lambda i, cols: (0, 0)),
            ],
            out_specs=pl.BlockSpec((piece, w), lambda i, cols: (0, 0)),
        ),
        compiler_params=pltpu.CompilerParams(vmem_limit_bytes=KERNEL_VMEM),
        cost_estimate=LIGHT,
        name="own_half",
    )(cols, rows, both)


def down_rows(routed, hidden, start, total, hidden_width):
    n_slots, width = routed.shape
    w = hidden.shape[1]
    span = min(1024, width)

    def body(routed_ref, hidden_ref, *refs):
        down_ref, turned = refs[-2:]

        @pl.when(pl.program_id(0) == 0)
        def _():
            turned[...] = hidden_ref[...].T

        down_ref[...] = jnp.dot(turned[...], routed_ref[...], preferred_element_type=f32).astype(bf16)

    aliased = [] if total is None else [total]
    return pl.pallas_call(
        body,
        out_shape=jax.ShapeDtypeStruct((hidden_width, width), bf16),
        grid=(width // span,),
        in_specs=[
            pl.BlockSpec((n_slots, span), lambda i: (0, i)),
            pl.BlockSpec((n_slots, w), lambda i: (0, 0)),
        ]
        + [pl.BlockSpec(memory_space=pl.ANY) for _ in aliased],
        out_specs=pl.BlockSpec((pl.Element(w), pl.Element(span)), lambda i: (start, i * span)),
        scratch_shapes=[pltpu.VMEM((w, n_slots), bf16)],
        input_output_aliases={2: 0} if aliased else {},
        compiler_params=pltpu.CompilerParams(vmem_limit_bytes=KERNEL_VMEM),
        cost_estimate=LIGHT,
        name="down_rows",
    )(routed, hidden, *aliased)


def join_halves(own, arrived, start, totals, hidden_width):
    piece, both_width = own.shape
    w = both_width // 2
    r = min(256, piece)
    n_in = 1 + len(arrived)

    def body(*refs):
        gate_ref, up_ref = refs[-2:]
        for at, out_ref in ((slice(0, w), gate_ref), (slice(w, 2 * w), up_ref)):
            total = refs[0][:, at].astype(f32)
            for x in refs[1:n_in]:
                total = total + x[:, at].astype(f32)
            out_ref[...] = (grad_scale * total).astype(bf16)

    aliased = [] if totals is None else list(totals)
    shape = jax.ShapeDtypeStruct((piece, hidden_width), bf16)
    out_spec = pl.BlockSpec((pl.Element(r), pl.Element(w)), lambda i: (i * r, start))
    return pl.pallas_call(
        body,
        out_shape=(shape, shape),
        grid=(piece // r,),
        in_specs=[pl.BlockSpec((r, both_width), lambda i: (i, 0))] * n_in
        + [pl.BlockSpec(memory_space=pl.ANY) for _ in aliased],
        out_specs=(out_spec, out_spec),
        input_output_aliases={n_in: 0, n_in + 1: 1} if aliased else {},
        compiler_params=pltpu.CompilerParams(vmem_limit_bytes=KERNEL_VMEM),
        cost_estimate=LIGHT,
        name="join_halves",
    )(own, *arrived, *aliased)


def spread_back(parts, starts, gate_mat, up_mat, table, tok_rows, first, heights):
    n_peers, _, cap = table.shape
    half = n_peers // 2
    width, hidden_width = gate_mat.shape
    cols = min(512, width)
    rows = half * cap
    shift = 0 if first else 1
    owner = [(i, b) for i, height in enumerate(heights) for b in range(height)]

    def body(*refs):
        part_refs = refs[: len(parts)]
        gate_ref, up_ref, table_ref = refs[len(parts) : len(parts) + 3]
        out_refs = refs[len(parts) + 3 :]
        total = jnp.zeros((rows, cols), f32)
        for start, part_ref in zip(starts, part_refs):
            w = part_ref.shape[1] // 2
            total += dot(part_ref[:, :w], gate_ref[:, start : start + w], ((1,), (1,)))
            total += dot(part_ref[:, w:], up_ref[:, start : start + w], ((1,), (1,)))
        terms = total.astype(bf16)
        for j, (i, b) in enumerate(owner):
            tok = table_ref[j, 0:1, :]
            place = (lax.broadcasted_iota(i32, (tok_rows, cap), 0).astype(f32) == tok).astype(bf16)
            spread = jnp.dot(place, terms[j * cap : (j + 1) * cap], preferred_element_type=f32)
            out_refs[i][b * tok_rows : (b + 1) * tok_rows, :] = spread.astype(bf16)

    return pl.pallas_call(
        body,
        out_shape=[jax.ShapeDtypeStruct((h * tok_rows, width), bf16) for h in heights],
        grid=(width // cols,),
        in_specs=[pl.BlockSpec((rows, x.shape[1]), lambda j: (shift, 0)) for x in parts]
        + [
            pl.BlockSpec((cols, hidden_width), lambda j: (j, 0)),
            pl.BlockSpec((cols, hidden_width), lambda j: (j, 0)),
            pl.BlockSpec((half, 2, cap), lambda j: (shift, 0, 0)),
        ],
        out_specs=[pl.BlockSpec((h * tok_rows, cols), lambda j: (0, j)) for h in heights],
        compiler_params=pltpu.CompilerParams(vmem_limit_bytes=KERNEL_VMEM),
        cost_estimate=LIGHT,
        name="spread_back",
    )(*parts, gate_mat, up_mat, table)


def local(tokens, out_grad, gate_saved, probs, expert_ids, w_gate, w_up, w_down):
    n_peers = lax.axis_size("expert")
    n_dp = lax.axis_size("dp")
    group = lax.axis_index("dp")
    tok_rows, model_width = tokens.shape
    top_k = expert_ids.shape[1]
    hidden_width = w_up.shape[2]
    cap = min(tok_rows, 2 * tok_rows * top_k // n_peers)
    n_routes = tok_rows * top_k
    n_slots = n_peers * cap
    gate_mat, up_mat, down_mat = w_gate[0], w_up[0], w_down[0]

    experts = jnp.arange(n_peers, dtype=i32)
    hit = expert_ids[:, :, None] == experts[None, None, :]
    named = jnp.any(hit, axis=1)
    weight = jnp.sum(jnp.where(hit, probs[:, :, None], 0.0), axis=1)
    rank = jnp.cumsum(named.astype(i32), axis=0) - 1
    slots = jnp.arange(cap, dtype=i32)
    in_slot = named[:, :, None] & (rank[:, :, None] == slots[None, None, :])
    tok_of = jnp.sum(
        jnp.where(in_slot, jnp.arange(1, tok_rows + 1, dtype=f32)[:, None, None], 0.0), axis=0
    ) - 1.0
    choice = jnp.sum(jnp.where(hit, jnp.arange(top_k, dtype=f32)[None, :, None], 0.0), axis=1)
    choice_of = jnp.sum(jnp.where(in_slot, choice[:, :, None], 0.0), axis=0)
    weight_of = jnp.sum(jnp.where(in_slot, weight[:, :, None], 0.0), axis=0)
    table = lax.all_to_all(
        jnp.concatenate([tok_of, weight_of], axis=1),
        "expert",
        split_axis=0,
        concat_axis=0,
        tiled=True,
    )
    ring = Ring()
    table = table.reshape(n_peers, 2, cap)[ring.order]
    widths = chunk_widths(hidden_width)
    starts = [sum(widths[:i]) for i in range(len(widths))]
    route_gates = jnp.transpose(gate_saved, (1, 0, 2)).reshape(n_routes, hidden_width)
    route_of = (tok_of + tok_rows * choice_of).astype(i32).reshape(n_slots, 1)
    pick = (route_of == jnp.arange(n_routes, dtype=i32)[None, :]).astype(bf16)
    send_gate = [
        dot(pick, route_gates[:, s : s + w], ((1,), (0,))).astype(bf16).reshape(n_peers, cap, w)
        for s, w in zip(starts, widths)
    ]
    (rows_in, routed), mark, (send_gate[1:],) = gather_rows(
        ring, tokens, out_grad, table.transpose(0, 2, 1), cap, [send_gate[1:]]
    )

    def send_chunk(i, mark):
        part = send_gate[i]
        if mark is not None:
            part, _ = lax.optimization_barrier((part, mark))
        return lax.all_to_all(part, "expert", split_axis=0, concat_axis=0, tiled=True)

    recv_gate = [send_chunk(i, m) for i, m in zip(range(len(widths)), (None, mark))]

    piece = model_width // n_dp
    shifts = [[(i, (i + d) % n_dp) for i in range(n_dp)] for d in range(n_dp)]

    peer_cols = lax.rem(group + jnp.arange(1, n_dp, dtype=i32), n_dp)
    own_cols = group.reshape(1).astype(i32)
    both_parts, hidden_parts, arrivals, own_parts = [], [], [], []
    rows_now, routed_now = rows_in, routed
    for c, w in enumerate(widths):
        if c >= 2:
            own = own_half(own_cols, rows_now, both_parts[c - 2], piece)
            own_parts.append(own)
            rows_now, own_parts[-1], arrivals[c - 2] = lax.optimization_barrier(
                (rows_now, own, arrivals[c - 2])
            )
        hidden, both, sent = chunk_grads(
            ring.order,
            peer_cols,
            rows_now,
            routed_now,
            recv_gate[c],
            up_mat,
            down_mat,
            starts[c],
            piece,
        )
        both_parts.append(both)
        hidden_parts.append(hidden)
        arrivals.append(
            [
                lax.ppermute(sent[(d - 1) * piece : d * piece], "dp", shifts[d])
                for d in range(1, n_dp)
            ]
        )
        rows_now, routed_now, _ = lax.optimization_barrier((rows_now, routed_now, sent))
        if c + 2 < len(widths):
            recv_gate.append(send_chunk(c + 2, sent))

    heights = [1] + [2] * (ring.far - 1) + [1]
    theirs = spread_back(both_parts, starts, gate_mat, up_mat, table, tok_rows, True, heights)
    handed = [ring.other_core(x) for x in theirs]
    sum_down = None
    for c, hidden in enumerate(hidden_parts):
        hidden, _ = lax.optimization_barrier((hidden, theirs))
        sum_down = down_rows(routed_now, hidden, starts[c], sum_down, hidden_width)
    low = hidden_width // n_dp
    sent = [
        lax.dynamic_slice_in_dim(sum_down, lax.rem(group + d, n_dp) * low, low, 0)
        for d in range(1, n_dp)
    ]
    last, arrivals[:-1], sent = lax.optimization_barrier((both_parts[-1], arrivals[:-1], sent))
    mine = spread_back(
        both_parts[:-1] + [last], starts, gate_mat, up_mat, table, tok_rows, False, heights
    )
    mine, handed, sent, arrivals[-1] = lax.optimization_barrier((mine, handed, sent, arrivals[-1]))
    arrived = [lax.ppermute(part, "dp", shifts[d]) for d, part in enumerate(sent, 1)]
    late = list(range(len(own_parts), len(widths)))

    def half_of(c, mark):
        both, _ = lax.optimization_barrier((both_parts[c], mark))
        return own_half(own_cols, rows_now, both, piece)

    fills = [lambda mark, c=c: half_of(c, mark) for c in late]
    input_grad, late_parts = sum_back(ring, handed, mine, tok_rows, fills)
    arrived, _ = lax.optimization_barrier((arrived, input_grad))
    totals = None
    for c, part in enumerate(own_parts + late_parts):
        totals = join_halves(part, arrivals[c], starts[c], totals, hidden_width)
    grad_gate, grad_up = totals
    grad_down = join_down(own_cols, sum_down, arrived)[None]
    return (input_grad, grad_gate[None], grad_up[None], grad_down)


def solution(mesh):
    return jax.shard_map(
        local,
        mesh=mesh,
        in_specs=(
            P(("dp", "expert"), None),
            P(("dp", "expert"), None),
            P(("dp", "expert"), None, None),
            P(("dp", "expert"), None),
            P(("dp", "expert"), None),
            P("expert", None, None),
            P("expert", None, None),
            P("expert", None, None),
        ),
        out_specs=(
            P(("dp", "expert"), None),
            P("expert", "dp", None),
            P("expert", "dp", None),
            P("expert", "dp", None),
        ),
        check_vma=False,
    )
```

```python
import jax
import jax.numpy as jnp
import numpy as np
from jax import lax
from jax.experimental import pallas as pl
from jax.experimental.pallas import tpu as pltpu
from jax.sharding import PartitionSpec as P

grad_scale = 0.0625
f32 = jnp.float32
bf16 = jnp.bfloat16
i32 = jnp.int32
KERNEL_VMEM = 60 * 1024 * 1024
LIGHT = pl.CostEstimate(flops=1000, bytes_accessed=1000, transcendentals=0)


def dot(a, b, dims):
    return lax.dot_general(a, b, (dims, ((), ())), preferred_element_type=f32)


def chunk_widths(width):
    lanes = width // 128
    shares = (3, 7, 11)
    ends = [-(-lanes * x // 11) * 128 for x in shares]
    return [e - s for s, e in zip([0] + ends, ends) if e > s]


def chip_cycle(n_chips):
    cols = n_chips // 4
    if n_chips % 4 or cols < 2:
        return list(range(n_chips))
    walk = [(row, 0) for row in range(4)]
    for step, row in enumerate((3, 2, 1, 0)):
        across = range(1, cols) if step % 2 == 0 else range(cols - 1, 0, -1)
        walk += [(row, col) for col in across]
    return [row * cols + col for row, col in walk]


def put_rows(order, table, shards, rows, routed, cap):
    count = len(shards)
    n_peers, _, _ = table.shape
    width = shards[0][0].shape[1]

    def body(order_ref, table_ref, *refs):
        parts = refs[: 2 * count]
        rows_ref, routed_ref = refs[-2:]
        step = pl.program_id(0)
        for i in range(count):

            @pl.when(step == i)
            def _():
                info = table_ref[0]
                place = (
                    lax.broadcasted_iota(i32, (cap, tok_rows_of), 1).astype(f32) == info[:, 0:1]
                ).astype(bf16)
                rows_ref[...] = jnp.dot(
                    place, parts[2 * i][...], preferred_element_type=f32
                ).astype(bf16)
                picked = jnp.dot(place, parts[2 * i + 1][...], preferred_element_type=f32)
                routed_ref[...] = (info[:, 1:2] * picked).astype(bf16)

    tok_rows_of = shards[0][2]
    in_specs = [pl.BlockSpec((1, cap, 2), lambda i, order: (order[i], 0, 0))]
    operands = [table]
    for tok, grad, height, tok_at, grad_at in shards:
        in_specs.append(pl.BlockSpec((height, width), lambda i, order, a=tok_at: (a, 0)))
        in_specs.append(pl.BlockSpec((height, width), lambda i, order, a=grad_at: (a, 0)))
        operands += [tok, grad]
    aliases = {}
    if rows is not None:
        aliases = {1 + len(operands): 0, 2 + len(operands): 1}
        in_specs += [pl.BlockSpec(memory_space=pl.ANY)] * 2
        operands += [rows, routed]
    n_slots = n_peers * cap
    shape = jax.ShapeDtypeStruct((n_slots, width), bf16)
    out_spec = pl.BlockSpec((cap, width), lambda i, order: (order[i], 0))
    return pl.pallas_call(
        body,
        out_shape=(shape, shape),
        grid_spec=pltpu.PrefetchScalarGridSpec(
            num_scalar_prefetch=1,
            grid=(count,),
            in_specs=in_specs,
            out_specs=(out_spec, out_spec),
        ),
        input_output_aliases=aliases,
        compiler_params=pltpu.CompilerParams(vmem_limit_bytes=KERNEL_VMEM),
        cost_estimate=pl.CostEstimate(
            flops=4 * count * cap * tok_rows_of * width,
            bytes_accessed=4 * count * (tok_rows_of + cap) * width,
            transcendentals=0,
        ),
        name="put_rows",
    )(order, *operands)


class Ring:
    def __init__(self):
        self.n_peers = lax.axis_size("expert")
        self.n = self.n_peers // 2
        self.far = self.n // 2
        self.names = [self.far]
        for d in range(self.far - 1, 0, -1):
            self.names += [d, -d]
        self.names.append(0)
        cycle = chip_cycle(self.n)
        spot = [cycle.index(c) for c in range(self.n)]
        chips = range(self.n)
        self.fwd = [(2 * cycle[i] + c, 2 * cycle[(i + 1) % self.n] + c) for i in chips for c in (0, 1)]
        self.bwd = [(b, a) for a, b in self.fwd]
        self.swap = [(i, i ^ 1) for i in range(self.n_peers)]
        table = np.zeros((self.n_peers, self.n_peers), np.int32)
        for e in range(self.n_peers):
            for core in (0, 1):
                for j, d in enumerate(self.names):
                    chip = cycle[(spot[e // 2] - d) % self.n]
                    table[e, core * self.n + j] = 2 * chip + (e % 2 if core else 1 - e % 2)
        self.order = jnp.asarray(table)[lax.axis_index("expert")]

    def at(self, distance, other):
        return self.names.index(distance) + (0 if other else self.n)

    def ahead(self, x):
        return lax.ppermute(x, "expert", self.fwd)

    def behind(self, x):
        return lax.ppermute(x, "expert", self.bwd)

    def other_core(self, x):
        return lax.ppermute(x, "expert", self.swap)


def gather_rows(ring, tokens, out_grad, table, cap, beside):
    tok_rows = tokens.shape[0]
    own = jnp.concatenate([tokens, out_grad], axis=0)
    beside = list(beside)

    def whole(x):
        return (x, x, tok_rows, 0, 1)

    def place(spots, shards, state):
        return put_rows(np.array(spots, np.int32), table, shards, *state, cap)

    state = (None, None)
    ahead, behind = own, own
    pending = ([ring.at(0, False), ring.at(0, True)], [whole(own), whole(ring.other_core(own))])
    marks = []
    for d in range(1, ring.far):
        ahead, behind = ring.ahead(ahead), ring.behind(behind)
        if d >= 2:
            state = place(*pending[0], state)
            pending = pending[1:]
            ahead, behind, state = lax.optimization_barrier((ahead, behind, state))
            if d - 2 < len(beside):
                ahead, behind, beside[d - 2] = lax.optimization_barrier(
                    (ahead, behind, beside[d - 2])
                )
        else:
            pending = [pending]
        marks.append((ahead, behind))
        pending.append(
            (
                [ring.at(d, False), ring.at(-d, False), ring.at(d, True), ring.at(-d, True)],
                [whole(x) for x in (ahead, behind, ring.other_core(ahead), ring.other_core(behind))],
            )
        )
    far_tok = ring.ahead(ahead[:tok_rows])
    far_grad = ring.behind(behind[tok_rows:])
    state = place(*pending[0], state)
    far_tok, far_grad, state = lax.optimization_barrier((far_tok, far_grad, state))
    marks.append((far_tok, far_grad))
    for spots, shards in pending[1:]:
        state = place(spots, shards, state)
    state = place(
        [ring.at(ring.far, False), ring.at(ring.far, True)],
        [
            (far_tok, far_grad, tok_rows, 0, 0),
            (ring.other_core(far_tok), ring.other_core(far_grad), tok_rows, 0, 0),
        ],
        state,
    )
    return state, marks, beside


def add_blocks(blocks, tok_rows, split, cols):
    operands = [x for terms in blocks for x in terms]
    half = tok_rows // 2

    def body(*refs):
        outs, at = refs[len(operands) :], 0
        for i, terms in enumerate(blocks):
            for lower in (0, half):
                total = jnp.zeros((half, cols), f32)
                for j, (_, _, rows, first, _) in enumerate(terms):
                    if first <= lower < first + rows:
                        total += refs[at + j][lower - first : lower - first + half, :].astype(f32)
                if split:
                    outs[1 if lower else 0][...] = total.astype(bf16)
                else:
                    outs[i][lower : lower + half, :] = total.astype(bf16)
            at += len(terms)

    height, count = (half, 2) if split else (tok_rows, len(blocks))
    out = pl.pallas_call(
        body,
        out_shape=[jax.ShapeDtypeStruct((height, cols), bf16)] * count,
        grid=(1,),
        in_specs=[
            pl.BlockSpec((rows, cols), lambda i, at=at, col=col: (at, col))
            for _, at, rows, _, col in operands
        ],
        out_specs=[pl.BlockSpec((height, cols), lambda i: (0, 0))] * count,
        compiler_params=pltpu.CompilerParams(vmem_limit_bytes=KERNEL_VMEM),
        cost_estimate=LIGHT,
        name="add_blocks",
    )(*[x[0] for x in operands])
    return list(out)


def sum_back(ring, handed, mine, tok_rows, fills):
    width = mine[0].shape[1]
    cols, half = width // 2, tok_rows // 2
    terms = [{}, {}]
    j = 0
    for piece, own in zip(handed, mine):
        for at in range(piece.shape[0] // tok_rows):
            for h in (0, 1):
                terms[h][ring.names[j]] = [(x, at, tok_rows, 0, h) for x in (own, piece)]
            j += 1

    moving = []
    for h in (0, 1):
        top, low = add_blocks([terms[h][ring.far]], tok_rows, True, cols)
        moving.append([(ring.ahead(top), 0, half, 0, 0), (ring.behind(low), 0, half, half, 0)])
    mark, filled = moving[0][0][0], []
    for d in range(ring.far - 1, 0, -1):
        for h in (0, 1):
            ahead, behind = add_blocks(
                [terms[h][-d] + moving[h][:1], terms[h][d] + moving[h][1:]], tok_rows, False, cols
            )
            ahead, behind = ring.ahead(ahead), ring.behind(behind)
            if h == 0 and len(filled) < len(fills):
                done = fills[len(filled)](mark)
                ahead, behind, done = lax.optimization_barrier((ahead, behind, done))
                filled.append(done)
            moving[h] = [(ahead, 0, tok_rows, 0, 0), (behind, 0, tok_rows, 0, 0)]
        mark = moving[0][0][0]
    for fill in fills[len(filled) :]:
        filled.append(fill(mark))
    done = [add_blocks([terms[h][0] + moving[h]], tok_rows, False, cols)[0] for h in (0, 1)]
    return jnp.concatenate(done, axis=1), filled


def join_down(group, total, arrived):
    low, width = arrived[0].shape
    r = low // 4 if low % 64 == 0 else low
    steps = low // r

    def body(group_ref, *refs):
        out = refs[0][...].astype(f32)
        for x in refs[1:-1]:
            out = out + x[...].astype(f32)
        refs[-1][...] = (grad_scale * out).astype(bf16)

    return pl.pallas_call(
        body,
        out_shape=jax.ShapeDtypeStruct((low, width), bf16),
        grid_spec=pltpu.PrefetchScalarGridSpec(
            num_scalar_prefetch=1,
            grid=(steps,),
            in_specs=[pl.BlockSpec((r, width), lambda i, group: (group[0] * steps + i, 0))]
            + [pl.BlockSpec((r, width), lambda i, group: (i, 0))] * len(arrived),
            out_specs=pl.BlockSpec((r, width), lambda i, group: (i, 0)),
        ),
        compiler_params=pltpu.CompilerParams(vmem_limit_bytes=KERNEL_VMEM),
        cost_estimate=LIGHT,
        name="join_down",
    )(group, total, *arrived)


def blocks_per_step(n_blocks, cap):
    return max(b for b in range(1, n_blocks + 1) if n_blocks % b == 0 and b * cap <= 768)


def chunk_grads(order, cols, rows, routed, gate, up_mat, down_mat, start, piece):
    n_slots, width = rows.shape
    n_peers, cap, w = gate.shape
    n = blocks_per_step(n_peers, cap)
    r = n * cap
    n_rows, n_cols = n_slots // r, cols.shape[0]

    def body(order_ref, cols_ref, rows_ref, routed_ref, up_ref, down_ref, col_ref, *refs):
        gate_refs, (hidden_ref, both_ref, part_ref, held) = refs[:n], refs[n:]
        step = pl.program_id(0)

        @pl.when(step < n_rows)
        def _():
            up_all = jnp.dot(rows_ref[...], up_ref[...], preferred_element_type=f32)
            grad_all = dot(routed_ref[...], down_ref[...], ((1,), (1,)))
            for b in range(n):
                at = slice(b * cap, (b + 1) * cap)
                up_act, hidden_grad = up_all[at], grad_all[at]
                gate_val = gate_refs[b][0].astype(f32)
                gate_sig = jax.nn.sigmoid(gate_val)
                gate_act = gate_val * gate_sig
                hidden_ref[at, :] = (gate_act * up_act).astype(bf16)
                both_ref[at, w:] = (hidden_grad * gate_act).astype(bf16)
                both_ref[at, :w] = (
                    hidden_grad * up_act * gate_sig * (1.0 + gate_val * (1.0 - gate_sig))
                ).astype(bf16)
            held[pl.ds(pl.multiple_of(step * r, r), r), :] = both_ref[...]

        @pl.when(step >= n_rows)
        def _():
            part_ref[...] = dot(col_ref[...], held[...], ((0,), (0,))).astype(bf16)

    def row(i):
        return jnp.minimum(i, n_rows - 1)

    def col(i):
        return jnp.maximum(i - n_rows, 0)

    return pl.pallas_call(
        body,
        out_shape=(
            jax.ShapeDtypeStruct((n_slots, w), bf16),
            jax.ShapeDtypeStruct((n_slots, 2 * w), bf16),
            jax.ShapeDtypeStruct((n_cols * piece, 2 * w), bf16),
        ),
        grid_spec=pltpu.PrefetchScalarGridSpec(
            num_scalar_prefetch=2,
            grid=(n_rows + n_cols,),
            in_specs=[
                pl.BlockSpec((r, width), lambda i, order, cols: (row(i), 0)),
                pl.BlockSpec((r, width), lambda i, order, cols: (row(i), 0)),
                pl.BlockSpec((pl.Element(width), pl.Element(w)), lambda i, order, cols: (0, start)),
                pl.BlockSpec((pl.Element(w), pl.Element(width)), lambda i, order, cols: (start, 0)),
                pl.BlockSpec((n_slots, piece), lambda i, order, cols: (0, cols[col(i)])),
            ]
            + [
                pl.BlockSpec((1, cap, w), lambda i, order, cols, b=b: (order[n * row(i) + b], 0, 0))
                for b in range(n)
            ],
            out_specs=(
                pl.BlockSpec((r, w), lambda i, order, cols: (row(i), 0)),
                pl.BlockSpec((r, 2 * w), lambda i, order, cols: (row(i), 0)),
                pl.BlockSpec((piece, 2 * w), lambda i, order, cols: (col(i), 0)),
            ),
            scratch_shapes=[pltpu.VMEM((n_slots, 2 * w), bf16)],
        ),
        compiler_params=pltpu.CompilerParams(vmem_limit_bytes=KERNEL_VMEM),
        cost_estimate=LIGHT,
        name="chunk_grads",
    )(order, cols, rows, routed, up_mat, down_mat, rows, *[gate] * n)


def own_half(cols, rows, both, piece):
    n_slots = rows.shape[0]
    w = both.shape[1]

    def body(cols_ref, rows_ref, both_ref, own_ref):
        own_ref[...] = dot(rows_ref[...], both_ref[...], ((0,), (0,))).astype(bf16)

    return pl.pallas_call(
        body,
        out_shape=jax.ShapeDtypeStruct((piece, w), bf16),
        grid_spec=pltpu.PrefetchScalarGridSpec(
            num_scalar_prefetch=1,
            grid=(1,),
            in_specs=[
                pl.BlockSpec((n_slots, piece), lambda i, cols: (0, cols[0])),
                pl.BlockSpec((n_slots, w), lambda i, cols: (0, 0)),
            ],
            out_specs=pl.BlockSpec((piece, w), lambda i, cols: (0, 0)),
        ),
        compiler_params=pltpu.CompilerParams(vmem_limit_bytes=KERNEL_VMEM),
        cost_estimate=LIGHT,
        name="own_half",
    )(cols, rows, both)


def down_rows(routed, hidden, start, total, hidden_width):
    n_slots, width = routed.shape
    w = hidden.shape[1]
    span = min(1024, width)

    def body(routed_ref, hidden_ref, *refs):
        down_ref, turned = refs[-2:]

        @pl.when(pl.program_id(0) == 0)
        def _():
            turned[...] = hidden_ref[...].T

        down_ref[...] = jnp.dot(turned[...], routed_ref[...], preferred_element_type=f32).astype(bf16)

    aliased = [] if total is None else [total]
    return pl.pallas_call(
        body,
        out_shape=jax.ShapeDtypeStruct((hidden_width, width), bf16),
        grid=(width // span,),
        in_specs=[
            pl.BlockSpec((n_slots, span), lambda i: (0, i)),
            pl.BlockSpec((n_slots, w), lambda i: (0, 0)),
        ]
        + [pl.BlockSpec(memory_space=pl.ANY) for _ in aliased],
        out_specs=pl.BlockSpec((pl.Element(w), pl.Element(span)), lambda i: (start, i * span)),
        scratch_shapes=[pltpu.VMEM((w, n_slots), bf16)],
        input_output_aliases={2: 0} if aliased else {},
        compiler_params=pltpu.CompilerParams(vmem_limit_bytes=KERNEL_VMEM),
        cost_estimate=LIGHT,
        name="down_rows",
    )(routed, hidden, *aliased)


def join_halves(own, arrived, start, totals, hidden_width):
    piece, both_width = own.shape
    w = both_width // 2
    r = min(256, piece)
    n_in = 1 + len(arrived)

    def body(*refs):
        gate_ref, up_ref = refs[-2:]
        for at, out_ref in ((slice(0, w), gate_ref), (slice(w, 2 * w), up_ref)):
            total = refs[0][:, at].astype(f32)
            for x in refs[1:n_in]:
                total = total + x[:, at].astype(f32)
            out_ref[...] = (grad_scale * total).astype(bf16)

    aliased = [] if totals is None else list(totals)
    shape = jax.ShapeDtypeStruct((piece, hidden_width), bf16)
    out_spec = pl.BlockSpec((pl.Element(r), pl.Element(w)), lambda i: (i * r, start))
    return pl.pallas_call(
        body,
        out_shape=(shape, shape),
        grid=(piece // r,),
        in_specs=[pl.BlockSpec((r, both_width), lambda i: (i, 0))] * n_in
        + [pl.BlockSpec(memory_space=pl.ANY) for _ in aliased],
        out_specs=(out_spec, out_spec),
        input_output_aliases={n_in: 0, n_in + 1: 1} if aliased else {},
        compiler_params=pltpu.CompilerParams(vmem_limit_bytes=KERNEL_VMEM),
        cost_estimate=LIGHT,
        name="join_halves",
    )(own, *arrived, *aliased)


def spread_back(parts, starts, gate_mat, up_mat, table, tok_rows, first, heights):
    n_peers, _, cap = table.shape
    half = n_peers // 2
    width, hidden_width = gate_mat.shape
    cols = min(512, width)
    rows = half * cap
    shift = 0 if first else 1
    owner = [(i, b) for i, height in enumerate(heights) for b in range(height)]

    def body(*refs):
        part_refs = refs[: len(parts)]
        gate_ref, up_ref, table_ref = refs[len(parts) : len(parts) + 3]
        out_refs = refs[len(parts) + 3 :]
        total = jnp.zeros((rows, cols), f32)
        for start, part_ref in zip(starts, part_refs):
            w = part_ref.shape[1] // 2
            total += dot(part_ref[:, :w], gate_ref[:, start : start + w], ((1,), (1,)))
            total += dot(part_ref[:, w:], up_ref[:, start : start + w], ((1,), (1,)))
        terms = total.astype(bf16)
        for j, (i, b) in enumerate(owner):
            tok = table_ref[j, 0:1, :]
            place = (lax.broadcasted_iota(i32, (tok_rows, cap), 0).astype(f32) == tok).astype(bf16)
            spread = jnp.dot(place, terms[j * cap : (j + 1) * cap], preferred_element_type=f32)
            out_refs[i][b * tok_rows : (b + 1) * tok_rows, :] = spread.astype(bf16)

    return pl.pallas_call(
        body,
        out_shape=[jax.ShapeDtypeStruct((h * tok_rows, width), bf16) for h in heights],
        grid=(width // cols,),
        in_specs=[pl.BlockSpec((rows, x.shape[1]), lambda j: (shift, 0)) for x in parts]
        + [
            pl.BlockSpec((cols, hidden_width), lambda j: (j, 0)),
            pl.BlockSpec((cols, hidden_width), lambda j: (j, 0)),
            pl.BlockSpec((half, 2, cap), lambda j: (shift, 0, 0)),
        ],
        out_specs=[pl.BlockSpec((h * tok_rows, cols), lambda j: (0, j)) for h in heights],
        compiler_params=pltpu.CompilerParams(vmem_limit_bytes=KERNEL_VMEM),
        cost_estimate=LIGHT,
        name="spread_back",
    )(*parts, gate_mat, up_mat, table)


def local(tokens, out_grad, gate_saved, probs, expert_ids, w_gate, w_up, w_down):
    n_peers = lax.axis_size("expert")
    n_dp = lax.axis_size("dp")
    group = lax.axis_index("dp")
    tok_rows, model_width = tokens.shape
    top_k = expert_ids.shape[1]
    hidden_width = w_up.shape[2]
    cap = min(tok_rows, 2 * tok_rows * top_k // n_peers)
    n_routes = tok_rows * top_k
    n_slots = n_peers * cap
    gate_mat, up_mat, down_mat = w_gate[0], w_up[0], w_down[0]

    experts = jnp.arange(n_peers, dtype=i32)
    hit = expert_ids[:, :, None] == experts[None, None, :]
    named = jnp.any(hit, axis=1)
    weight = jnp.sum(jnp.where(hit, probs[:, :, None], 0.0), axis=1)
    rank = jnp.cumsum(named.astype(i32), axis=0) - 1
    slots = jnp.arange(cap, dtype=i32)
    in_slot = named[:, :, None] & (rank[:, :, None] == slots[None, None, :])
    tok_of = jnp.sum(
        jnp.where(in_slot, jnp.arange(1, tok_rows + 1, dtype=f32)[:, None, None], 0.0), axis=0
    ) - 1.0
    choice = jnp.sum(jnp.where(hit, jnp.arange(top_k, dtype=f32)[None, :, None], 0.0), axis=1)
    choice_of = jnp.sum(jnp.where(in_slot, choice[:, :, None], 0.0), axis=0)
    weight_of = jnp.sum(jnp.where(in_slot, weight[:, :, None], 0.0), axis=0)
    table = lax.all_to_all(
        jnp.concatenate([tok_of, weight_of], axis=1),
        "expert",
        split_axis=0,
        concat_axis=0,
        tiled=True,
    )
    ring = Ring()
    table = table.reshape(n_peers, 2, cap)[ring.order]
    widths = chunk_widths(hidden_width)
    starts = [sum(widths[:i]) for i in range(len(widths))]
    route_gates = jnp.transpose(gate_saved, (1, 0, 2)).reshape(n_routes, hidden_width)
    route_of = (tok_of + tok_rows * choice_of).astype(i32).reshape(n_slots, 1)
    pick = (route_of == jnp.arange(n_routes, dtype=i32)[None, :]).astype(bf16)
    send_gate = [
        dot(pick, route_gates[:, s : s + w], ((1,), (0,))).astype(bf16).reshape(n_peers, cap, w)
        for s, w in zip(starts, widths)
    ]
    (rows_in, routed), marks, (send_gate[1:],) = gather_rows(
        ring, tokens, out_grad, table.transpose(0, 2, 1), cap, [send_gate[1:]]
    )

    def send_chunk(i, mark):
        part = send_gate[i]
        if mark is not None:
            part, _ = lax.optimization_barrier((part, mark))
        return lax.all_to_all(part, "expert", split_axis=0, concat_axis=0, tiled=True)

    recv_gate = [send_chunk(i, m) for i, m in zip(range(len(widths)), (None, marks[-1]))]

    piece = model_width // n_dp
    shifts = [[(i, (i + d) % n_dp) for i in range(n_dp)] for d in range(n_dp)]

    peer_cols = lax.rem(group + jnp.arange(1, n_dp, dtype=i32), n_dp)
    own_cols = group.reshape(1).astype(i32)
    both_parts, hidden_parts, arrivals, own_parts = [], [], [], []
    rows_now, routed_now = rows_in, routed
    for c, w in enumerate(widths):
        if c >= 2:
            for both in both_parts[len(own_parts) :]:
                own_parts.append(own_half(own_cols, rows_now, both, piece))
            rows_now, own_parts, arrivals[c - 2] = lax.optimization_barrier(
                (rows_now, own_parts, arrivals[c - 2])
            )
        hidden, both, sent = chunk_grads(
            ring.order,
            peer_cols,
            rows_now,
            routed_now,
            recv_gate[c],
            up_mat,
            down_mat,
            starts[c],
            piece,
        )
        both_parts.append(both)
        hidden_parts.append(hidden)
        arrivals.append(
            [
                lax.ppermute(sent[(d - 1) * piece : d * piece], "dp", shifts[d])
                for d in range(1, n_dp)
            ]
        )
        rows_now, routed_now, _ = lax.optimization_barrier((rows_now, routed_now, sent))
        if c + 2 < len(widths):
            recv_gate.append(send_chunk(c + 2, sent))

    heights = [1] + [2] * (ring.far - 1) + [1]
    theirs = spread_back(both_parts, starts, gate_mat, up_mat, table, tok_rows, True, heights)
    handed = [ring.other_core(x) for x in theirs]
    sum_down = None
    for c, hidden in enumerate(hidden_parts):
        hidden, _ = lax.optimization_barrier((hidden, theirs))
        sum_down = down_rows(routed_now, hidden, starts[c], sum_down, hidden_width)
    low = hidden_width // n_dp
    sent = [
        lax.dynamic_slice_in_dim(sum_down, lax.rem(group + d, n_dp) * low, low, 0)
        for d in range(1, n_dp)
    ]
    last, arrivals[:-1], sent = lax.optimization_barrier((both_parts[-1], arrivals[:-1], sent))
    mine = spread_back(
        both_parts[:-1] + [last], starts, gate_mat, up_mat, table, tok_rows, False, heights
    )
    mine, handed, sent, arrivals[-1] = lax.optimization_barrier((mine, handed, sent, arrivals[-1]))
    arrived = [lax.ppermute(part, "dp", shifts[d]) for d, part in enumerate(sent, 1)]
    late = list(range(len(own_parts), len(widths)))

    def late_halves(mark):
        parts, _ = lax.optimization_barrier((both_parts, mark))
        return [own_half(own_cols, rows_now, parts[c], piece) for c in late]

    def join_early(mark):
        parts, _ = lax.optimization_barrier((own_parts, mark))
        joined = None
        for c, part in enumerate(parts):
            joined = join_halves(part, arrivals[c], starts[c], joined, hidden_width)
        return joined

    input_grad, (late_parts, totals) = sum_back(
        ring, handed, mine, tok_rows, [late_halves, join_early]
    )
    arrived, _ = lax.optimization_barrier((arrived, input_grad))
    for c, part in zip(late, late_parts):
        totals = join_halves(part, arrivals[c], starts[c], totals, hidden_width)
    grad_gate, grad_up = totals
    grad_down = join_down(own_cols, sum_down, arrived)[None]
    return (input_grad, grad_gate[None], grad_up[None], grad_down)


def solution(mesh):
    return jax.shard_map(
        local,
        mesh=mesh,
        in_specs=(
            P(("dp", "expert"), None),
            P(("dp", "expert"), None),
            P(("dp", "expert"), None, None),
            P(("dp", "expert"), None),
            P(("dp", "expert"), None),
            P("expert", None, None),
            P("expert", None, None),
            P("expert", None, None),
        ),
        out_specs=(
            P(("dp", "expert"), None),
            P("expert", "dp", None),
            P("expert", "dp", None),
            P("expert", "dp", None),
        ),
        check_vma=False,
    )
```

```python
import jax
import jax.numpy as jnp
import numpy as np
from jax import lax
from jax.experimental import pallas as pl
from jax.experimental.pallas import tpu as pltpu
from jax.sharding import PartitionSpec as P

grad_scale = 0.0625
f32 = jnp.float32
bf16 = jnp.bfloat16
i32 = jnp.int32
KERNEL_VMEM = 60 * 1024 * 1024
LIGHT = pl.CostEstimate(flops=1000, bytes_accessed=1000, transcendentals=0)


def dot(a, b, dims):
    return lax.dot_general(a, b, (dims, ((), ())), preferred_element_type=f32)


def chunk_widths(width):
    lanes = width // 128
    shares = (3, 7, 11)
    ends = [-(-lanes * x // 11) * 128 for x in shares]
    return [e - s for s, e in zip([0] + ends, ends) if e > s]


def chip_cycle(n_chips):
    cols = n_chips // 4
    if n_chips % 4 or cols < 2:
        return list(range(n_chips))
    walk = [(row, 0) for row in range(4)]
    for step, row in enumerate((3, 2, 1, 0)):
        across = range(1, cols) if step % 2 == 0 else range(cols - 1, 0, -1)
        walk += [(row, col) for col in across]
    return [row * cols + col for row, col in walk]


def put_rows(order, table, shards, rows, routed, cap):
    count = len(shards)
    n_peers, _, _ = table.shape
    width = shards[0][0].shape[1]

    def body(order_ref, table_ref, *refs):
        parts = refs[: 2 * count]
        rows_ref, routed_ref = refs[-2:]
        step = pl.program_id(0)
        for i in range(count):

            @pl.when(step == i)
            def _():
                info = table_ref[0]
                place = (
                    lax.broadcasted_iota(i32, (cap, tok_rows_of), 1).astype(f32) == info[:, 0:1]
                ).astype(bf16)
                rows_ref[...] = jnp.dot(
                    place, parts[2 * i][...], preferred_element_type=f32
                ).astype(bf16)
                picked = jnp.dot(place, parts[2 * i + 1][...], preferred_element_type=f32)
                routed_ref[...] = (info[:, 1:2] * picked).astype(bf16)

    tok_rows_of = shards[0][2]
    in_specs = [pl.BlockSpec((1, cap, 2), lambda i, order: (order[i], 0, 0))]
    operands = [table]
    for tok, grad, height, tok_at, grad_at in shards:
        in_specs.append(pl.BlockSpec((height, width), lambda i, order, a=tok_at: (a, 0)))
        in_specs.append(pl.BlockSpec((height, width), lambda i, order, a=grad_at: (a, 0)))
        operands += [tok, grad]
    aliases = {}
    if rows is not None:
        aliases = {1 + len(operands): 0, 2 + len(operands): 1}
        in_specs += [pl.BlockSpec(memory_space=pl.ANY)] * 2
        operands += [rows, routed]
    n_slots = n_peers * cap
    shape = jax.ShapeDtypeStruct((n_slots, width), bf16)
    out_spec = pl.BlockSpec((cap, width), lambda i, order: (order[i], 0))
    return pl.pallas_call(
        body,
        out_shape=(shape, shape),
        grid_spec=pltpu.PrefetchScalarGridSpec(
            num_scalar_prefetch=1,
            grid=(count,),
            in_specs=in_specs,
            out_specs=(out_spec, out_spec),
        ),
        input_output_aliases=aliases,
        compiler_params=pltpu.CompilerParams(vmem_limit_bytes=KERNEL_VMEM),
        cost_estimate=pl.CostEstimate(
            flops=4 * count * cap * tok_rows_of * width,
            bytes_accessed=4 * count * (tok_rows_of + cap) * width,
            transcendentals=0,
        ),
        name="put_rows",
    )(order, *operands)


class Ring:
    def __init__(self):
        self.n_peers = lax.axis_size("expert")
        self.n = self.n_peers // 2
        self.far = self.n // 2
        self.names = [self.far]
        for d in range(self.far - 1, 0, -1):
            self.names += [d, -d]
        self.names.append(0)
        cycle = chip_cycle(self.n)
        spot = [cycle.index(c) for c in range(self.n)]
        chips = range(self.n)
        self.fwd = [(2 * cycle[i] + c, 2 * cycle[(i + 1) % self.n] + c) for i in chips for c in (0, 1)]
        self.bwd = [(b, a) for a, b in self.fwd]
        self.swap = [(i, i ^ 1) for i in range(self.n_peers)]
        table = np.zeros((self.n_peers, self.n_peers), np.int32)
        for e in range(self.n_peers):
            for core in (0, 1):
                for j, d in enumerate(self.names):
                    chip = cycle[(spot[e // 2] - d) % self.n]
                    table[e, core * self.n + j] = 2 * chip + (e % 2 if core else 1 - e % 2)
        self.order = jnp.asarray(table)[lax.axis_index("expert")]

    def at(self, distance, other):
        return self.names.index(distance) + (0 if other else self.n)

    def ahead(self, x):
        return lax.ppermute(x, "expert", self.fwd)

    def behind(self, x):
        return lax.ppermute(x, "expert", self.bwd)

    def other_core(self, x):
        return lax.ppermute(x, "expert", self.swap)


def gather_rows(ring, tokens, out_grad, table, cap, beside):
    tok_rows = tokens.shape[0]
    own = jnp.concatenate([tokens, out_grad], axis=0)
    beside = list(beside)

    def whole(x):
        return (x, x, tok_rows, 0, 1)

    def place(spots, shards, state):
        return put_rows(np.array(spots, np.int32), table, shards, *state, cap)

    state = (None, None)
    ahead, behind = own, own
    pending = ([ring.at(0, False), ring.at(0, True)], [whole(own), whole(ring.other_core(own))])
    marks = []
    for d in range(1, ring.far):
        ahead, behind = ring.ahead(ahead), ring.behind(behind)
        if d >= 2:
            state = place(*pending[0], state)
            pending = pending[1:]
            ahead, behind, state = lax.optimization_barrier((ahead, behind, state))
            if d - 2 < len(beside):
                ahead, behind, beside[d - 2] = lax.optimization_barrier(
                    (ahead, behind, beside[d - 2])
                )
        else:
            pending = [pending]
        marks.append((ahead, behind))
        pending.append(
            (
                [ring.at(d, False), ring.at(-d, False), ring.at(d, True), ring.at(-d, True)],
                [whole(x) for x in (ahead, behind, ring.other_core(ahead), ring.other_core(behind))],
            )
        )
    far_tok = ring.ahead(ahead[:tok_rows])
    far_grad = ring.behind(behind[tok_rows:])
    state = place(*pending[0], state)
    far_tok, far_grad, state = lax.optimization_barrier((far_tok, far_grad, state))
    marks.append((far_tok, far_grad))
    for spots, shards in pending[1:]:
        state = place(spots, shards, state)
    state = place(
        [ring.at(ring.far, False), ring.at(ring.far, True)],
        [
            (far_tok, far_grad, tok_rows, 0, 0),
            (ring.other_core(far_tok), ring.other_core(far_grad), tok_rows, 0, 0),
        ],
        state,
    )
    return state, marks, beside


def add_blocks(blocks, tok_rows, split, cols):
    operands = [x for terms in blocks for x in terms]
    half = tok_rows // 2

    def body(*refs):
        outs, at = refs[len(operands) :], 0
        for i, terms in enumerate(blocks):
            for lower in (0, half):
                total = jnp.zeros((half, cols), f32)
                for j, (_, _, rows, first, _) in enumerate(terms):
                    if first <= lower < first + rows:
                        total += refs[at + j][lower - first : lower - first + half, :].astype(f32)
                if split:
                    outs[1 if lower else 0][...] = total.astype(bf16)
                else:
                    outs[i][lower : lower + half, :] = total.astype(bf16)
            at += len(terms)

    height, count = (half, 2) if split else (tok_rows, len(blocks))
    out = pl.pallas_call(
        body,
        out_shape=[jax.ShapeDtypeStruct((height, cols), bf16)] * count,
        grid=(1,),
        in_specs=[
            pl.BlockSpec((rows, cols), lambda i, at=at, col=col: (at, col))
            for _, at, rows, _, col in operands
        ],
        out_specs=[pl.BlockSpec((height, cols), lambda i: (0, 0))] * count,
        compiler_params=pltpu.CompilerParams(vmem_limit_bytes=KERNEL_VMEM),
        cost_estimate=LIGHT,
        name="add_blocks",
    )(*[x[0] for x in operands])
    return list(out)


def sum_back(ring, handed, mine, tok_rows, fills):
    width = mine[0].shape[1]
    cols, half = width // 2, tok_rows // 2
    terms = [{}, {}]
    j = 0
    for piece, own in zip(handed, mine):
        for at in range(piece.shape[0] // tok_rows):
            for h in (0, 1):
                terms[h][ring.names[j]] = [(x, at, tok_rows, 0, h) for x in (own, piece)]
            j += 1

    moving = []
    for h in (0, 1):
        top, low = add_blocks([terms[h][ring.far]], tok_rows, True, cols)
        moving.append([(ring.ahead(top), 0, half, 0, 0), (ring.behind(low), 0, half, half, 0)])
    mark, filled = moving[0][0][0], []
    for d in range(ring.far - 1, 0, -1):
        for h in (0, 1):
            ahead, behind = add_blocks(
                [terms[h][-d] + moving[h][:1], terms[h][d] + moving[h][1:]], tok_rows, False, cols
            )
            ahead, behind = ring.ahead(ahead), ring.behind(behind)
            if h == 0 and len(filled) < len(fills):
                done = fills[len(filled)](mark)
                ahead, behind, done = lax.optimization_barrier((ahead, behind, done))
                filled.append(done)
            moving[h] = [(ahead, 0, tok_rows, 0, 0), (behind, 0, tok_rows, 0, 0)]
        mark = moving[0][0][0]
    for fill in fills[len(filled) :]:
        filled.append(fill(mark))
    done = [add_blocks([terms[h][0] + moving[h]], tok_rows, False, cols)[0] for h in (0, 1)]
    return jnp.concatenate(done, axis=1), filled


def join_down(terms):
    low, width = terms[0].shape
    r = low // 4 if low % 64 == 0 else low

    def body(*refs):
        out = refs[0][...].astype(f32)
        for x in refs[1:-1]:
            out = out + x[...].astype(f32)
        refs[-1][...] = (grad_scale * out).astype(bf16)

    spec = pl.BlockSpec((r, width), lambda i: (i, 0))
    return pl.pallas_call(
        body,
        out_shape=jax.ShapeDtypeStruct((low, width), bf16),
        grid=(low // r,),
        in_specs=[spec] * len(terms),
        out_specs=spec,
        compiler_params=pltpu.CompilerParams(vmem_limit_bytes=KERNEL_VMEM),
        cost_estimate=LIGHT,
        name="join_down",
    )(*terms)


def blocks_per_step(n_blocks, cap):
    return max(b for b in range(1, n_blocks + 1) if n_blocks % b == 0 and b * cap <= 768)


def chunk_grads(order, cols, rows, routed, gate, up_mat, down_mat, start, piece):
    n_slots, width = rows.shape
    n_peers, cap, w = gate.shape
    n = blocks_per_step(n_peers, cap)
    r = n * cap
    n_rows, n_cols = n_slots // r, cols.shape[0]

    def body(order_ref, cols_ref, rows_ref, routed_ref, up_ref, down_ref, col_ref, *refs):
        gate_refs, (hidden_ref, both_ref, part_ref, held) = refs[:n], refs[n:]
        step = pl.program_id(0)

        @pl.when(step < n_rows)
        def _():
            up_all = jnp.dot(rows_ref[...], up_ref[...], preferred_element_type=f32)
            grad_all = dot(routed_ref[...], down_ref[...], ((1,), (1,)))
            for b in range(n):
                at = slice(b * cap, (b + 1) * cap)
                up_act, hidden_grad = up_all[at], grad_all[at]
                gate_val = gate_refs[b][0].astype(f32)
                gate_sig = jax.nn.sigmoid(gate_val)
                gate_act = gate_val * gate_sig
                hidden_ref[at, :] = (gate_act * up_act).astype(bf16)
                both_ref[at, w:] = (hidden_grad * gate_act).astype(bf16)
                both_ref[at, :w] = (
                    hidden_grad * up_act * gate_sig * (1.0 + gate_val * (1.0 - gate_sig))
                ).astype(bf16)
            held[pl.ds(pl.multiple_of(step * r, r), r), :] = both_ref[...]

        @pl.when(step >= n_rows)
        def _():
            part_ref[...] = dot(col_ref[...], held[...], ((0,), (0,))).astype(bf16)

    def row(i):
        return jnp.minimum(i, n_rows - 1)

    def col(i):
        return jnp.maximum(i - n_rows, 0)

    return pl.pallas_call(
        body,
        out_shape=(
            jax.ShapeDtypeStruct((n_slots, w), bf16),
            jax.ShapeDtypeStruct((n_slots, 2 * w), bf16),
            jax.ShapeDtypeStruct((n_cols * piece, 2 * w), bf16),
        ),
        grid_spec=pltpu.PrefetchScalarGridSpec(
            num_scalar_prefetch=2,
            grid=(n_rows + n_cols,),
            in_specs=[
                pl.BlockSpec((r, width), lambda i, order, cols: (row(i), 0)),
                pl.BlockSpec((r, width), lambda i, order, cols: (row(i), 0)),
                pl.BlockSpec((pl.Element(width), pl.Element(w)), lambda i, order, cols: (0, start)),
                pl.BlockSpec((pl.Element(w), pl.Element(width)), lambda i, order, cols: (start, 0)),
                pl.BlockSpec((n_slots, piece), lambda i, order, cols: (0, cols[col(i)])),
            ]
            + [
                pl.BlockSpec((1, cap, w), lambda i, order, cols, b=b: (order[n * row(i) + b], 0, 0))
                for b in range(n)
            ],
            out_specs=(
                pl.BlockSpec((r, w), lambda i, order, cols: (row(i), 0)),
                pl.BlockSpec((r, 2 * w), lambda i, order, cols: (row(i), 0)),
                pl.BlockSpec((piece, 2 * w), lambda i, order, cols: (col(i), 0)),
            ),
            scratch_shapes=[pltpu.VMEM((n_slots, 2 * w), bf16)],
        ),
        compiler_params=pltpu.CompilerParams(vmem_limit_bytes=KERNEL_VMEM),
        cost_estimate=LIGHT,
        name="chunk_grads",
    )(order, cols, rows, routed, up_mat, down_mat, rows, *[gate] * n)


def own_half(cols, rows, both, piece):
    n_slots = rows.shape[0]
    w = both.shape[1]

    def body(cols_ref, rows_ref, both_ref, own_ref):
        own_ref[...] = dot(rows_ref[...], both_ref[...], ((0,), (0,))).astype(bf16)

    return pl.pallas_call(
        body,
        out_shape=jax.ShapeDtypeStruct((piece, w), bf16),
        grid_spec=pltpu.PrefetchScalarGridSpec(
            num_scalar_prefetch=1,
            grid=(1,),
            in_specs=[
                pl.BlockSpec((n_slots, piece), lambda i, cols: (0, cols[0])),
                pl.BlockSpec((n_slots, w), lambda i, cols: (0, 0)),
            ],
            out_specs=pl.BlockSpec((piece, w), lambda i, cols: (0, 0)),
        ),
        compiler_params=pltpu.CompilerParams(vmem_limit_bytes=KERNEL_VMEM),
        cost_estimate=LIGHT,
        name="own_half",
    )(cols, rows, both)


def down_rows(order, routed, hidden_parts, starts):
    n_slots, width = routed.shape
    hidden_width = sum(x.shape[1] for x in hidden_parts)
    n_parts = order.shape[0]
    low = hidden_width // n_parts
    span = min(512, width)
    n_in = len(hidden_parts)

    def body(order_ref, routed_ref, *refs):
        turned, held = refs[-2:]

        @pl.when(pl.program_id(0) == 0)
        def _():
            for start, x in zip(starts, refs[:n_in]):
                turned[start : start + x.shape[1], :] = x[...].T

        held[...] = jnp.dot(turned[...], routed_ref[...], preferred_element_type=f32).astype(bf16)
        for d, out_ref in enumerate(refs[n_in:-2]):
            out_ref[...] = held[pl.ds(pl.multiple_of(order_ref[d] * low, 16), low), :]

    return pl.pallas_call(
        body,
        out_shape=[jax.ShapeDtypeStruct((low, width), bf16)] * n_parts,
        grid_spec=pltpu.PrefetchScalarGridSpec(
            num_scalar_prefetch=1,
            grid=(width // span,),
            in_specs=[pl.BlockSpec((n_slots, span), lambda i, order: (0, i))]
            + [pl.BlockSpec(x.shape, lambda i, order: (0, 0)) for x in hidden_parts],
            out_specs=[pl.BlockSpec((low, span), lambda i, order: (0, i))] * n_parts,
            scratch_shapes=[
                pltpu.VMEM((hidden_width, n_slots), bf16),
                pltpu.VMEM((hidden_width, span), bf16),
            ],
        ),
        compiler_params=pltpu.CompilerParams(vmem_limit_bytes=KERNEL_VMEM),
        cost_estimate=LIGHT,
        name="down_rows",
    )(order, routed, *hidden_parts)


def join_halves(own_parts, arrivals, starts, hidden_width):
    piece = own_parts[0].shape[0]
    r = min(128, piece)
    operands = [x for own, arrived in zip(own_parts, arrivals) for x in [own] + list(arrived)]
    each = len(operands) // len(own_parts)

    def body(*refs):
        gate_ref, up_ref = refs[-2:]
        for c, start in enumerate(starts):
            terms = refs[c * each : (c + 1) * each]
            w = terms[0].shape[1] // 2
            for at, out_ref in ((slice(0, w), gate_ref), (slice(w, 2 * w), up_ref)):
                total = terms[0][:, at].astype(f32)
                for x in terms[1:]:
                    total = total + x[:, at].astype(f32)
                out_ref[:, start : start + w] = (grad_scale * total).astype(bf16)

    shape = jax.ShapeDtypeStruct((piece, hidden_width), bf16)
    out_spec = pl.BlockSpec((r, hidden_width), lambda i: (i, 0))
    return pl.pallas_call(
        body,
        out_shape=(shape, shape),
        grid=(piece // r,),
        in_specs=[pl.BlockSpec((r, x.shape[1]), lambda i: (i, 0)) for x in operands],
        out_specs=(out_spec, out_spec),
        compiler_params=pltpu.CompilerParams(vmem_limit_bytes=KERNEL_VMEM),
        cost_estimate=LIGHT,
        name="join_halves",
    )(*operands)


def spread_back(parts, starts, gate_mat, up_mat, table, tok_rows, first, heights):
    n_peers, _, cap = table.shape
    half = n_peers // 2
    width, hidden_width = gate_mat.shape
    cols = min(512, width)
    rows = half * cap
    shift = 0 if first else 1
    owner = [(i, b) for i, height in enumerate(heights) for b in range(height)]

    def body(*refs):
        part_refs = refs[: len(parts)]
        gate_ref, up_ref, table_ref = refs[len(parts) : len(parts) + 3]
        out_refs = refs[len(parts) + 3 :]
        total = jnp.zeros((rows, cols), f32)
        for start, part_ref in zip(starts, part_refs):
            w = part_ref.shape[1] // 2
            total += dot(part_ref[:, :w], gate_ref[:, start : start + w], ((1,), (1,)))
            total += dot(part_ref[:, w:], up_ref[:, start : start + w], ((1,), (1,)))
        terms = total.astype(bf16)
        for j, (i, b) in enumerate(owner):
            tok = table_ref[j, 0:1, :]
            place = (lax.broadcasted_iota(i32, (tok_rows, cap), 0).astype(f32) == tok).astype(bf16)
            spread = jnp.dot(place, terms[j * cap : (j + 1) * cap], preferred_element_type=f32)
            out_refs[i][b * tok_rows : (b + 1) * tok_rows, :] = spread.astype(bf16)

    return pl.pallas_call(
        body,
        out_shape=[jax.ShapeDtypeStruct((h * tok_rows, width), bf16) for h in heights],
        grid=(width // cols,),
        in_specs=[pl.BlockSpec((rows, x.shape[1]), lambda j: (shift, 0)) for x in parts]
        + [
            pl.BlockSpec((cols, hidden_width), lambda j: (j, 0)),
            pl.BlockSpec((cols, hidden_width), lambda j: (j, 0)),
            pl.BlockSpec((half, 2, cap), lambda j: (shift, 0, 0)),
        ],
        out_specs=[pl.BlockSpec((h * tok_rows, cols), lambda j: (0, j)) for h in heights],
        compiler_params=pltpu.CompilerParams(vmem_limit_bytes=KERNEL_VMEM),
        cost_estimate=LIGHT,
        name="spread_back",
    )(*parts, gate_mat, up_mat, table)


def local(tokens, out_grad, gate_saved, probs, expert_ids, w_gate, w_up, w_down):
    n_peers = lax.axis_size("expert")
    n_dp = lax.axis_size("dp")
    group = lax.axis_index("dp")
    tok_rows, model_width = tokens.shape
    top_k = expert_ids.shape[1]
    hidden_width = w_up.shape[2]
    cap = min(tok_rows, 2 * tok_rows * top_k // n_peers)
    n_routes = tok_rows * top_k
    n_slots = n_peers * cap
    gate_mat, up_mat, down_mat = w_gate[0], w_up[0], w_down[0]

    experts = jnp.arange(n_peers, dtype=i32)
    hit = expert_ids[:, :, None] == experts[None, None, :]
    named = jnp.any(hit, axis=1)
    weight = jnp.sum(jnp.where(hit, probs[:, :, None], 0.0), axis=1)
    rank = jnp.cumsum(named.astype(i32), axis=0) - 1
    slots = jnp.arange(cap, dtype=i32)
    in_slot = named[:, :, None] & (rank[:, :, None] == slots[None, None, :])
    tok_of = jnp.sum(
        jnp.where(in_slot, jnp.arange(1, tok_rows + 1, dtype=f32)[:, None, None], 0.0), axis=0
    ) - 1.0
    choice = jnp.sum(jnp.where(hit, jnp.arange(top_k, dtype=f32)[None, :, None], 0.0), axis=1)
    choice_of = jnp.sum(jnp.where(in_slot, choice[:, :, None], 0.0), axis=0)
    weight_of = jnp.sum(jnp.where(in_slot, weight[:, :, None], 0.0), axis=0)
    table = lax.all_to_all(
        jnp.concatenate([tok_of, weight_of], axis=1),
        "expert",
        split_axis=0,
        concat_axis=0,
        tiled=True,
    )
    ring = Ring()
    table = table.reshape(n_peers, 2, cap)[ring.order]
    widths = chunk_widths(hidden_width)
    starts = [sum(widths[:i]) for i in range(len(widths))]
    route_gates = jnp.transpose(gate_saved, (1, 0, 2)).reshape(n_routes, hidden_width)
    route_of = (tok_of + tok_rows * choice_of).astype(i32).reshape(n_slots, 1)
    pick = (route_of == jnp.arange(n_routes, dtype=i32)[None, :]).astype(bf16)
    send_gate = [
        dot(pick, route_gates[:, s : s + w], ((1,), (0,))).astype(bf16).reshape(n_peers, cap, w)
        for s, w in zip(starts, widths)
    ]
    (rows_in, routed), marks, (send_gate[1:],) = gather_rows(
        ring, tokens, out_grad, table.transpose(0, 2, 1), cap, [send_gate[1:]]
    )

    def send_chunk(i, mark):
        part = send_gate[i]
        if mark is not None:
            part, _ = lax.optimization_barrier((part, mark))
        return lax.all_to_all(part, "expert", split_axis=0, concat_axis=0, tiled=True)

    recv_gate = [send_chunk(i, m) for i, m in zip(range(len(widths)), (None, marks[-1]))]

    piece = model_width // n_dp
    shifts = [[(i, (i + d) % n_dp) for i in range(n_dp)] for d in range(n_dp)]

    peer_cols = lax.rem(group + jnp.arange(1, n_dp, dtype=i32), n_dp)
    own_cols = group.reshape(1).astype(i32)
    both_parts, hidden_parts, arrivals, own_parts = [], [], [], []
    rows_now, routed_now = rows_in, routed
    for c, w in enumerate(widths):
        if c >= 2:
            for both in both_parts[len(own_parts) :]:
                own_parts.append(own_half(own_cols, rows_now, both, piece))
            rows_now, own_parts, arrivals[c - 2] = lax.optimization_barrier(
                (rows_now, own_parts, arrivals[c - 2])
            )
        hidden, both, sent = chunk_grads(
            ring.order,
            peer_cols,
            rows_now,
            routed_now,
            recv_gate[c],
            up_mat,
            down_mat,
            starts[c],
            piece,
        )
        both_parts.append(both)
        hidden_parts.append(hidden)
        arrivals.append(
            [
                lax.ppermute(sent[(d - 1) * piece : d * piece], "dp", shifts[d])
                for d in range(1, n_dp)
            ]
        )
        rows_now, routed_now, _ = lax.optimization_barrier((rows_now, routed_now, sent))
        if c + 2 < len(widths):
            recv_gate.append(send_chunk(c + 2, sent))

    heights = [1] + [2] * (ring.far - 1) + [1]
    theirs = spread_back(both_parts, starts, gate_mat, up_mat, table, tok_rows, True, heights)
    handed = [ring.other_core(x) for x in theirs]
    hidden_parts, _ = lax.optimization_barrier((hidden_parts, theirs))
    down_order = lax.rem(group + jnp.arange(n_dp, dtype=i32), n_dp)
    down, *sent = down_rows(down_order, routed_now, hidden_parts, starts)
    last, arrivals[:-1], sent = lax.optimization_barrier((both_parts[-1], arrivals[:-1], sent))
    mine = spread_back(
        both_parts[:-1] + [last], starts, gate_mat, up_mat, table, tok_rows, False, heights
    )
    parts, _ = lax.optimization_barrier((both_parts, mine))
    for both in parts[len(own_parts) :]:
        own_parts.append(own_half(own_cols, rows_now, both, piece))
    mine, handed, sent, own_parts, arrivals[-1] = lax.optimization_barrier(
        (mine, handed, sent, own_parts, arrivals[-1])
    )
    arrived = [lax.ppermute(part, "dp", shifts[d]) for d, part in enumerate(sent, 1)]
    input_grad, _ = sum_back(ring, handed, mine, tok_rows, [])
    own_parts, _ = lax.optimization_barrier((own_parts, input_grad))
    grad_gate, grad_up = join_halves(own_parts, arrivals, starts, hidden_width)
    arrived, grad_gate = lax.optimization_barrier((arrived, grad_gate))
    grad_down = join_down([down] + arrived)[None]
    return (input_grad, grad_gate[None], grad_up[None], grad_down)


def solution(mesh):
    return jax.shard_map(
        local,
        mesh=mesh,
        in_specs=(
            P(("dp", "expert"), None),
            P(("dp", "expert"), None),
            P(("dp", "expert"), None, None),
            P(("dp", "expert"), None),
            P(("dp", "expert"), None),
            P("expert", None, None),
            P("expert", None, None),
            P("expert", None, None),
        ),
        out_specs=(
            P(("dp", "expert"), None),
            P("expert", "dp", None),
            P("expert", "dp", None),
            P("expert", "dp", None),
        ),
        check_vma=False,
    )
```

```python
import jax
import jax.numpy as jnp
import numpy as np
from jax import lax
from jax.experimental import pallas as pl
from jax.experimental.pallas import tpu as pltpu
from jax.sharding import PartitionSpec as P

grad_scale = 0.0625
f32 = jnp.float32
bf16 = jnp.bfloat16
i32 = jnp.int32
KERNEL_VMEM = 60 * 1024 * 1024
LIGHT = pl.CostEstimate(flops=1000, bytes_accessed=1000, transcendentals=0)


def dot(a, b, dims):
    return lax.dot_general(a, b, (dims, ((), ())), preferred_element_type=f32)


def chunk_widths(width):
    lanes = width // 128
    shares = (3, 7, 11)
    ends = [-(-lanes * x // 11) * 128 for x in shares]
    return [e - s for s, e in zip([0] + ends, ends) if e > s]


def chip_cycle(n_chips):
    cols = n_chips // 4
    if n_chips % 4 or cols < 2:
        return list(range(n_chips))
    walk = [(row, 0) for row in range(4)]
    for step, row in enumerate((3, 2, 1, 0)):
        across = range(1, cols) if step % 2 == 0 else range(cols - 1, 0, -1)
        walk += [(row, col) for col in across]
    return [row * cols + col for row, col in walk]


def put_rows(order, table, shards, rows, routed, cap):
    count = len(shards)
    n_peers, _, _ = table.shape
    width = shards[0][0].shape[1]

    def body(order_ref, table_ref, *refs):
        parts = refs[: 2 * count]
        rows_ref, routed_ref = refs[-2:]
        step = pl.program_id(0)
        for i in range(count):

            @pl.when(step == i)
            def _():
                info = table_ref[0]
                place = (
                    lax.broadcasted_iota(i32, (cap, tok_rows_of), 1).astype(f32) == info[:, 0:1]
                ).astype(bf16)
                rows_ref[...] = jnp.dot(
                    place, parts[2 * i][...], preferred_element_type=f32
                ).astype(bf16)
                picked = jnp.dot(place, parts[2 * i + 1][...], preferred_element_type=f32)
                routed_ref[...] = (info[:, 1:2] * picked).astype(bf16)

    tok_rows_of = shards[0][2]
    in_specs = [pl.BlockSpec((1, cap, 2), lambda i, order: (order[i], 0, 0))]
    operands = [table]
    for tok, grad, height, tok_at, grad_at in shards:
        in_specs.append(pl.BlockSpec((height, width), lambda i, order, a=tok_at: (a, 0)))
        in_specs.append(pl.BlockSpec((height, width), lambda i, order, a=grad_at: (a, 0)))
        operands += [tok, grad]
    aliases = {}
    if rows is not None:
        aliases = {1 + len(operands): 0, 2 + len(operands): 1}
        in_specs += [pl.BlockSpec(memory_space=pl.ANY)] * 2
        operands += [rows, routed]
    n_slots = n_peers * cap
    shape = jax.ShapeDtypeStruct((n_slots, width), bf16)
    out_spec = pl.BlockSpec((cap, width), lambda i, order: (order[i], 0))
    return pl.pallas_call(
        body,
        out_shape=(shape, shape),
        grid_spec=pltpu.PrefetchScalarGridSpec(
            num_scalar_prefetch=1,
            grid=(count,),
            in_specs=in_specs,
            out_specs=(out_spec, out_spec),
        ),
        input_output_aliases=aliases,
        compiler_params=pltpu.CompilerParams(vmem_limit_bytes=KERNEL_VMEM),
        cost_estimate=pl.CostEstimate(
            flops=4 * count * cap * tok_rows_of * width,
            bytes_accessed=4 * count * (tok_rows_of + cap) * width,
            transcendentals=0,
        ),
        name="put_rows",
    )(order, *operands)


class Ring:
    def __init__(self):
        self.n_peers = lax.axis_size("expert")
        self.n = self.n_peers // 2
        self.far = self.n // 2
        self.names = [self.far]
        for d in range(self.far - 1, 0, -1):
            self.names += [d, -d]
        self.names.append(0)
        cycle = chip_cycle(self.n)
        spot = [cycle.index(c) for c in range(self.n)]
        chips = range(self.n)
        self.fwd = [(2 * cycle[i] + c, 2 * cycle[(i + 1) % self.n] + c) for i in chips for c in (0, 1)]
        self.bwd = [(b, a) for a, b in self.fwd]
        self.swap = [(i, i ^ 1) for i in range(self.n_peers)]
        table = np.zeros((self.n_peers, self.n_peers), np.int32)
        for e in range(self.n_peers):
            for core in (0, 1):
                for j, d in enumerate(self.names):
                    chip = cycle[(spot[e // 2] - d) % self.n]
                    table[e, core * self.n + j] = 2 * chip + (e % 2 if core else 1 - e % 2)
        self.order = jnp.asarray(table)[lax.axis_index("expert")]

    def at(self, distance, other):
        return self.names.index(distance) + (0 if other else self.n)

    def ahead(self, x):
        return lax.ppermute(x, "expert", self.fwd)

    def behind(self, x):
        return lax.ppermute(x, "expert", self.bwd)

    def other_core(self, x):
        return lax.ppermute(x, "expert", self.swap)


def gather_rows(ring, tokens, out_grad, table, cap, beside):
    tok_rows = tokens.shape[0]
    own = jnp.concatenate([tokens, out_grad], axis=0)
    beside = list(beside)

    def whole(x):
        return (x, x, tok_rows, 0, 1)

    def place(spots, shards, state):
        return put_rows(np.array(spots, np.int32), table, shards, *state, cap)

    state = (None, None)
    ahead, behind = own, own
    pending = ([ring.at(0, False), ring.at(0, True)], [whole(own), whole(ring.other_core(own))])
    marks = []
    for d in range(1, ring.far):
        ahead, behind = ring.ahead(ahead), ring.behind(behind)
        if d >= 2:
            state = place(*pending[0], state)
            pending = pending[1:]
            ahead, behind, state = lax.optimization_barrier((ahead, behind, state))
            if d - 2 < len(beside):
                ahead, behind, beside[d - 2] = lax.optimization_barrier(
                    (ahead, behind, beside[d - 2])
                )
        else:
            pending = [pending]
        marks.append((ahead, behind))
        pending.append(
            (
                [ring.at(d, False), ring.at(-d, False), ring.at(d, True), ring.at(-d, True)],
                [whole(x) for x in (ahead, behind, ring.other_core(ahead), ring.other_core(behind))],
            )
        )
    far_tok = ring.ahead(ahead[:tok_rows])
    far_grad = ring.behind(behind[tok_rows:])
    state = place(*pending[0], state)
    far_tok, far_grad, state = lax.optimization_barrier((far_tok, far_grad, state))
    marks.append((far_tok, far_grad))
    for spots, shards in pending[1:]:
        state = place(spots, shards, state)
    state = place(
        [ring.at(ring.far, False), ring.at(ring.far, True)],
        [
            (far_tok, far_grad, tok_rows, 0, 0),
            (ring.other_core(far_tok), ring.other_core(far_grad), tok_rows, 0, 0),
        ],
        state,
    )
    return state, marks, beside


def add_blocks(blocks, tok_rows, split, cols, joined=False):
    operands = [x for terms in blocks for x in terms]
    half = tok_rows // 2

    def body(*refs):
        outs, at = refs[len(operands) :], 0
        for i, terms in enumerate(blocks):
            for lower in (0, half):
                total = jnp.zeros((half, cols), f32)
                for j, (_, _, rows, first, _) in enumerate(terms):
                    if first <= lower < first + rows:
                        total += refs[at + j][lower - first : lower - first + half, :].astype(f32)
                if split:
                    outs[1 if lower else 0][...] = total.astype(bf16)
                elif joined:
                    outs[0][lower : lower + half, i * cols : (i + 1) * cols] = total.astype(bf16)
                else:
                    outs[i][lower : lower + half, :] = total.astype(bf16)
            at += len(terms)

    height, count = (half, 2) if split else (tok_rows, 1 if joined else len(blocks))
    wide = len(blocks) * cols if joined else cols
    out = pl.pallas_call(
        body,
        out_shape=[jax.ShapeDtypeStruct((height, wide), bf16)] * count,
        grid=(1,),
        in_specs=[
            pl.BlockSpec((rows, cols), lambda i, at=at, col=col: (at, col))
            for _, at, rows, _, col in operands
        ],
        out_specs=[pl.BlockSpec((height, wide), lambda i: (0, 0))] * count,
        compiler_params=pltpu.CompilerParams(vmem_limit_bytes=KERNEL_VMEM),
        cost_estimate=LIGHT,
        name="add_blocks",
    )(*[x[0] for x in operands])
    return list(out)


def sum_back(ring, handed, mine, tok_rows, between):
    width = mine[0].shape[1]
    cols, half = width // 2, tok_rows // 2

    def terms_of(h, own_pieces):
        terms, j = {}, 0
        for piece, own in zip(handed, own_pieces):
            for at in range(piece.shape[0] // tok_rows):
                terms[ring.names[j]] = [(x, at, tok_rows, 0, h) for x in (own, piece)]
                j += 1
        return terms

    def first(terms):
        top, low = add_blocks([terms[ring.far]], tok_rows, True, cols)
        return [(ring.ahead(top), 0, half, 0, 0), (ring.behind(low), 0, half, half, 0)]

    terms = [terms_of(0, mine)]
    (top, *at_top), (low, *at_low) = first(terms[0])
    mine, between, top, low = lax.optimization_barrier((mine, between, top, low))
    moving = [[(top, *at_top), (low, *at_low)]]
    terms.append(terms_of(1, mine))
    moving.append(first(terms[1]))
    for d in range(ring.far - 1, 0, -1):
        for h in (0, 1):
            ahead, behind = add_blocks(
                [terms[h][-d] + moving[h][:1], terms[h][d] + moving[h][1:]], tok_rows, False, cols
            )
            ahead, behind = ring.ahead(ahead), ring.behind(behind)
            moving[h] = [(ahead, 0, tok_rows, 0, 0), (behind, 0, tok_rows, 0, 0)]
    done = add_blocks([terms[h][0] + moving[h] for h in (0, 1)], tok_rows, False, cols, True)
    return done[0], between


def join_down(terms):
    low, width = terms[0].shape
    r = low // 4 if low % 64 == 0 else low

    def body(*refs):
        out = refs[0][...].astype(f32)
        for x in refs[1:-1]:
            out = out + x[...].astype(f32)
        refs[-1][...] = (grad_scale * out).astype(bf16)

    spec = pl.BlockSpec((r, width), lambda i: (i, 0))
    return pl.pallas_call(
        body,
        out_shape=jax.ShapeDtypeStruct((low, width), bf16),
        grid=(low // r,),
        in_specs=[spec] * len(terms),
        out_specs=spec,
        compiler_params=pltpu.CompilerParams(vmem_limit_bytes=KERNEL_VMEM),
        cost_estimate=LIGHT,
        name="join_down",
    )(*terms)


def blocks_per_step(n_blocks, cap):
    return max(b for b in range(1, n_blocks + 1) if n_blocks % b == 0 and b * cap <= 768)


def chunk_grads(order, cols, rows, routed, gate, up_mat, down_mat, start, piece):
    n_slots, width = rows.shape
    n_peers, cap, w = gate.shape
    n = blocks_per_step(n_peers, cap)
    r = n * cap
    n_rows, n_cols = n_slots // r, cols.shape[0]

    def body(order_ref, cols_ref, rows_ref, routed_ref, up_ref, down_ref, col_ref, *refs):
        gate_refs, (hidden_ref, both_ref, part_ref, held) = refs[:n], refs[n:]
        step = pl.program_id(0)

        @pl.when(step < n_rows)
        def _():
            up_all = jnp.dot(rows_ref[...], up_ref[...], preferred_element_type=f32)
            grad_all = dot(routed_ref[...], down_ref[...], ((1,), (1,)))
            for b in range(n):
                at = slice(b * cap, (b + 1) * cap)
                up_act, hidden_grad = up_all[at], grad_all[at]
                gate_val = gate_refs[b][0].astype(f32)
                gate_sig = jax.nn.sigmoid(gate_val)
                gate_act = gate_val * gate_sig
                hidden_ref[at, :] = (gate_act * up_act).astype(bf16)
                both_ref[at, w:] = (hidden_grad * gate_act).astype(bf16)
                both_ref[at, :w] = (
                    hidden_grad * up_act * gate_sig * (1.0 + gate_val * (1.0 - gate_sig))
                ).astype(bf16)
            held[pl.ds(pl.multiple_of(step * r, r), r), :] = both_ref[...]

        @pl.when(step >= n_rows)
        def _():
            part_ref[...] = dot(col_ref[...], held[...], ((0,), (0,))).astype(bf16)

    def row(i):
        return jnp.minimum(i, n_rows - 1)

    def col(i):
        return jnp.maximum(i - n_rows, 0)

    return pl.pallas_call(
        body,
        out_shape=(
            jax.ShapeDtypeStruct((n_slots, w), bf16),
            jax.ShapeDtypeStruct((n_slots, 2 * w), bf16),
            jax.ShapeDtypeStruct((n_cols * piece, 2 * w), bf16),
        ),
        grid_spec=pltpu.PrefetchScalarGridSpec(
            num_scalar_prefetch=2,
            grid=(n_rows + n_cols,),
            in_specs=[
                pl.BlockSpec((r, width), lambda i, order, cols: (row(i), 0)),
                pl.BlockSpec((r, width), lambda i, order, cols: (row(i), 0)),
                pl.BlockSpec((pl.Element(width), pl.Element(w)), lambda i, order, cols: (0, start)),
                pl.BlockSpec((pl.Element(w), pl.Element(width)), lambda i, order, cols: (start, 0)),
                pl.BlockSpec((n_slots, piece), lambda i, order, cols: (0, cols[col(i)])),
            ]
            + [
                pl.BlockSpec((1, cap, w), lambda i, order, cols, b=b: (order[n * row(i) + b], 0, 0))
                for b in range(n)
            ],
            out_specs=(
                pl.BlockSpec((r, w), lambda i, order, cols: (row(i), 0)),
                pl.BlockSpec((r, 2 * w), lambda i, order, cols: (row(i), 0)),
                pl.BlockSpec((piece, 2 * w), lambda i, order, cols: (col(i), 0)),
            ),
            scratch_shapes=[pltpu.VMEM((n_slots, 2 * w), bf16)],
        ),
        compiler_params=pltpu.CompilerParams(vmem_limit_bytes=KERNEL_VMEM),
        cost_estimate=LIGHT,
        name="chunk_grads",
    )(order, cols, rows, routed, up_mat, down_mat, rows, *[gate] * n)


def own_half(cols, rows, both, piece):
    n_slots = rows.shape[0]
    w = both.shape[1]

    def body(cols_ref, rows_ref, both_ref, own_ref):
        own_ref[...] = dot(rows_ref[...], both_ref[...], ((0,), (0,))).astype(bf16)

    return pl.pallas_call(
        body,
        out_shape=jax.ShapeDtypeStruct((piece, w), bf16),
        grid_spec=pltpu.PrefetchScalarGridSpec(
            num_scalar_prefetch=1,
            grid=(1,),
            in_specs=[
                pl.BlockSpec((n_slots, piece), lambda i, cols: (0, cols[0])),
                pl.BlockSpec((n_slots, w), lambda i, cols: (0, 0)),
            ],
            out_specs=pl.BlockSpec((piece, w), lambda i, cols: (0, 0)),
        ),
        compiler_params=pltpu.CompilerParams(vmem_limit_bytes=KERNEL_VMEM),
        cost_estimate=LIGHT,
        name="own_half",
    )(cols, rows, both)


def down_rows(order, routed, hidden_parts, starts):
    n_slots, width = routed.shape
    hidden_width = sum(x.shape[1] for x in hidden_parts)
    n_parts = order.shape[0]
    low = hidden_width // n_parts
    span = min(512, width)
    n_in = len(hidden_parts)

    def body(order_ref, routed_ref, *refs):
        turned, held = refs[-2:]

        @pl.when(pl.program_id(0) == 0)
        def _():
            for start, x in zip(starts, refs[:n_in]):
                turned[start : start + x.shape[1], :] = x[...].T

        held[...] = jnp.dot(turned[...], routed_ref[...], preferred_element_type=f32).astype(bf16)
        for d, out_ref in enumerate(refs[n_in:-2]):
            out_ref[...] = held[pl.ds(pl.multiple_of(order_ref[d] * low, 16), low), :]

    return pl.pallas_call(
        body,
        out_shape=[jax.ShapeDtypeStruct((low, width), bf16)] * n_parts,
        grid_spec=pltpu.PrefetchScalarGridSpec(
            num_scalar_prefetch=1,
            grid=(width // span,),
            in_specs=[pl.BlockSpec((n_slots, span), lambda i, order: (0, i))]
            + [pl.BlockSpec(x.shape, lambda i, order: (0, 0)) for x in hidden_parts],
            out_specs=[pl.BlockSpec((low, span), lambda i, order: (0, i))] * n_parts,
            scratch_shapes=[
                pltpu.VMEM((hidden_width, n_slots), bf16),
                pltpu.VMEM((hidden_width, span), bf16),
            ],
        ),
        compiler_params=pltpu.CompilerParams(vmem_limit_bytes=KERNEL_VMEM),
        cost_estimate=LIGHT,
        name="down_rows",
    )(order, routed, *hidden_parts)


def join_halves(own_parts, arrivals, starts, hidden_width):
    piece = own_parts[0].shape[0]
    r = min(128, piece)
    operands = [x for own, arrived in zip(own_parts, arrivals) for x in [own] + list(arrived)]
    each = len(operands) // len(own_parts)

    def body(*refs):
        gate_ref, up_ref = refs[-2:]
        for c, start in enumerate(starts):
            terms = refs[c * each : (c + 1) * each]
            w = terms[0].shape[1] // 2
            for at, out_ref in ((slice(0, w), gate_ref), (slice(w, 2 * w), up_ref)):
                total = terms[0][:, at].astype(f32)
                for x in terms[1:]:
                    total = total + x[:, at].astype(f32)
                out_ref[:, start : start + w] = (grad_scale * total).astype(bf16)

    shape = jax.ShapeDtypeStruct((piece, hidden_width), bf16)
    out_spec = pl.BlockSpec((r, hidden_width), lambda i: (i, 0))
    return pl.pallas_call(
        body,
        out_shape=(shape, shape),
        grid=(piece // r,),
        in_specs=[pl.BlockSpec((r, x.shape[1]), lambda i: (i, 0)) for x in operands],
        out_specs=(out_spec, out_spec),
        compiler_params=pltpu.CompilerParams(vmem_limit_bytes=KERNEL_VMEM),
        cost_estimate=LIGHT,
        name="join_halves",
    )(*operands)


def spread_back(parts, starts, gate_mat, up_mat, table, tok_rows, first, heights):
    n_peers, _, cap = table.shape
    half = n_peers // 2
    width, hidden_width = gate_mat.shape
    cols = min(512, width)
    rows = half * cap
    shift = 0 if first else 1
    owner = [(i, b) for i, height in enumerate(heights) for b in range(height)]

    def body(*refs):
        part_refs = refs[: len(parts)]
        gate_ref, up_ref, table_ref = refs[len(parts) : len(parts) + 3]
        out_refs = refs[len(parts) + 3 :]
        total = jnp.zeros((rows, cols), f32)
        for start, part_ref in zip(starts, part_refs):
            w = part_ref.shape[1] // 2
            total += dot(part_ref[:, :w], gate_ref[:, start : start + w], ((1,), (1,)))
            total += dot(part_ref[:, w:], up_ref[:, start : start + w], ((1,), (1,)))
        terms = total.astype(bf16)
        for j, (i, b) in enumerate(owner):
            tok = table_ref[j, 0:1, :]
            place = (lax.broadcasted_iota(i32, (tok_rows, cap), 0).astype(f32) == tok).astype(bf16)
            spread = jnp.dot(place, terms[j * cap : (j + 1) * cap], preferred_element_type=f32)
            out_refs[i][b * tok_rows : (b + 1) * tok_rows, :] = spread.astype(bf16)

    return pl.pallas_call(
        body,
        out_shape=[jax.ShapeDtypeStruct((h * tok_rows, width), bf16) for h in heights],
        grid=(width // cols,),
        in_specs=[pl.BlockSpec((rows, x.shape[1]), lambda j: (shift, 0)) for x in parts]
        + [
            pl.BlockSpec((cols, hidden_width), lambda j: (j, 0)),
            pl.BlockSpec((cols, hidden_width), lambda j: (j, 0)),
            pl.BlockSpec((half, 2, cap), lambda j: (shift, 0, 0)),
        ],
        out_specs=[pl.BlockSpec((h * tok_rows, cols), lambda j: (0, j)) for h in heights],
        compiler_params=pltpu.CompilerParams(vmem_limit_bytes=KERNEL_VMEM),
        cost_estimate=LIGHT,
        name="spread_back",
    )(*parts, gate_mat, up_mat, table)


def local(tokens, out_grad, gate_saved, probs, expert_ids, w_gate, w_up, w_down):
    n_peers = lax.axis_size("expert")
    n_dp = lax.axis_size("dp")
    group = lax.axis_index("dp")
    tok_rows, model_width = tokens.shape
    top_k = expert_ids.shape[1]
    hidden_width = w_up.shape[2]
    cap = min(tok_rows, 2 * tok_rows * top_k // n_peers)
    n_routes = tok_rows * top_k
    n_slots = n_peers * cap
    gate_mat, up_mat, down_mat = w_gate[0], w_up[0], w_down[0]

    experts = jnp.arange(n_peers, dtype=i32)
    hit = expert_ids[:, :, None] == experts[None, None, :]
    named = jnp.any(hit, axis=1)
    weight = jnp.sum(jnp.where(hit, probs[:, :, None], 0.0), axis=1)
    rank = jnp.cumsum(named.astype(i32), axis=0) - 1
    slots = jnp.arange(cap, dtype=i32)
    in_slot = named[:, :, None] & (rank[:, :, None] == slots[None, None, :])
    tok_of = jnp.sum(
        jnp.where(in_slot, jnp.arange(1, tok_rows + 1, dtype=f32)[:, None, None], 0.0), axis=0
    ) - 1.0
    choice = jnp.sum(jnp.where(hit, jnp.arange(top_k, dtype=f32)[None, :, None], 0.0), axis=1)
    choice_of = jnp.sum(jnp.where(in_slot, choice[:, :, None], 0.0), axis=0)
    weight_of = jnp.sum(jnp.where(in_slot, weight[:, :, None], 0.0), axis=0)
    table = lax.all_to_all(
        jnp.concatenate([tok_of, weight_of], axis=1),
        "expert",
        split_axis=0,
        concat_axis=0,
        tiled=True,
    )
    ring = Ring()
    table = table.reshape(n_peers, 2, cap)[ring.order]
    widths = chunk_widths(hidden_width)
    starts = [sum(widths[:i]) for i in range(len(widths))]
    route_gates = jnp.transpose(gate_saved, (1, 0, 2)).reshape(n_routes, hidden_width)
    route_of = (tok_of + tok_rows * choice_of).astype(i32).reshape(n_slots, 1)
    pick = (route_of == jnp.arange(n_routes, dtype=i32)[None, :]).astype(bf16)
    send_gate = [
        dot(pick, route_gates[:, s : s + w], ((1,), (0,))).astype(bf16).reshape(n_peers, cap, w)
        for s, w in zip(starts, widths)
    ]
    (rows_in, routed), marks, (send_gate[1:],) = gather_rows(
        ring, tokens, out_grad, table.transpose(0, 2, 1), cap, [send_gate[1:]]
    )

    def send_chunk(i, mark):
        part = send_gate[i]
        if mark is not None:
            part, _ = lax.optimization_barrier((part, mark))
        return lax.all_to_all(part, "expert", split_axis=0, concat_axis=0, tiled=True)

    recv_gate = [send_chunk(i, m) for i, m in zip(range(len(widths)), (None, marks[-1]))]

    piece = model_width // n_dp
    shifts = [[(i, (i + d) % n_dp) for i in range(n_dp)] for d in range(n_dp)]

    peer_cols = lax.rem(group + jnp.arange(1, n_dp, dtype=i32), n_dp)
    own_cols = group.reshape(1).astype(i32)
    both_parts, hidden_parts, arrivals, own_parts = [], [], [], []
    rows_now, routed_now = rows_in, routed
    for c, w in enumerate(widths):
        if c >= 2:
            for both in both_parts[len(own_parts) :]:
                own_parts.append(own_half(own_cols, rows_now, both, piece))
            rows_now, own_parts, arrivals[c - 2] = lax.optimization_barrier(
                (rows_now, own_parts, arrivals[c - 2])
            )
        hidden, both, sent = chunk_grads(
            ring.order,
            peer_cols,
            rows_now,
            routed_now,
            recv_gate[c],
            up_mat,
            down_mat,
            starts[c],
            piece,
        )
        both_parts.append(both)
        hidden_parts.append(hidden)
        arrivals.append(
            [
                lax.ppermute(sent[(d - 1) * piece : d * piece], "dp", shifts[d])
                for d in range(1, n_dp)
            ]
        )
        rows_now, routed_now, _ = lax.optimization_barrier((rows_now, routed_now, sent))
        if c + 2 < len(widths):
            recv_gate.append(send_chunk(c + 2, sent))

    heights = [1] + [2] * (ring.far - 1) + [1]
    theirs = spread_back(both_parts, starts, gate_mat, up_mat, table, tok_rows, True, heights)
    handed = [ring.other_core(x) for x in theirs]
    hidden_parts, _ = lax.optimization_barrier((hidden_parts, theirs))
    down_order = lax.rem(group + jnp.arange(n_dp, dtype=i32), n_dp)
    down, *sent = down_rows(down_order, routed_now, hidden_parts, starts)
    last, arrivals[:-1], sent = lax.optimization_barrier((both_parts[-1], arrivals[:-1], sent))
    mine = spread_back(
        both_parts[:-1] + [last], starts, gate_mat, up_mat, table, tok_rows, False, heights
    )
    parts, _ = lax.optimization_barrier((both_parts, mine))
    for both in parts[len(own_parts) :]:
        own_parts.append(own_half(own_cols, rows_now, both, piece))
    mine, handed = lax.optimization_barrier((mine, handed))
    input_grad, (own_parts, arrivals[-1], sent) = sum_back(
        ring, handed, mine, tok_rows, (own_parts, arrivals[-1], sent)
    )
    arrived = [lax.ppermute(part, "dp", shifts[d]) for d, part in enumerate(sent, 1)]
    own_parts, _ = lax.optimization_barrier((own_parts, input_grad))
    grad_gate, grad_up = join_halves(own_parts, arrivals, starts, hidden_width)
    arrived, grad_gate = lax.optimization_barrier((arrived, grad_gate))
    grad_down = join_down([down] + arrived)[None]
    return (input_grad, grad_gate[None], grad_up[None], grad_down)


def solution(mesh):
    return jax.shard_map(
        local,
        mesh=mesh,
        in_specs=(
            P(("dp", "expert"), None),
            P(("dp", "expert"), None),
            P(("dp", "expert"), None, None),
            P(("dp", "expert"), None),
            P(("dp", "expert"), None),
            P("expert", None, None),
            P("expert", None, None),
            P("expert", None, None),
        ),
        out_specs=(
            P(("dp", "expert"), None),
            P("expert", "dp", None),
            P("expert", "dp", None),
            P("expert", "dp", None),
        ),
        check_vma=False,
    )
```

```python
import jax
import jax.numpy as jnp
import numpy as np
from jax import lax
from jax.experimental import pallas as pl
from jax.experimental.pallas import tpu as pltpu
from jax.sharding import PartitionSpec as P

grad_scale = 0.0625
f32 = jnp.float32
bf16 = jnp.bfloat16
i32 = jnp.int32
KERNEL_VMEM = 60 * 1024 * 1024
LIGHT = pl.CostEstimate(flops=1000, bytes_accessed=1000, transcendentals=0)


def dot(a, b, dims):
    return lax.dot_general(a, b, (dims, ((), ())), preferred_element_type=f32)


def chunk_widths(width):
    lanes = width // 128
    shares = (3, 7, 11)
    ends = [-(-lanes * x // 11) * 128 for x in shares]
    return [e - s for s, e in zip([0] + ends, ends) if e > s]


def chip_cycle(n_chips):
    cols = n_chips // 4
    if n_chips % 4 or cols < 2:
        return list(range(n_chips))
    walk = [(row, 0) for row in range(4)]
    for step, row in enumerate((3, 2, 1, 0)):
        across = range(1, cols) if step % 2 == 0 else range(cols - 1, 0, -1)
        walk += [(row, col) for col in across]
    return [row * cols + col for row, col in walk]


def put_rows(order, table, shards, rows, routed, cap):
    count = len(shards)
    n_peers, _, _ = table.shape
    width = shards[0][0].shape[1]

    def body(order_ref, table_ref, *refs):
        parts = refs[: 2 * count]
        rows_ref, routed_ref = refs[-2:]
        step = pl.program_id(0)
        for i in range(count):

            @pl.when(step == i)
            def _():
                info = table_ref[0]
                place = (
                    lax.broadcasted_iota(i32, (cap, tok_rows_of), 1).astype(f32) == info[:, 0:1]
                ).astype(bf16)
                rows_ref[...] = jnp.dot(
                    place, parts[2 * i][...], preferred_element_type=f32
                ).astype(bf16)
                picked = jnp.dot(place, parts[2 * i + 1][...], preferred_element_type=f32)
                routed_ref[...] = (info[:, 1:2] * picked).astype(bf16)

    tok_rows_of = shards[0][2]
    in_specs = [pl.BlockSpec((1, cap, 2), lambda i, order: (order[i], 0, 0))]
    operands = [table]
    for tok, grad, height, tok_at, grad_at in shards:
        in_specs.append(pl.BlockSpec((height, width), lambda i, order, a=tok_at: (a, 0)))
        in_specs.append(pl.BlockSpec((height, width), lambda i, order, a=grad_at: (a, 0)))
        operands += [tok, grad]
    aliases = {}
    if rows is not None:
        aliases = {1 + len(operands): 0, 2 + len(operands): 1}
        in_specs += [pl.BlockSpec(memory_space=pl.ANY)] * 2
        operands += [rows, routed]
    n_slots = n_peers * cap
    shape = jax.ShapeDtypeStruct((n_slots, width), bf16)
    out_spec = pl.BlockSpec((cap, width), lambda i, order: (order[i], 0))
    return pl.pallas_call(
        body,
        out_shape=(shape, shape),
        grid_spec=pltpu.PrefetchScalarGridSpec(
            num_scalar_prefetch=1,
            grid=(count,),
            in_specs=in_specs,
            out_specs=(out_spec, out_spec),
        ),
        input_output_aliases=aliases,
        compiler_params=pltpu.CompilerParams(vmem_limit_bytes=KERNEL_VMEM),
        cost_estimate=pl.CostEstimate(
            flops=4 * count * cap * tok_rows_of * width,
            bytes_accessed=4 * count * (tok_rows_of + cap) * width,
            transcendentals=0,
        ),
        name="put_rows",
    )(order, *operands)


class Ring:
    def __init__(self):
        self.n_peers = lax.axis_size("expert")
        self.n = self.n_peers // 2
        self.far = self.n // 2
        self.names = [self.far]
        for d in range(self.far - 1, 0, -1):
            self.names += [d, -d]
        self.names.append(0)
        cycle = chip_cycle(self.n)
        spot = [cycle.index(c) for c in range(self.n)]
        chips = range(self.n)
        self.fwd = [(2 * cycle[i] + c, 2 * cycle[(i + 1) % self.n] + c) for i in chips for c in (0, 1)]
        self.bwd = [(b, a) for a, b in self.fwd]
        self.swap = [(i, i ^ 1) for i in range(self.n_peers)]
        table = np.zeros((self.n_peers, self.n_peers), np.int32)
        for e in range(self.n_peers):
            for core in (0, 1):
                for j, d in enumerate(self.names):
                    chip = cycle[(spot[e // 2] - d) % self.n]
                    table[e, core * self.n + j] = 2 * chip + (e % 2 if core else 1 - e % 2)
        self.order = jnp.asarray(table)[lax.axis_index("expert")]

    def at(self, distance, other):
        return self.names.index(distance) + (0 if other else self.n)

    def ahead(self, x):
        return lax.ppermute(x, "expert", self.fwd)

    def behind(self, x):
        return lax.ppermute(x, "expert", self.bwd)

    def other_core(self, x):
        return lax.ppermute(x, "expert", self.swap)


def gather_rows(ring, tokens, out_grad, table, cap, beside):
    tok_rows = tokens.shape[0]
    own = jnp.concatenate([tokens, out_grad], axis=0)
    beside = list(beside)

    def whole(x):
        return (x, x, tok_rows, 0, 1)

    def place(spots, shards, state):
        return put_rows(np.array(spots, np.int32), table, shards, *state, cap)

    state = (None, None)
    ahead, behind = own, own
    pending = ([ring.at(0, False), ring.at(0, True)], [whole(own), whole(ring.other_core(own))])
    marks = []
    for d in range(1, ring.far):
        ahead, behind = ring.ahead(ahead), ring.behind(behind)
        if d >= 2:
            state = place(*pending[0], state)
            pending = pending[1:]
            ahead, behind, state = lax.optimization_barrier((ahead, behind, state))
            if d - 2 < len(beside):
                ahead, behind, beside[d - 2] = lax.optimization_barrier(
                    (ahead, behind, beside[d - 2])
                )
        else:
            pending = [pending]
        marks.append((ahead, behind))
        pending.append(
            (
                [ring.at(d, False), ring.at(-d, False), ring.at(d, True), ring.at(-d, True)],
                [whole(x) for x in (ahead, behind, ring.other_core(ahead), ring.other_core(behind))],
            )
        )
    far_tok = ring.ahead(ahead[:tok_rows])
    far_grad = ring.behind(behind[tok_rows:])
    state = place(*pending[0], state)
    far_tok, far_grad, state = lax.optimization_barrier((far_tok, far_grad, state))
    marks.append((far_tok, far_grad))
    for spots, shards in pending[1:]:
        state = place(spots, shards, state)
    state = place(
        [ring.at(ring.far, False), ring.at(ring.far, True)],
        [
            (far_tok, far_grad, tok_rows, 0, 0),
            (ring.other_core(far_tok), ring.other_core(far_grad), tok_rows, 0, 0),
        ],
        state,
    )
    return state, marks, beside


def add_blocks(blocks, tok_rows, split, cols, joined=False):
    operands = [x for terms in blocks for x in terms]
    half = tok_rows // 2

    def body(*refs):
        outs, at = refs[len(operands) :], 0
        for i, terms in enumerate(blocks):
            for lower in (0, half):
                total = jnp.zeros((half, cols), f32)
                for j, (_, _, rows, first, _) in enumerate(terms):
                    if first <= lower < first + rows:
                        total += refs[at + j][lower - first : lower - first + half, :].astype(f32)
                if split:
                    outs[1 if lower else 0][...] = total.astype(bf16)
                elif joined:
                    outs[0][lower : lower + half, i * cols : (i + 1) * cols] = total.astype(bf16)
                else:
                    outs[i][lower : lower + half, :] = total.astype(bf16)
            at += len(terms)

    height, count = (half, 2) if split else (tok_rows, 1 if joined else len(blocks))
    wide = len(blocks) * cols if joined else cols
    out = pl.pallas_call(
        body,
        out_shape=[jax.ShapeDtypeStruct((height, wide), bf16)] * count,
        grid=(1,),
        in_specs=[
            pl.BlockSpec((rows, cols), lambda i, at=at, col=col: (at, col))
            for _, at, rows, _, col in operands
        ],
        out_specs=[pl.BlockSpec((height, wide), lambda i: (0, 0))] * count,
        compiler_params=pltpu.CompilerParams(vmem_limit_bytes=KERNEL_VMEM),
        cost_estimate=LIGHT,
        name="add_blocks",
    )(*[x[0] for x in operands])
    return list(out)


def sum_back(ring, handed, mine, tok_rows, between):
    width = mine[0].shape[1]
    cols, half = width // 2, tok_rows // 2

    def terms_of(h, own_pieces):
        terms, j = {}, 0
        for piece, own in zip(handed, own_pieces):
            for at in range(piece.shape[0] // tok_rows):
                terms[ring.names[j]] = [(x, at, tok_rows, 0, h) for x in (own, piece)]
                j += 1
        return terms

    def first(terms):
        top, low = add_blocks([terms[ring.far]], tok_rows, True, cols)
        return [(ring.ahead(top), 0, half, 0, 0), (ring.behind(low), 0, half, half, 0)]

    terms = [terms_of(0, mine)]
    (top, *at_top), (low, *at_low) = first(terms[0])
    mine, between, top, low = lax.optimization_barrier((mine, between, top, low))
    moving = [[(top, *at_top), (low, *at_low)]]
    terms.append(terms_of(1, mine))
    moving.append(first(terms[1]))
    for d in range(ring.far - 1, 0, -1):
        for h in (0, 1):
            ahead, behind = add_blocks(
                [terms[h][-d] + moving[h][:1], terms[h][d] + moving[h][1:]], tok_rows, False, cols
            )
            ahead, behind = ring.ahead(ahead), ring.behind(behind)
            moving[h] = [(ahead, 0, tok_rows, 0, 0), (behind, 0, tok_rows, 0, 0)]
    done = add_blocks([terms[h][0] + moving[h] for h in (0, 1)], tok_rows, False, cols, True)
    return done[0], between


def join_down(terms, piece, total):
    low, width = terms[0].shape
    r = low // 2 if low % 32 == 0 else low
    steps = low // r
    aliased = [] if total is None else [total]

    def body(*refs):
        out = refs[0][...].astype(f32)
        for x in refs[1 : len(terms)]:
            out = out + x[...].astype(f32)
        refs[-1][...] = (grad_scale * out).astype(bf16)

    return pl.pallas_call(
        body,
        out_shape=jax.ShapeDtypeStruct((2 * low, width), bf16),
        grid=(steps,),
        in_specs=[pl.BlockSpec((r, width), lambda i: (i, 0))] * len(terms)
        + [pl.BlockSpec(memory_space=pl.ANY) for _ in aliased],
        out_specs=pl.BlockSpec((r, width), lambda i: (piece * steps + i, 0)),
        input_output_aliases={len(terms): 0} if aliased else {},
        compiler_params=pltpu.CompilerParams(vmem_limit_bytes=KERNEL_VMEM),
        cost_estimate=LIGHT,
        name="join_down",
    )(*terms, *aliased)


def blocks_per_step(n_blocks, cap):
    return max(b for b in range(1, n_blocks + 1) if n_blocks % b == 0 and b * cap <= 768)


def chunk_grads(order, cols, rows, routed, gate, up_mat, down_mat, start, piece):
    n_slots, width = rows.shape
    n_peers, cap, w = gate.shape
    n = blocks_per_step(n_peers, cap)
    r = n * cap
    n_rows, n_cols = n_slots // r, cols.shape[0]

    def body(order_ref, cols_ref, rows_ref, routed_ref, up_ref, down_ref, col_ref, *refs):
        gate_refs, (hidden_ref, both_ref, part_ref, held) = refs[:n], refs[n:]
        step = pl.program_id(0)

        @pl.when(step < n_rows)
        def _():
            up_all = jnp.dot(rows_ref[...], up_ref[...], preferred_element_type=f32)
            grad_all = dot(routed_ref[...], down_ref[...], ((1,), (1,)))
            for b in range(n):
                at = slice(b * cap, (b + 1) * cap)
                up_act, hidden_grad = up_all[at], grad_all[at]
                gate_val = gate_refs[b][0].astype(f32)
                gate_sig = jax.nn.sigmoid(gate_val)
                gate_act = gate_val * gate_sig
                hidden_ref[at, :] = (gate_act * up_act).astype(bf16)
                both_ref[at, w:] = (hidden_grad * gate_act).astype(bf16)
                both_ref[at, :w] = (
                    hidden_grad * up_act * gate_sig * (1.0 + gate_val * (1.0 - gate_sig))
                ).astype(bf16)
            held[pl.ds(pl.multiple_of(step * r, r), r), :] = both_ref[...]

        @pl.when(step >= n_rows)
        def _():
            part_ref[...] = dot(col_ref[...], held[...], ((0,), (0,))).astype(bf16)

    def row(i):
        return jnp.minimum(i, n_rows - 1)

    def col(i):
        return jnp.maximum(i - n_rows, 0)

    return pl.pallas_call(
        body,
        out_shape=(
            jax.ShapeDtypeStruct((n_slots, w), bf16),
            jax.ShapeDtypeStruct((n_slots, 2 * w), bf16),
            jax.ShapeDtypeStruct((n_cols * piece, 2 * w), bf16),
        ),
        grid_spec=pltpu.PrefetchScalarGridSpec(
            num_scalar_prefetch=2,
            grid=(n_rows + n_cols,),
            in_specs=[
                pl.BlockSpec((r, width), lambda i, order, cols: (row(i), 0)),
                pl.BlockSpec((r, width), lambda i, order, cols: (row(i), 0)),
                pl.BlockSpec((pl.Element(width), pl.Element(w)), lambda i, order, cols: (0, start)),
                pl.BlockSpec((pl.Element(w), pl.Element(width)), lambda i, order, cols: (start, 0)),
                pl.BlockSpec((n_slots, piece), lambda i, order, cols: (0, cols[col(i)])),
            ]
            + [
                pl.BlockSpec((1, cap, w), lambda i, order, cols, b=b: (order[n * row(i) + b], 0, 0))
                for b in range(n)
            ],
            out_specs=(
                pl.BlockSpec((r, w), lambda i, order, cols: (row(i), 0)),
                pl.BlockSpec((r, 2 * w), lambda i, order, cols: (row(i), 0)),
                pl.BlockSpec((piece, 2 * w), lambda i, order, cols: (col(i), 0)),
            ),
            scratch_shapes=[pltpu.VMEM((n_slots, 2 * w), bf16)],
        ),
        compiler_params=pltpu.CompilerParams(vmem_limit_bytes=KERNEL_VMEM),
        cost_estimate=LIGHT,
        name="chunk_grads",
    )(order, cols, rows, routed, up_mat, down_mat, rows, *[gate] * n)


def own_half(cols, rows, both, piece):
    n_slots = rows.shape[0]
    w = both.shape[1]

    def body(cols_ref, rows_ref, both_ref, own_ref):
        own_ref[...] = dot(rows_ref[...], both_ref[...], ((0,), (0,))).astype(bf16)

    return pl.pallas_call(
        body,
        out_shape=jax.ShapeDtypeStruct((piece, w), bf16),
        grid_spec=pltpu.PrefetchScalarGridSpec(
            num_scalar_prefetch=1,
            grid=(1,),
            in_specs=[
                pl.BlockSpec((n_slots, piece), lambda i, cols: (0, cols[0])),
                pl.BlockSpec((n_slots, w), lambda i, cols: (0, 0)),
            ],
            out_specs=pl.BlockSpec((piece, w), lambda i, cols: (0, 0)),
        ),
        compiler_params=pltpu.CompilerParams(vmem_limit_bytes=KERNEL_VMEM),
        cost_estimate=LIGHT,
        name="own_half",
    )(cols, rows, both)


def down_rows(order, routed, hidden_parts, starts):
    n_slots, width = routed.shape
    hidden_width = sum(x.shape[1] for x in hidden_parts)
    n_parts = order.shape[0]
    n_parts, low = 2 * n_parts, hidden_width // (2 * n_parts)
    span = min(512, width)
    n_in = len(hidden_parts)

    def body(order_ref, routed_ref, *refs):
        turned, held = refs[-2:]

        @pl.when(pl.program_id(0) == 0)
        def _():
            for start, x in zip(starts, refs[:n_in]):
                turned[start : start + x.shape[1], :] = x[...].T

        held[...] = jnp.dot(turned[...], routed_ref[...], preferred_element_type=f32).astype(bf16)
        for d, out_ref in enumerate(refs[n_in:-2]):
            out_ref[...] = held[
                pl.ds(pl.multiple_of((2 * order_ref[d // 2] + d % 2) * low, 16), low), :
            ]

    return pl.pallas_call(
        body,
        out_shape=[jax.ShapeDtypeStruct((low, width), bf16)] * n_parts,
        grid_spec=pltpu.PrefetchScalarGridSpec(
            num_scalar_prefetch=1,
            grid=(width // span,),
            in_specs=[pl.BlockSpec((n_slots, span), lambda i, order: (0, i))]
            + [pl.BlockSpec(x.shape, lambda i, order: (0, 0)) for x in hidden_parts],
            out_specs=[pl.BlockSpec((low, span), lambda i, order: (0, i))] * n_parts,
            scratch_shapes=[
                pltpu.VMEM((hidden_width, n_slots), bf16),
                pltpu.VMEM((hidden_width, span), bf16),
            ],
        ),
        compiler_params=pltpu.CompilerParams(vmem_limit_bytes=KERNEL_VMEM),
        cost_estimate=LIGHT,
        name="down_rows",
    )(order, routed, *hidden_parts)


def join_halves(own_parts, arrivals, starts, hidden_width):
    piece = own_parts[0].shape[0]
    r = min(128, piece)
    operands = [x for own, arrived in zip(own_parts, arrivals) for x in [own] + list(arrived)]
    each = len(operands) // len(own_parts)

    def body(*refs):
        gate_ref, up_ref = refs[-2:]
        for c, start in enumerate(starts):
            terms = refs[c * each : (c + 1) * each]
            w = terms[0].shape[1] // 2
            for at, out_ref in ((slice(0, w), gate_ref), (slice(w, 2 * w), up_ref)):
                total = terms[0][:, at].astype(f32)
                for x in terms[1:]:
                    total = total + x[:, at].astype(f32)
                out_ref[:, start : start + w] = (grad_scale * total).astype(bf16)

    shape = jax.ShapeDtypeStruct((piece, hidden_width), bf16)
    out_spec = pl.BlockSpec((r, hidden_width), lambda i: (i, 0))
    return pl.pallas_call(
        body,
        out_shape=(shape, shape),
        grid=(piece // r,),
        in_specs=[pl.BlockSpec((r, x.shape[1]), lambda i: (i, 0)) for x in operands],
        out_specs=(out_spec, out_spec),
        compiler_params=pltpu.CompilerParams(vmem_limit_bytes=KERNEL_VMEM),
        cost_estimate=LIGHT,
        name="join_halves",
    )(*operands)


def spread_back(parts, starts, gate_mat, up_mat, table, tok_rows, first, heights):
    n_peers, _, cap = table.shape
    half = n_peers // 2
    width, hidden_width = gate_mat.shape
    cols = min(512, width)
    rows = half * cap
    shift = 0 if first else 1
    owner = [(i, b) for i, height in enumerate(heights) for b in range(height)]

    def body(*refs):
        part_refs = refs[: len(parts)]
        gate_ref, up_ref, table_ref = refs[len(parts) : len(parts) + 3]
        out_refs = refs[len(parts) + 3 :]
        total = jnp.zeros((rows, cols), f32)
        for start, part_ref in zip(starts, part_refs):
            w = part_ref.shape[1] // 2
            total += dot(part_ref[:, :w], gate_ref[:, start : start + w], ((1,), (1,)))
            total += dot(part_ref[:, w:], up_ref[:, start : start + w], ((1,), (1,)))
        terms = total.astype(bf16)
        for j, (i, b) in enumerate(owner):
            tok = table_ref[j, 0:1, :]
            place = (lax.broadcasted_iota(i32, (tok_rows, cap), 0).astype(f32) == tok).astype(bf16)
            spread = jnp.dot(place, terms[j * cap : (j + 1) * cap], preferred_element_type=f32)
            out_refs[i][b * tok_rows : (b + 1) * tok_rows, :] = spread.astype(bf16)

    return pl.pallas_call(
        body,
        out_shape=[jax.ShapeDtypeStruct((h * tok_rows, width), bf16) for h in heights],
        grid=(width // cols,),
        in_specs=[pl.BlockSpec((rows, x.shape[1]), lambda j: (shift, 0)) for x in parts]
        + [
            pl.BlockSpec((cols, hidden_width), lambda j: (j, 0)),
            pl.BlockSpec((cols, hidden_width), lambda j: (j, 0)),
            pl.BlockSpec((half, 2, cap), lambda j: (shift, 0, 0)),
        ],
        out_specs=[pl.BlockSpec((h * tok_rows, cols), lambda j: (0, j)) for h in heights],
        compiler_params=pltpu.CompilerParams(vmem_limit_bytes=KERNEL_VMEM),
        cost_estimate=LIGHT,
        name="spread_back",
    )(*parts, gate_mat, up_mat, table)


def local(tokens, out_grad, gate_saved, probs, expert_ids, w_gate, w_up, w_down):
    n_peers = lax.axis_size("expert")
    n_dp = lax.axis_size("dp")
    group = lax.axis_index("dp")
    tok_rows, model_width = tokens.shape
    top_k = expert_ids.shape[1]
    hidden_width = w_up.shape[2]
    cap = min(tok_rows, 2 * tok_rows * top_k // n_peers)
    n_routes = tok_rows * top_k
    n_slots = n_peers * cap
    gate_mat, up_mat, down_mat = w_gate[0], w_up[0], w_down[0]

    experts = jnp.arange(n_peers, dtype=i32)
    hit = expert_ids[:, :, None] == experts[None, None, :]
    named = jnp.any(hit, axis=1)
    weight = jnp.sum(jnp.where(hit, probs[:, :, None], 0.0), axis=1)
    rank = jnp.cumsum(named.astype(i32), axis=0) - 1
    slots = jnp.arange(cap, dtype=i32)
    in_slot = named[:, :, None] & (rank[:, :, None] == slots[None, None, :])
    tok_of = jnp.sum(
        jnp.where(in_slot, jnp.arange(1, tok_rows + 1, dtype=f32)[:, None, None], 0.0), axis=0
    ) - 1.0
    choice = jnp.sum(jnp.where(hit, jnp.arange(top_k, dtype=f32)[None, :, None], 0.0), axis=1)
    choice_of = jnp.sum(jnp.where(in_slot, choice[:, :, None], 0.0), axis=0)
    weight_of = jnp.sum(jnp.where(in_slot, weight[:, :, None], 0.0), axis=0)
    table = lax.all_to_all(
        jnp.concatenate([tok_of, weight_of], axis=1),
        "expert",
        split_axis=0,
        concat_axis=0,
        tiled=True,
    )
    ring = Ring()
    table = table.reshape(n_peers, 2, cap)[ring.order]
    widths = chunk_widths(hidden_width)
    starts = [sum(widths[:i]) for i in range(len(widths))]
    route_gates = jnp.transpose(gate_saved, (1, 0, 2)).reshape(n_routes, hidden_width)
    route_of = (tok_of + tok_rows * choice_of).astype(i32).reshape(n_slots, 1)
    pick = (route_of == jnp.arange(n_routes, dtype=i32)[None, :]).astype(bf16)
    send_gate = [
        dot(pick, route_gates[:, s : s + w], ((1,), (0,))).astype(bf16).reshape(n_peers, cap, w)
        for s, w in zip(starts, widths)
    ]
    (rows_in, routed), marks, (send_gate[1:],) = gather_rows(
        ring, tokens, out_grad, table.transpose(0, 2, 1), cap, [send_gate[1:]]
    )

    def send_chunk(i, mark):
        part = send_gate[i]
        if mark is not None:
            part, _ = lax.optimization_barrier((part, mark))
        return lax.all_to_all(part, "expert", split_axis=0, concat_axis=0, tiled=True)

    recv_gate = [send_chunk(i, m) for i, m in zip(range(len(widths)), (None, marks[-1]))]

    piece = model_width // n_dp
    shifts = [[(i, (i + d) % n_dp) for i in range(n_dp)] for d in range(n_dp)]

    peer_cols = lax.rem(group + jnp.arange(1, n_dp, dtype=i32), n_dp)
    own_cols = group.reshape(1).astype(i32)
    both_parts, hidden_parts, arrivals, own_parts = [], [], [], []
    rows_now, routed_now = rows_in, routed
    for c, w in enumerate(widths):
        if c >= 2:
            for both in both_parts[len(own_parts) :]:
                own_parts.append(own_half(own_cols, rows_now, both, piece))
            rows_now, own_parts, arrivals[c - 2] = lax.optimization_barrier(
                (rows_now, own_parts, arrivals[c - 2])
            )
        hidden, both, sent = chunk_grads(
            ring.order,
            peer_cols,
            rows_now,
            routed_now,
            recv_gate[c],
            up_mat,
            down_mat,
            starts[c],
            piece,
        )
        both_parts.append(both)
        hidden_parts.append(hidden)
        arrivals.append(
            [
                lax.ppermute(sent[(d - 1) * piece : d * piece], "dp", shifts[d])
                for d in range(1, n_dp)
            ]
        )
        rows_now, routed_now, _ = lax.optimization_barrier((rows_now, routed_now, sent))
        if c + 2 < len(widths):
            recv_gate.append(send_chunk(c + 2, sent))

    heights = [1] + [2] * (ring.far - 1) + [1]
    theirs = spread_back(both_parts, starts, gate_mat, up_mat, table, tok_rows, True, heights)
    handed = [ring.other_core(x) for x in theirs]
    hidden_parts, _ = lax.optimization_barrier((hidden_parts, theirs))
    down_order = lax.rem(group + jnp.arange(n_dp, dtype=i32), n_dp)
    sent = down_rows(down_order, routed_now, hidden_parts, starts)
    own_down, sent = sent[:2], sent[2:]
    last, arrivals[:-1], sent = lax.optimization_barrier((both_parts[-1], arrivals[:-1], sent))
    mine = spread_back(
        both_parts[:-1] + [last], starts, gate_mat, up_mat, table, tok_rows, False, heights
    )
    parts, _ = lax.optimization_barrier((both_parts, mine))
    for both in parts[len(own_parts) :]:
        own_parts.append(own_half(own_cols, rows_now, both, piece))
    mine, handed = lax.optimization_barrier((mine, handed))
    input_grad, (own_parts, arrivals[-1], sent) = sum_back(
        ring, handed, mine, tok_rows, (own_parts, arrivals[-1], sent)
    )
    arrived = [lax.ppermute(part, "dp", shifts[1 + i // 2]) for i, part in enumerate(sent)]
    own_parts, _ = lax.optimization_barrier((own_parts, input_grad))
    grad_gate, grad_up = join_halves(own_parts, arrivals, starts, hidden_width)
    arrived[::2], grad_gate = lax.optimization_barrier((arrived[::2], grad_gate))
    grad_down = None
    for k in (0, 1):
        grad_down = join_down([own_down[k]] + arrived[k::2], k, grad_down)
        if k == 0:
            grad_down, arrived[1::2] = lax.optimization_barrier((grad_down, arrived[1::2]))
    grad_down = grad_down[None]
    return (input_grad, grad_gate[None], grad_up[None], grad_down)


def solution(mesh):
    return jax.shard_map(
        local,
        mesh=mesh,
        in_specs=(
            P(("dp", "expert"), None),
            P(("dp", "expert"), None),
            P(("dp", "expert"), None, None),
            P(("dp", "expert"), None),
            P(("dp", "expert"), None),
            P("expert", None, None),
            P("expert", None, None),
            P("expert", None, None),
        ),
        out_specs=(
            P(("dp", "expert"), None),
            P("expert", "dp", None),
            P("expert", "dp", None),
            P("expert", "dp", None),
        ),
        check_vma=False,
    )
```

```python
import jax
import jax.numpy as jnp
import numpy as np
from jax import lax
from jax.experimental import pallas as pl
from jax.experimental.pallas import tpu as pltpu
from jax.sharding import PartitionSpec as P

grad_scale = 0.0625
f32 = jnp.float32
bf16 = jnp.bfloat16
i32 = jnp.int32
KERNEL_VMEM = 60 * 1024 * 1024
LIGHT = pl.CostEstimate(flops=1000, bytes_accessed=1000, transcendentals=0)


def dot(a, b, dims):
    return lax.dot_general(a, b, (dims, ((), ())), preferred_element_type=f32)


def chunk_widths(width):
    lanes = width // 128
    shares = (2, 6, 11)
    ends = [-(-lanes * x // 11) * 128 for x in shares]
    return [e - s for s, e in zip([0] + ends, ends) if e > s]


def chip_cycle(n_chips):
    cols = n_chips // 4
    if n_chips % 4 or cols < 2:
        return list(range(n_chips))
    walk = [(row, 0) for row in range(4)]
    for step, row in enumerate((3, 2, 1, 0)):
        across = range(1, cols) if step % 2 == 0 else range(cols - 1, 0, -1)
        walk += [(row, col) for col in across]
    return [row * cols + col for row, col in walk]


def put_rows(order, table, shards, rows, routed, cap):
    count = len(shards)
    n_peers, _, _ = table.shape
    width = shards[0][0].shape[1]

    def body(order_ref, table_ref, *refs):
        parts = refs[: 2 * count]
        rows_ref, routed_ref = refs[-2:]
        step = pl.program_id(0)
        for i in range(count):

            @pl.when(step == i)
            def _():
                info = table_ref[0]
                place = (
                    lax.broadcasted_iota(i32, (cap, tok_rows_of), 1).astype(f32) == info[:, 0:1]
                ).astype(bf16)
                rows_ref[...] = jnp.dot(
                    place, parts[2 * i][...], preferred_element_type=f32
                ).astype(bf16)
                picked = jnp.dot(place, parts[2 * i + 1][...], preferred_element_type=f32)
                routed_ref[...] = (info[:, 1:2] * picked).astype(bf16)

    tok_rows_of = shards[0][2]
    in_specs = [pl.BlockSpec((1, cap, 2), lambda i, order: (order[i], 0, 0))]
    operands = [table]
    for tok, grad, height, tok_at, grad_at in shards:
        in_specs.append(pl.BlockSpec((height, width), lambda i, order, a=tok_at: (a, 0)))
        in_specs.append(pl.BlockSpec((height, width), lambda i, order, a=grad_at: (a, 0)))
        operands += [tok, grad]
    aliases = {}
    if rows is not None:
        aliases = {1 + len(operands): 0, 2 + len(operands): 1}
        in_specs += [pl.BlockSpec(memory_space=pl.ANY)] * 2
        operands += [rows, routed]
    n_slots = n_peers * cap
    shape = jax.ShapeDtypeStruct((n_slots, width), bf16)
    out_spec = pl.BlockSpec((cap, width), lambda i, order: (order[i], 0))
    return pl.pallas_call(
        body,
        out_shape=(shape, shape),
        grid_spec=pltpu.PrefetchScalarGridSpec(
            num_scalar_prefetch=1,
            grid=(count,),
            in_specs=in_specs,
            out_specs=(out_spec, out_spec),
        ),
        input_output_aliases=aliases,
        compiler_params=pltpu.CompilerParams(vmem_limit_bytes=KERNEL_VMEM),
        cost_estimate=pl.CostEstimate(
            flops=4 * count * cap * tok_rows_of * width,
            bytes_accessed=4 * count * (tok_rows_of + cap) * width,
            transcendentals=0,
        ),
        name="put_rows",
    )(order, *operands)


class Ring:
    def __init__(self):
        self.n_peers = lax.axis_size("expert")
        self.n = self.n_peers // 2
        self.far = self.n // 2
        self.names = [self.far]
        for d in range(self.far - 1, 0, -1):
            self.names += [d, -d]
        self.names.append(0)
        cycle = chip_cycle(self.n)
        spot = [cycle.index(c) for c in range(self.n)]
        chips = range(self.n)
        self.fwd = [(2 * cycle[i] + c, 2 * cycle[(i + 1) % self.n] + c) for i in chips for c in (0, 1)]
        self.bwd = [(b, a) for a, b in self.fwd]
        self.swap = [(i, i ^ 1) for i in range(self.n_peers)]
        table = np.zeros((self.n_peers, self.n_peers), np.int32)
        for e in range(self.n_peers):
            for core in (0, 1):
                for j, d in enumerate(self.names):
                    chip = cycle[(spot[e // 2] - d) % self.n]
                    table[e, core * self.n + j] = 2 * chip + (e % 2 if core else 1 - e % 2)
        self.order = jnp.asarray(table)[lax.axis_index("expert")]

    def at(self, distance, other):
        return self.names.index(distance) + (0 if other else self.n)

    def ahead(self, x):
        return lax.ppermute(x, "expert", self.fwd)

    def behind(self, x):
        return lax.ppermute(x, "expert", self.bwd)

    def other_core(self, x):
        return lax.ppermute(x, "expert", self.swap)


def gather_rows(ring, tokens, out_grad, table, cap, beside):
    tok_rows = tokens.shape[0]
    own = jnp.concatenate([tokens, out_grad], axis=0)
    beside = list(beside)

    def whole(x):
        return (x, x, tok_rows, 0, 1)

    def place(spots, shards, state):
        return put_rows(np.array(spots, np.int32), table, shards, *state, cap)

    state = (None, None)
    ahead, behind = own, own
    pending = ([ring.at(0, False), ring.at(0, True)], [whole(own), whole(ring.other_core(own))])
    marks = []
    for d in range(1, ring.far):
        ahead, behind = ring.ahead(ahead), ring.behind(behind)
        if d >= 2:
            state = place(*pending[0], state)
            pending = pending[1:]
            ahead, behind, state = lax.optimization_barrier((ahead, behind, state))
            if d - 2 < len(beside):
                ahead, behind, beside[d - 2] = lax.optimization_barrier(
                    (ahead, behind, beside[d - 2])
                )
        else:
            pending = [pending]
        marks.append((ahead, behind))
        pending.append(
            (
                [ring.at(d, False), ring.at(-d, False), ring.at(d, True), ring.at(-d, True)],
                [whole(x) for x in (ahead, behind, ring.other_core(ahead), ring.other_core(behind))],
            )
        )
    far_tok = ring.ahead(ahead[:tok_rows])
    far_grad = ring.behind(behind[tok_rows:])
    state = place(*pending[0], state)
    far_tok, far_grad, state = lax.optimization_barrier((far_tok, far_grad, state))
    marks.append((far_tok, far_grad))
    for spots, shards in pending[1:]:
        state = place(spots, shards, state)
    state = place(
        [ring.at(ring.far, False), ring.at(ring.far, True)],
        [
            (far_tok, far_grad, tok_rows, 0, 0),
            (ring.other_core(far_tok), ring.other_core(far_grad), tok_rows, 0, 0),
        ],
        state,
    )
    return state, marks, beside


def add_blocks(blocks, tok_rows, split, cols, joined=False):
    operands = [x for terms in blocks for x in terms]
    half = tok_rows // 2

    def body(*refs):
        outs, at = refs[len(operands) :], 0
        for i, terms in enumerate(blocks):
            for lower in (0, half):
                total = jnp.zeros((half, cols), f32)
                for j, (_, _, rows, first, _) in enumerate(terms):
                    if first <= lower < first + rows:
                        total += refs[at + j][lower - first : lower - first + half, :].astype(f32)
                if split:
                    outs[1 if lower else 0][...] = total.astype(bf16)
                elif joined:
                    outs[0][lower : lower + half, i * cols : (i + 1) * cols] = total.astype(bf16)
                else:
                    outs[i][lower : lower + half, :] = total.astype(bf16)
            at += len(terms)

    height, count = (half, 2) if split else (tok_rows, 1 if joined else len(blocks))
    wide = len(blocks) * cols if joined else cols
    out = pl.pallas_call(
        body,
        out_shape=[jax.ShapeDtypeStruct((height, wide), bf16)] * count,
        grid=(1,),
        in_specs=[
            pl.BlockSpec((rows, cols), lambda i, at=at, col=col: (at, col))
            for _, at, rows, _, col in operands
        ],
        out_specs=[pl.BlockSpec((height, wide), lambda i: (0, 0))] * count,
        compiler_params=pltpu.CompilerParams(vmem_limit_bytes=KERNEL_VMEM),
        cost_estimate=LIGHT,
        name="add_blocks",
    )(*[x[0] for x in operands])
    return list(out)


def sum_back(ring, handed, mine, tok_rows, between):
    width = mine[0].shape[1]
    cols, half = width // 2, tok_rows // 2

    def terms_of(h, own_pieces):
        terms, j = {}, 0
        for piece, own in zip(handed, own_pieces):
            for at in range(piece.shape[0] // tok_rows):
                terms[ring.names[j]] = [(x, at, tok_rows, 0, h) for x in (own, piece)]
                j += 1
        return terms

    def first(terms):
        top, low = add_blocks([terms[ring.far]], tok_rows, True, cols)
        return [(ring.ahead(top), 0, half, 0, 0), (ring.behind(low), 0, half, half, 0)]

    terms = [terms_of(0, mine)]
    (top, *at_top), (low, *at_low) = first(terms[0])
    mine, between, top, low = lax.optimization_barrier((mine, between, top, low))
    moving = [[(top, *at_top), (low, *at_low)]]
    terms.append(terms_of(1, mine))
    moving.append(first(terms[1]))
    for d in range(ring.far - 1, 0, -1):
        for h in (0, 1):
            ahead, behind = add_blocks(
                [terms[h][-d] + moving[h][:1], terms[h][d] + moving[h][1:]], tok_rows, False, cols
            )
            ahead, behind = ring.ahead(ahead), ring.behind(behind)
            moving[h] = [(ahead, 0, tok_rows, 0, 0), (behind, 0, tok_rows, 0, 0)]
    done = add_blocks([terms[h][0] + moving[h] for h in (0, 1)], tok_rows, False, cols, True)
    return done[0], between


def join_down(terms, piece, total):
    low, width = terms[0].shape
    r = low // 2 if low % 32 == 0 else low
    steps = low // r
    aliased = [] if total is None else [total]

    def body(*refs):
        out = refs[0][...].astype(f32)
        for x in refs[1 : len(terms)]:
            out = out + x[...].astype(f32)
        refs[-1][...] = (grad_scale * out).astype(bf16)

    return pl.pallas_call(
        body,
        out_shape=jax.ShapeDtypeStruct((2 * low, width), bf16),
        grid=(steps,),
        in_specs=[pl.BlockSpec((r, width), lambda i: (i, 0))] * len(terms)
        + [pl.BlockSpec(memory_space=pl.ANY) for _ in aliased],
        out_specs=pl.BlockSpec((r, width), lambda i: (piece * steps + i, 0)),
        input_output_aliases={len(terms): 0} if aliased else {},
        compiler_params=pltpu.CompilerParams(vmem_limit_bytes=KERNEL_VMEM),
        cost_estimate=LIGHT,
        name="join_down",
    )(*terms, *aliased)


def blocks_per_step(n_blocks, cap):
    return max(b for b in range(1, n_blocks + 1) if n_blocks % b == 0 and b * cap <= 768)


def chunk_grads(order, cols, rows, routed, gate, up_mat, down_mat, start, piece):
    n_slots, width = rows.shape
    n_peers, cap, w = gate.shape
    n = blocks_per_step(n_peers, cap)
    r = n * cap
    n_rows, n_cols = n_slots // r, cols.shape[0]

    def body(order_ref, cols_ref, rows_ref, routed_ref, up_ref, down_ref, col_ref, *refs):
        gate_refs, (hidden_ref, both_ref, part_ref, held) = refs[:n], refs[n:]
        step = pl.program_id(0)

        @pl.when(step < n_rows)
        def _():
            up_all = jnp.dot(rows_ref[...], up_ref[...], preferred_element_type=f32)
            grad_all = dot(routed_ref[...], down_ref[...], ((1,), (1,)))
            for b in range(n):
                at = slice(b * cap, (b + 1) * cap)
                up_act, hidden_grad = up_all[at], grad_all[at]
                gate_val = gate_refs[b][0].astype(f32)
                gate_sig = jax.nn.sigmoid(gate_val)
                gate_act = gate_val * gate_sig
                hidden_ref[at, :] = (gate_act * up_act).astype(bf16)
                both_ref[at, w:] = (hidden_grad * gate_act).astype(bf16)
                both_ref[at, :w] = (
                    hidden_grad * up_act * gate_sig * (1.0 + gate_val * (1.0 - gate_sig))
                ).astype(bf16)
            held[pl.ds(pl.multiple_of(step * r, r), r), :] = both_ref[...]

        @pl.when(step >= n_rows)
        def _():
            part_ref[...] = dot(col_ref[...], held[...], ((0,), (0,))).astype(bf16)

    def row(i):
        return jnp.minimum(i, n_rows - 1)

    def col(i):
        return jnp.maximum(i - n_rows, 0)

    return pl.pallas_call(
        body,
        out_shape=(
            jax.ShapeDtypeStruct((n_slots, w), bf16),
            jax.ShapeDtypeStruct((n_slots, 2 * w), bf16),
            jax.ShapeDtypeStruct((n_cols * piece, 2 * w), bf16),
        ),
        grid_spec=pltpu.PrefetchScalarGridSpec(
            num_scalar_prefetch=2,
            grid=(n_rows + n_cols,),
            in_specs=[
                pl.BlockSpec((r, width), lambda i, order, cols: (row(i), 0)),
                pl.BlockSpec((r, width), lambda i, order, cols: (row(i), 0)),
                pl.BlockSpec((pl.Element(width), pl.Element(w)), lambda i, order, cols: (0, start)),
                pl.BlockSpec((pl.Element(w), pl.Element(width)), lambda i, order, cols: (start, 0)),
                pl.BlockSpec((n_slots, piece), lambda i, order, cols: (0, cols[col(i)])),
            ]
            + [
                pl.BlockSpec((1, cap, w), lambda i, order, cols, b=b: (order[n * row(i) + b], 0, 0))
                for b in range(n)
            ],
            out_specs=(
                pl.BlockSpec((r, w), lambda i, order, cols: (row(i), 0)),
                pl.BlockSpec((r, 2 * w), lambda i, order, cols: (row(i), 0)),
                pl.BlockSpec((piece, 2 * w), lambda i, order, cols: (col(i), 0)),
            ),
            scratch_shapes=[pltpu.VMEM((n_slots, 2 * w), bf16)],
        ),
        compiler_params=pltpu.CompilerParams(vmem_limit_bytes=KERNEL_VMEM),
        cost_estimate=LIGHT,
        name="chunk_grads",
    )(order, cols, rows, routed, up_mat, down_mat, rows, *[gate] * n)


def own_half(cols, rows, both, piece):
    n_slots = rows.shape[0]
    w = both.shape[1]

    def body(cols_ref, rows_ref, both_ref, own_ref):
        own_ref[...] = dot(rows_ref[...], both_ref[...], ((0,), (0,))).astype(bf16)

    return pl.pallas_call(
        body,
        out_shape=jax.ShapeDtypeStruct((piece, w), bf16),
        grid_spec=pltpu.PrefetchScalarGridSpec(
            num_scalar_prefetch=1,
            grid=(1,),
            in_specs=[
                pl.BlockSpec((n_slots, piece), lambda i, cols: (0, cols[0])),
                pl.BlockSpec((n_slots, w), lambda i, cols: (0, 0)),
            ],
            out_specs=pl.BlockSpec((piece, w), lambda i, cols: (0, 0)),
        ),
        compiler_params=pltpu.CompilerParams(vmem_limit_bytes=KERNEL_VMEM),
        cost_estimate=LIGHT,
        name="own_half",
    )(cols, rows, both)


def down_rows(order, routed, hidden_parts, starts):
    n_slots, width = routed.shape
    hidden_width = sum(x.shape[1] for x in hidden_parts)
    n_parts = order.shape[0]
    n_parts, low = 2 * n_parts, hidden_width // (2 * n_parts)
    span = min(512, width)
    n_in = len(hidden_parts)

    def body(order_ref, routed_ref, *refs):
        turned, held = refs[-2:]

        @pl.when(pl.program_id(0) == 0)
        def _():
            for start, x in zip(starts, refs[:n_in]):
                turned[start : start + x.shape[1], :] = x[...].T

        held[...] = jnp.dot(turned[...], routed_ref[...], preferred_element_type=f32).astype(bf16)
        for d, out_ref in enumerate(refs[n_in:-2]):
            out_ref[...] = held[
                pl.ds(pl.multiple_of((2 * order_ref[d // 2] + d % 2) * low, 16), low), :
            ]

    return pl.pallas_call(
        body,
        out_shape=[jax.ShapeDtypeStruct((low, width), bf16)] * n_parts,
        grid_spec=pltpu.PrefetchScalarGridSpec(
            num_scalar_prefetch=1,
            grid=(width // span,),
            in_specs=[pl.BlockSpec((n_slots, span), lambda i, order: (0, i))]
            + [pl.BlockSpec(x.shape, lambda i, order: (0, 0)) for x in hidden_parts],
            out_specs=[pl.BlockSpec((low, span), lambda i, order: (0, i))] * n_parts,
            scratch_shapes=[
                pltpu.VMEM((hidden_width, n_slots), bf16),
                pltpu.VMEM((hidden_width, span), bf16),
            ],
        ),
        compiler_params=pltpu.CompilerParams(vmem_limit_bytes=KERNEL_VMEM),
        cost_estimate=LIGHT,
        name="down_rows",
    )(order, routed, *hidden_parts)


def join_halves(own_parts, arrivals, starts, hidden_width):
    piece = own_parts[0].shape[0]
    r = min(128, piece)
    operands = [x for own, arrived in zip(own_parts, arrivals) for x in [own] + list(arrived)]
    each = len(operands) // len(own_parts)

    def body(*refs):
        gate_ref, up_ref = refs[-2:]
        for c, start in enumerate(starts):
            terms = refs[c * each : (c + 1) * each]
            w = terms[0].shape[1] // 2
            for at, out_ref in ((slice(0, w), gate_ref), (slice(w, 2 * w), up_ref)):
                total = terms[0][:, at].astype(f32)
                for x in terms[1:]:
                    total = total + x[:, at].astype(f32)
                out_ref[:, start : start + w] = (grad_scale * total).astype(bf16)

    shape = jax.ShapeDtypeStruct((piece, hidden_width), bf16)
    out_spec = pl.BlockSpec((r, hidden_width), lambda i: (i, 0))
    return pl.pallas_call(
        body,
        out_shape=(shape, shape),
        grid=(piece // r,),
        in_specs=[pl.BlockSpec((r, x.shape[1]), lambda i: (i, 0)) for x in operands],
        out_specs=(out_spec, out_spec),
        compiler_params=pltpu.CompilerParams(vmem_limit_bytes=KERNEL_VMEM),
        cost_estimate=LIGHT,
        name="join_halves",
    )(*operands)


def spread_back(parts, starts, gate_mat, up_mat, table, tok_rows, first, heights):
    n_peers, _, cap = table.shape
    half = n_peers // 2
    width, hidden_width = gate_mat.shape
    cols = min(512, width)
    rows = half * cap
    shift = 0 if first else 1
    owner = [(i, b) for i, height in enumerate(heights) for b in range(height)]

    def body(*refs):
        part_refs = refs[: len(parts)]
        gate_ref, up_ref, table_ref = refs[len(parts) : len(parts) + 3]
        out_refs = refs[len(parts) + 3 :]
        total = jnp.zeros((rows, cols), f32)
        for start, part_ref in zip(starts, part_refs):
            w = part_ref.shape[1] // 2
            total += dot(part_ref[:, :w], gate_ref[:, start : start + w], ((1,), (1,)))
            total += dot(part_ref[:, w:], up_ref[:, start : start + w], ((1,), (1,)))
        terms = total.astype(bf16)
        for j, (i, b) in enumerate(owner):
            tok = table_ref[j, 0:1, :]
            place = (lax.broadcasted_iota(i32, (tok_rows, cap), 0).astype(f32) == tok).astype(bf16)
            spread = jnp.dot(place, terms[j * cap : (j + 1) * cap], preferred_element_type=f32)
            out_refs[i][b * tok_rows : (b + 1) * tok_rows, :] = spread.astype(bf16)

    return pl.pallas_call(
        body,
        out_shape=[jax.ShapeDtypeStruct((h * tok_rows, width), bf16) for h in heights],
        grid=(width // cols,),
        in_specs=[pl.BlockSpec((rows, x.shape[1]), lambda j: (shift, 0)) for x in parts]
        + [
            pl.BlockSpec((cols, hidden_width), lambda j: (j, 0)),
            pl.BlockSpec((cols, hidden_width), lambda j: (j, 0)),
            pl.BlockSpec((half, 2, cap), lambda j: (shift, 0, 0)),
        ],
        out_specs=[pl.BlockSpec((h * tok_rows, cols), lambda j: (0, j)) for h in heights],
        compiler_params=pltpu.CompilerParams(vmem_limit_bytes=KERNEL_VMEM),
        cost_estimate=LIGHT,
        name="spread_back",
    )(*parts, gate_mat, up_mat, table)


def local(tokens, out_grad, gate_saved, probs, expert_ids, w_gate, w_up, w_down):
    n_peers = lax.axis_size("expert")
    n_dp = lax.axis_size("dp")
    group = lax.axis_index("dp")
    tok_rows, model_width = tokens.shape
    top_k = expert_ids.shape[1]
    hidden_width = w_up.shape[2]
    cap = min(tok_rows, 2 * tok_rows * top_k // n_peers)
    n_routes = tok_rows * top_k
    n_slots = n_peers * cap
    gate_mat, up_mat, down_mat = w_gate[0], w_up[0], w_down[0]

    experts = jnp.arange(n_peers, dtype=i32)
    hit = expert_ids[:, :, None] == experts[None, None, :]
    named = jnp.any(hit, axis=1)
    weight = jnp.sum(jnp.where(hit, probs[:, :, None], 0.0), axis=1)
    rank = jnp.cumsum(named.astype(i32), axis=0) - 1
    slots = jnp.arange(cap, dtype=i32)
    in_slot = named[:, :, None] & (rank[:, :, None] == slots[None, None, :])
    tok_of = jnp.sum(
        jnp.where(in_slot, jnp.arange(1, tok_rows + 1, dtype=f32)[:, None, None], 0.0), axis=0
    ) - 1.0
    choice = jnp.sum(jnp.where(hit, jnp.arange(top_k, dtype=f32)[None, :, None], 0.0), axis=1)
    choice_of = jnp.sum(jnp.where(in_slot, choice[:, :, None], 0.0), axis=0)
    weight_of = jnp.sum(jnp.where(in_slot, weight[:, :, None], 0.0), axis=0)
    table = lax.all_to_all(
        jnp.concatenate([tok_of, weight_of], axis=1),
        "expert",
        split_axis=0,
        concat_axis=0,
        tiled=True,
    )
    ring = Ring()
    table = table.reshape(n_peers, 2, cap)[ring.order]
    widths = chunk_widths(hidden_width)
    starts = [sum(widths[:i]) for i in range(len(widths))]
    route_gates = jnp.transpose(gate_saved, (1, 0, 2)).reshape(n_routes, hidden_width)
    route_of = (tok_of + tok_rows * choice_of).astype(i32).reshape(n_slots, 1)
    pick = (route_of == jnp.arange(n_routes, dtype=i32)[None, :]).astype(bf16)
    send_gate = [
        dot(pick, route_gates[:, s : s + w], ((1,), (0,))).astype(bf16).reshape(n_peers, cap, w)
        for s, w in zip(starts, widths)
    ]
    (rows_in, routed), marks, (send_gate[1:],) = gather_rows(
        ring, tokens, out_grad, table.transpose(0, 2, 1), cap, [send_gate[1:]]
    )

    def send_chunk(i, mark):
        part = send_gate[i]
        if mark is not None:
            part, _ = lax.optimization_barrier((part, mark))
        return lax.all_to_all(part, "expert", split_axis=0, concat_axis=0, tiled=True)

    recv_gate = [send_chunk(i, m) for i, m in zip(range(len(widths)), (None, marks[-1]))]

    piece = model_width // n_dp
    shifts = [[(i, (i + d) % n_dp) for i in range(n_dp)] for d in range(n_dp)]

    peer_cols = lax.rem(group + jnp.arange(1, n_dp, dtype=i32), n_dp)
    own_cols = group.reshape(1).astype(i32)
    both_parts, hidden_parts, arrivals, own_parts = [], [], [], []
    rows_now, routed_now = rows_in, routed
    for c, w in enumerate(widths):
        if c >= 2:
            for both in both_parts[len(own_parts) :]:
                own_parts.append(own_half(own_cols, rows_now, both, piece))
            rows_now, own_parts, arrivals[c - 2] = lax.optimization_barrier(
                (rows_now, own_parts, arrivals[c - 2])
            )
        hidden, both, sent = chunk_grads(
            ring.order,
            peer_cols,
            rows_now,
            routed_now,
            recv_gate[c],
            up_mat,
            down_mat,
            starts[c],
            piece,
        )
        both_parts.append(both)
        hidden_parts.append(hidden)
        arrivals.append(
            [
                lax.ppermute(sent[(d - 1) * piece : d * piece], "dp", shifts[d])
                for d in range(1, n_dp)
            ]
        )
        rows_now, routed_now, _ = lax.optimization_barrier((rows_now, routed_now, sent))
        if c + 2 < len(widths):
            recv_gate.append(send_chunk(c + 2, sent))

    heights = [1] + [2] * (ring.far - 1) + [1]
    theirs = spread_back(both_parts, starts, gate_mat, up_mat, table, tok_rows, True, heights)
    handed = [ring.other_core(x) for x in theirs]
    hidden_parts, _ = lax.optimization_barrier((hidden_parts, theirs))
    down_order = lax.rem(group + jnp.arange(n_dp, dtype=i32), n_dp)
    sent = down_rows(down_order, routed_now, hidden_parts, starts)
    own_down, sent = sent[:2], sent[2:]
    last, arrivals[:-1], sent = lax.optimization_barrier((both_parts[-1], arrivals[:-1], sent))
    mine = spread_back(
        both_parts[:-1] + [last], starts, gate_mat, up_mat, table, tok_rows, False, heights
    )
    parts, _ = lax.optimization_barrier((both_parts, mine))
    for both in parts[len(own_parts) :]:
        own_parts.append(own_half(own_cols, rows_now, both, piece))
    mine, handed = lax.optimization_barrier((mine, handed))
    input_grad, (own_parts, arrivals[-1], sent) = sum_back(
        ring, handed, mine, tok_rows, (own_parts, arrivals[-1], sent)
    )
    arrived = [lax.ppermute(part, "dp", shifts[1 + i // 2]) for i, part in enumerate(sent)]
    own_parts, _ = lax.optimization_barrier((own_parts, input_grad))
    grad_gate, grad_up = join_halves(own_parts, arrivals, starts, hidden_width)
    arrived[::2], grad_gate = lax.optimization_barrier((arrived[::2], grad_gate))
    grad_down = None
    for k in (0, 1):
        grad_down = join_down([own_down[k]] + arrived[k::2], k, grad_down)
        if k == 0:
            grad_down, arrived[1::2] = lax.optimization_barrier((grad_down, arrived[1::2]))
    grad_down = grad_down[None]
    return (input_grad, grad_gate[None], grad_up[None], grad_down)


def solution(mesh):
    return jax.shard_map(
        local,
        mesh=mesh,
        in_specs=(
            P(("dp", "expert"), None),
            P(("dp", "expert"), None),
            P(("dp", "expert"), None, None),
            P(("dp", "expert"), None),
            P(("dp", "expert"), None),
            P("expert", None, None),
            P("expert", None, None),
            P("expert", None, None),
        ),
        out_specs=(
            P(("dp", "expert"), None),
            P("expert", "dp", None),
            P("expert", "dp", None),
            P("expert", "dp", None),
        ),
        check_vma=False,
    )
```
